256 devices in a mesh: pts: 32 (over x, z_lo, core), lat: 8 (over z_hi, y).
Axes of the slice: x: 4, y: 4, z: 8 (z_hi: 2, z_lo: 4; z = z_hi * 4 + z_lo), core: 2. Of those that a mesh axis runs over, the one named last changes fastest.
Arguments:
- latents: bfloat16 [8192, 128], P('lat'), may hold values from -9 to 9
- keys: bfloat16 [131072, 128], P('pts'), may hold values from -9 to 9
- values: bfloat16 [131072, 128], P('pts'), may hold values from -6 to 6
- sweep: int32 [131072], P('pts'), may hold values from 0 to 15
- sweep_bias: float32 [4, 16], replicated, may hold values from -4 to 4
- grad_out: bfloat16 [8192, 128], P('lat'), may hold values from -6 to 6
Outputs:
- grad_latents: float32 [8192, 128], P(('lat', 'pts'))
- grad_keys: float32 [131072, 128], P(('pts', 'lat'))
- grad_values: float32 [131072, 128], P(('pts', 'lat'))
- grad_bias: float32 [4, 16], replicated
The draws below stay inside these ranges and needn't reach their ends.
All inputs are finite; a program needn't handle non-finite values.
Results may differ from the reference program's by a relative error of at most 0.011.
Values sent between devices are 32-bit elements; how exact they have to be, the bound alone decides.
A program may use at most 64 MiB of HBM per device.

```python
import math
import jax
import jax.numpy as jnp
from jax import lax

HEADS = 4
HEAD_DIM = 32
SWEEPS = 16
NQ = 8192
NK = 131072


def draw_latents(key, part):
    key = jax.random.fold_in(key, 11)
    base = jnp.clip(jax.random.normal(key, (NQ, HEADS * HEAD_DIM), jnp.float32), -6.0, 6.0)
    return base.astype(jnp.bfloat16)


def draw_keys(key, part):
    key = jax.random.fold_in(key, 23)
    base = jnp.clip(jax.random.normal(key, (NK, HEADS * HEAD_DIM), jnp.float32), -6.0, 6.0)
    return base.astype(jnp.bfloat16)


def touch_ends(drawn, own_key, low, largest):
    longest = drawn.shape.index(max(drawn.shape))
    spots = []
    for shift in (0, 1):
        where = [jax.random.randint(jax.random.fold_in(own_key, axis), (), 0, length) for axis, length in enumerate(drawn.shape)]
        where[longest] = (where[longest] + shift) % drawn.shape[longest]
        spots.append(tuple(where))
    return drawn.at[spots[0]].set(low).at[spots[1]].set(largest)


def shard_levels(stream_key, shape, cuts, least, top_value):
    level = 1.0
    for axis_at, shards_of in cuts:
        steps = jax.random.uniform(jax.random.fold_in(jax.random.fold_in(stream_key, 6), axis_at), (shards_of,), jnp.float32, least / len(cuts), top_value / len(cuts))
        level = level * jnp.repeat(jnp.exp(steps), shape[axis_at] // shards_of).reshape((-1,) + (1,) * (len(shape) - 1 - axis_at))
    return level


def centred(rng, shape, spread, bound, split=(), held_as=jnp.bfloat16):
    loudness = shard_levels(rng, shape, split, -0.22, 0.18) if split else 1.0
    drawn = jax.random.normal(rng, shape, jnp.float32) * spread * loudness
    return jnp.minimum(jnp.maximum(drawn, -bound), bound).astype(held_as)


def setup_inputs(seed: int = 0) -> dict:
    key_of = jax.random.split(jax.random.key(seed), 7)
    latents = draw_latents(jax.random.fold_in(key_of[6], 71), 0)
    keys = draw_keys(jax.random.fold_in(key_of[6], 71), 0)
    values = centred(key_of[2], (NK, HEADS * HEAD_DIM), 1.0, 6.0, ((0, 32),))
    sweep = touch_ends(jax.random.randint(key_of[3], (NK,), 0, SWEEPS), jax.random.fold_in(key_of[3], 1), 0, SWEEPS - 1).astype(jnp.int32)
    sweep_bias = centred(key_of[4], (HEADS, SWEEPS), 1.0, 4.0, (), jnp.float32)
    grad_out = centred(key_of[5], (NQ, HEADS * HEAD_DIM), 1.0, 6.0, ((0, 8),))
    return {"latents": latents, "keys": keys, "values": values, "sweep": sweep, "sweep_bias": sweep_bias, "grad_out": grad_out}


def rounded(x):
    return lax.optimization_barrier(x.astype(jnp.bfloat16)).astype(jnp.float32)


def reference(latents, keys, values, sweep, sweep_bias, grad_out):
    query_rows = math.gcd(NQ, 512)
    blocks = NQ // query_rows
    key_heads = keys.astype(jnp.float32).reshape(NK, HEADS, HEAD_DIM)
    value_heads = values.astype(jnp.float32).reshape(NK, HEADS, HEAD_DIM)
    onehot = (sweep[:, None] == jnp.arange(SWEEPS, dtype=jnp.int32)[None, :]).astype(jnp.float32)
    columns = jnp.einsum("hs,cs->hc", sweep_bias, onehot, precision=lax.Precision.HIGHEST)
    query_heads = latents.astype(jnp.float32).reshape(blocks, query_rows, HEADS, HEAD_DIM)
    out_heads = grad_out.astype(jnp.float32).reshape(blocks, query_rows, HEADS, HEAD_DIM)
    factor = HEAD_DIM ** -0.5

    def step(carried, inputs):
        grad_k, grad_v, grad_b = carried
        query_block, grad_block = inputs
        scores = jnp.einsum("rhd,chd->hrc", query_block, key_heads) * factor + columns[:, None, :]
        out_prod = jnp.einsum("rhd,chd->hrc", grad_block, value_heads)
        row_top = jnp.max(scores, axis=-1, keepdims=True)
        expo = jnp.exp(scores - row_top)
        totals = jnp.sum(expo, axis=-1, keepdims=True)
        probs = expo / totals
        deltas = jnp.sum(probs * out_prod, axis=-1, keepdims=True)
        score_grad = probs * (out_prod - deltas)
        scaled = rounded(score_grad * factor)
        probs_low = rounded(probs)
        grad_q = jnp.einsum("hrc,chd->rhd", scaled, key_heads).reshape(query_rows, HEADS * HEAD_DIM)
        grad_k = grad_k + jnp.einsum("hrc,rhd->chd", scaled, query_block)
        grad_v = grad_v + jnp.einsum("hrc,rhd->chd", probs_low, grad_block)
        grad_b = grad_b + jnp.einsum("hc,cs->hs", jnp.sum(score_grad, axis=1), onehot, precision=lax.Precision.HIGHEST)
        return (grad_k, grad_v, grad_b), grad_q

    start = (jnp.zeros((NK, HEADS, HEAD_DIM), jnp.float32), jnp.zeros((NK, HEADS, HEAD_DIM), jnp.float32), jnp.zeros((HEADS, SWEEPS), jnp.float32))
    (grad_k, grad_v, grad_b), grad_q = lax.scan(step, start, (query_heads, out_heads))
    return (grad_q.reshape(NQ, HEADS * HEAD_DIM), grad_k.reshape(NK, HEADS * HEAD_DIM), grad_v.reshape(NK, HEADS * HEAD_DIM), grad_b)
```

```python
import functools
import math

import jax
import jax.numpy as jnp
from jax import lax
from jax.experimental import pallas as pl
from jax.experimental.pallas import tpu as pltpu
from jax.sharding import PartitionSpec as P

HEADS = 4
HEAD_DIM = 32
WIDTH = HEADS * HEAD_DIM
SWEEPS = 16
SCALE = HEAD_DIM**-0.5
LOG2E = math.log2(math.e)
TO_LOG2 = SCALE * LOG2E
YS = 4
ONES_ROW = 3 * SWEEPS
BF = jnp.bfloat16
F32 = jnp.float32
MESH = pl.DeviceIdType.MESH
VMEM_BYTES = 56 * 1024 * 1024


def dot(a, b):
    return jnp.dot(a, b, preferred_element_type=F32)


def three_pieces(x):
    hi = x.astype(BF)
    rest = x - hi.astype(F32)
    mid = rest.astype(BF)
    low = (rest - mid.astype(F32)).astype(BF)
    return hi, mid, low


def vmem_specs(count):
    return [pl.BlockSpec(memory_space=pltpu.VMEM)] * count


def stats_kernel(keys_ref, aux_ref, value_rows_ref, q_t_ref, g_t_ref, bias_rows_ref, out_ref, k_aux, q_feat, scores):
    points, latents = keys_ref.shape[0], q_t_ref.shape[1]
    cols = min(256, latents)
    tiles = latents // cols
    chunk = min(512, points)
    chunks = points // chunk

    k_aux[:, :WIDTH] = keys_ref[...]
    k_aux[:, WIDTH:] = aux_ref[...]
    for h in range(HEADS):
        for tile in range(tiles):
            n = h * tiles + tile
            q_feat[n, :WIDTH, :] = jnp.zeros((WIDTH, cols), BF)
            q_feat[n, h * HEAD_DIM : (h + 1) * HEAD_DIM, :] = q_t_ref[
                h * HEAD_DIM : (h + 1) * HEAD_DIM, tile * cols : (tile + 1) * cols
            ]
            q_feat[n, WIDTH : WIDTH + 64, :] = bias_rows_ref[h, :, tile * cols : (tile + 1) * cols]
            q_feat[n, WIDTH + 64 :, :] = jnp.zeros((WIDTH - 64, cols), BF)

    lowest = jnp.full((8, cols), -jnp.inf, F32)

    def score_chunk(n, slot, c, top):
        rows = pl.ds(pl.multiple_of(c * chunk, chunk), chunk)
        s = dot(k_aux[rows, :], q_feat[n]) * TO_LOG2
        scores[slot, rows, :] = s
        return jnp.maximum(top, jnp.max(s.reshape(chunk // 8, 8, cols), axis=0))

    first = lax.fori_loop(0, chunks, lambda c, top: score_chunk(0, 0, c, top), lowest)

    def per_tile(n, top_rows):
        slot = lax.rem(n, 2)
        top = jnp.max(top_rows, axis=0, keepdims=True)
        following = lax.rem(n + 1, HEADS * tiles)
        head = n // tiles

        def body(c, carried):
            next_top, total, out = carried
            next_top = score_chunk(following, 1 - slot, c, next_top)
            rows = pl.ds(pl.multiple_of(c * chunk, chunk), chunk)
            e = jnp.exp2(scores[slot, rows, :] - top)
            total = total + jnp.sum(e.reshape(chunk // 8, 8, cols), axis=0)
            out = out + dot(value_rows_ref[head, :, rows], e.astype(BF))
            return next_top, total, out

        next_top, total, out = lax.fori_loop(
            0, chunks, body, (lowest, jnp.zeros((8, cols), F32), jnp.zeros((48, cols), F32))
        )
        total = jnp.sum(total, axis=0, keepdims=True)
        g = g_t_ref[
            pl.ds(pl.multiple_of(head * HEAD_DIM, HEAD_DIM), HEAD_DIM),
            pl.ds(pl.multiple_of(lax.rem(n, tiles) * cols, cols), cols),
        ].astype(F32)
        weighted = jnp.sum(out[:HEAD_DIM] * g, axis=0, keepdims=True)
        rounded_total = out[HEAD_DIM : HEAD_DIM + 1]
        row = lax.broadcasted_iota(jnp.int32, (8, cols), 0)
        tile = jnp.where(
            row == 0, top, jnp.where(row == 1, total, jnp.where(row == 2, weighted, rounded_total))
        )
        for part in range(cols // 128):
            out_ref[n * (cols // 128) + part] = tile[:, part * 128 : (part + 1) * 128]
        return next_top

    lax.fori_loop(0, HEADS * tiles, per_tile, first)


def local_stats(keys, aux, value_rows, q_t, g_t, bias_rows):
    points, latents = keys.shape[0], q_t.shape[1]
    cols = min(256, latents)
    return pl.pallas_call(
        stats_kernel,
        out_shape=jax.ShapeDtypeStruct((HEADS * latents // 128, 8, 128), F32),
        in_specs=vmem_specs(6),
        out_specs=pl.BlockSpec(memory_space=pltpu.VMEM),
        scratch_shapes=[
            pltpu.VMEM((points, 2 * WIDTH), BF),
            pltpu.VMEM((HEADS * latents // cols, 2 * WIDTH, cols), BF),
            pltpu.VMEM((2, points, cols), F32),
        ],
        compiler_params=pltpu.CompilerParams(vmem_limit_bytes=VMEM_BYTES),
    )(keys, aux, value_rows, q_t, g_t, bias_rows)


def enter(axis, me, count):
    barrier = pltpu.get_barrier_semaphore()

    def greet(k, unused):
        pl.semaphore_signal(
            barrier, inc=1, device_id={axis: lax.rem(me + k, count)}, device_id_type=MESH
        )
        return unused

    lax.fori_loop(1, count, greet, 0)
    return barrier


def combine_kernel(count, stats_ref, out_ref, arrived, mine, final, sent_1, got_1, sent_2, got_2):
    me = lax.axis_index("pts")
    share = stats_ref.shape[0] // count
    barrier = enter("pts", me, count)
    pl.semaphore_wait(barrier, count - 1)

    def piece(k):
        there = lax.rem(me + k, count)
        return pltpu.make_async_remote_copy(
            src_ref=stats_ref.at[pl.ds(there * share, share)],
            dst_ref=arrived.at[me],
            send_sem=sent_1.at[k],
            recv_sem=got_1.at[k],
            device_id={"pts": there},
            device_id_type=MESH,
        )

    def result(k):
        there = lax.rem(me + k, count)
        return pltpu.make_async_remote_copy(
            src_ref=mine,
            dst_ref=final.at[me],
            send_sem=sent_2.at[k],
            recv_sem=got_2.at[k],
            device_id={"pts": there},
            device_id_type=MESH,
        )

    def every(action):
        def step(k, unused):
            action(k)
            return unused

        lax.fori_loop(1, count, step, 0)

    every(lambda k: piece(k).start())
    arrived[me] = stats_ref[pl.ds(me * share, share)]
    every(lambda k: piece(k).wait_recv())
    for part in range(share):
        top = arrived[:, part, 0, :]
        best = jnp.max(top, axis=0, keepdims=True)
        weight = jnp.exp2(top - best)
        total = jnp.sum(weight * arrived[:, part, 1, :], axis=0, keepdims=True)
        weighted = jnp.sum(weight * arrived[:, part, 2, :], axis=0, keepdims=True)
        rounded_total = jnp.sum(weight * arrived[:, part, 3, :], axis=0, keepdims=True)
        offset = (best + jnp.log(total) * LOG2E) * (-1.0 / TO_LOG2)
        row = lax.broadcasted_iota(jnp.int32, (8, 128), 0)
        mine[part] = jnp.where(row == 0, offset, -(weighted / rounded_total))
    every(lambda k: result(k).start())
    final[me] = mine[...]
    every(lambda k: result(k).wait_recv())
    out_ref[...] = final[...].reshape(out_ref.shape)
    every(lambda k: piece(k).wait_send())
    every(lambda k: result(k).wait_send())


def combined_stats(stats, count):
    share = stats.shape[0] // count
    return pl.pallas_call(
        functools.partial(combine_kernel, count),
        out_shape=jax.ShapeDtypeStruct(stats.shape, F32),
        in_specs=vmem_specs(1),
        out_specs=pl.BlockSpec(memory_space=pltpu.VMEM),
        scratch_shapes=[
            pltpu.VMEM((count, share, 8, 128), F32),
            pltpu.VMEM((share, 8, 128), F32),
            pltpu.VMEM((count, share, 8, 128), F32),
            pltpu.SemaphoreType.DMA((count,)),
            pltpu.SemaphoreType.DMA((count,)),
            pltpu.SemaphoreType.DMA((count,)),
            pltpu.SemaphoreType.DMA((count,)),
        ],
        compiler_params=pltpu.CompilerParams(collective_id=0, has_side_effects=True),
    )(stats)


def grads_kernel(
    keys_ref,
    values_ref,
    aux_ref,
    onehot_t_ref,
    k_t_ref,
    q_t_ref,
    g_t_ref,
    latents_ref,
    grad_out_ref,
    bias_rows_ref,
    stats_ref,
    grad_k_ref,
    grad_v_ref,
    grad_q_ref,
    bias_ref,
    k_aux,
    v_aux,
    k_t,
    onehot_t,
    q_feat,
    g_feat,
    q_stack,
    g_stack,
    probs,
    scaled,
    row_sums,
    part_sum,
    from_ring,
    from_z,
    grad_q_t,
    sent,
    got,
    sent_z,
    got_z,
):
    points, latents = keys_ref.shape[0], q_t_ref.shape[1]
    block = points // (2 * YS)
    half = block // 2
    cols = q_feat.shape[2]
    chunks = latents // cols

    lat = lax.axis_index("lat")
    z, y = lat // YS, lax.rem(lat, YS)
    up = z * YS + lax.rem(y + 1, YS)
    down = z * YS + lax.rem(y + YS - 1, YS)
    across = (1 - z) * YS + y

    barrier = pltpu.get_barrier_semaphore()
    for other in (up, down, across):
        pl.semaphore_signal(barrier, inc=1, device_id={"lat": other}, device_id_type=MESH)

    lane = lax.broadcasted_iota(jnp.int32, (latents, WIDTH), 1)
    row16 = lax.broadcasted_iota(jnp.int32, (16, 128), 0)
    for h in range(HEADS):
        mine = (lane >= h * HEAD_DIM) & (lane < (h + 1) * HEAD_DIM)
        for source, stack in ((latents_ref, q_stack), (grad_out_ref, g_stack)):
            stack[h * latents : (h + 1) * latents, :] = jnp.where(
                mine, source[...].astype(F32), 0.0
            ).astype(BF)
        for c in range(chunks):
            n = h * chunks + c
            here = slice(c * cols, (c + 1) * cols)
            for source, feat in ((q_t_ref, q_feat), (g_t_ref, g_feat)):
                feat[n] = jnp.zeros((2 * WIDTH, cols), BF)
                feat[n, h * HEAD_DIM : (h + 1) * HEAD_DIM, :] = source[
                    h * HEAD_DIM : (h + 1) * HEAD_DIM, here
                ]
            q_feat[n, WIDTH : WIDTH + ONES_ROW, :] = bias_rows_ref[h, :ONES_ROW, here]
            for part in range(cols // 128):
                tile = stats_ref[(h * latents + c * cols) // 128 + part]
                for index, feat in ((0, q_feat), (1, g_feat)):
                    hi, mid, low = three_pieces(tile[index : index + 1, :])
                    feat[n, WIDTH + ONES_ROW : WIDTH + ONES_ROW + 16, part * 128 : (part + 1) * 128] = (
                        jnp.where(
                            row16 == 0,
                            hi.astype(F32),
                            jnp.where(
                                row16 == 1,
                                mid.astype(F32),
                                jnp.where(row16 == 2, low.astype(F32), 0.0),
                            ),
                        ).astype(BF)
                    )
    grad_q_t[...] = jnp.zeros_like(grad_q_t)
    bias_ref[...] = jnp.zeros_like(bias_ref)
    lane_row = lax.broadcasted_iota(jnp.int32, (block, 128), 1)

    def compute(step, at_up, at_down):
        for row, at in ((0, at_up), (half, at_down)):
            source = pl.ds(pl.multiple_of(at, half), half)
            rows = pl.ds(row, half)
            k_aux[rows, :WIDTH] = keys_ref[source, :]
            k_aux[rows, WIDTH:] = aux_ref[source, :]
            v_aux[rows, :WIDTH] = values_ref[source, :]
            v_aux[rows, WIDTH:] = aux_ref[source, :]
            k_t[:, row : row + half] = k_t_ref[:, source]
            onehot_t[:, row : row + half] = onehot_t_ref[:, source]
        row_sums[...] = jnp.zeros_like(row_sums)

        def per_chunk(n, unused):
            s = dot(k_aux[...], q_feat[n])
            o = dot(v_aux[...], g_feat[n])
            p = jnp.exp2(s * TO_LOG2)
            score_grad = p * o
            where = pl.ds(pl.multiple_of(n * cols, cols), cols)
            probs[:, where] = p.astype(BF)
            scaled[:, where] = (score_grad * SCALE).astype(BF)
            folded = score_grad[:, :128]
            for part in range(1, cols // 128):
                folded = folded + score_grad[:, part * 128 : (part + 1) * 128]
            row_sums[...] += jnp.where(
                lane_row == n // chunks, jnp.sum(folded, axis=1, keepdims=True), 0.0
            )
            return unused

        lax.fori_loop(0, HEADS * chunks, per_chunk, 0)
        part_sum[step, :, :WIDTH] = dot(scaled[...], q_stack[...])
        part_sum[step, :, WIDTH:] = dot(probs[...], g_stack[...])
        for h in range(HEADS):
            grad_q_t[h * HEAD_DIM : (h + 1) * HEAD_DIM, :] += dot(
                k_t[h * HEAD_DIM : (h + 1) * HEAD_DIM, :], scaled[:, h * latents : (h + 1) * latents]
            )
        for piece in three_pieces(row_sums[...]):
            bias_ref[...] += dot(onehot_t[...], piece)

    def ring(step, upwards):
        rows = pl.ds(0, half) if upwards else pl.ds(half, half)
        return pltpu.make_async_remote_copy(
            src_ref=part_sum.at[step, rows],
            dst_ref=from_ring.at[step, rows],
            send_sem=sent.at[step, 0 if upwards else 1],
            recv_sem=got.at[step, 0 if upwards else 1],
            device_id={"lat": up if upwards else down},
            device_id_type=MESH,
        )

    over = pltpu.make_async_remote_copy(
        src_ref=part_sum.at[YS - 1],
        dst_ref=from_z,
        send_sem=sent_z,
        recv_sem=got_z,
        device_id={"lat": across},
        device_id_type=MESH,
    )

    def per_step(step, unused):
        turn = lax.rem(step, YS)
        owner_z = jnp.where(step < YS, 1 - z, z)
        y_up = lax.rem(y + 2 * YS - 1 - turn, YS)
        y_down = lax.rem(y + 1 + turn, YS)
        compute(
            step,
            (owner_z * YS + y_up) * block,
            (owner_z * YS + y_down) * block + half,
        )

        @pl.when(step == 0)
        def _():
            pl.semaphore_wait(barrier, 3)

        @pl.when(turn > 0)
        def _():
            for upwards in (True, False):
                ring(step - 1, upwards).wait_recv()
            part_sum[step] += from_ring[step - 1]

        @pl.when(turn < YS - 1)
        def _():
            for upwards in (True, False):
                ring(step, upwards).start()

        @pl.when(step == YS - 1)
        def _():
            over.start()

        return unused

    lax.fori_loop(0, 2 * YS, per_step, 0)
    grad_q_ref[...] = grad_q_t[...].T
    over.wait_recv()
    done = part_sum[2 * YS - 1] + from_z[...]
    grad_k_ref[...] = done[:, :WIDTH]
    grad_v_ref[...] = done[:, WIDTH:]
    for step in range(2 * YS):
        if step % YS < YS - 1:
            for upwards in (True, False):
                ring(step, upwards).wait_send()
    over.wait_send()


def gradients(*args):
    keys, q_t = args[0], args[5]
    points, latents = keys.shape[0], q_t.shape[1]
    block = points // (2 * YS)
    cols = min(512, latents)
    return pl.pallas_call(
        grads_kernel,
        out_shape=[
            jax.ShapeDtypeStruct((block, WIDTH), F32),
            jax.ShapeDtypeStruct((block, WIDTH), F32),
            jax.ShapeDtypeStruct((latents, WIDTH), F32),
            jax.ShapeDtypeStruct((SWEEPS, 128), F32),
        ],
        in_specs=vmem_specs(len(args)),
        out_specs=vmem_specs(4),
        scratch_shapes=[
            pltpu.VMEM((block, 2 * WIDTH), BF),
            pltpu.VMEM((block, 2 * WIDTH), BF),
            pltpu.VMEM((WIDTH, block), BF),
            pltpu.VMEM((SWEEPS, block), BF),
            pltpu.VMEM((HEADS * latents // cols, 2 * WIDTH, cols), BF),
            pltpu.VMEM((HEADS * latents // cols, 2 * WIDTH, cols), BF),
            pltpu.VMEM((HEADS * latents, WIDTH), BF),
            pltpu.VMEM((HEADS * latents, WIDTH), BF),
            pltpu.VMEM((block, HEADS * latents), BF),
            pltpu.VMEM((block, HEADS * latents), BF),
            pltpu.VMEM((block, 128), F32),
            pltpu.VMEM((2 * YS, block, 2 * WIDTH), F32),
            pltpu.VMEM((2 * YS, block, 2 * WIDTH), F32),
            pltpu.VMEM((block, 2 * WIDTH), F32),
            pltpu.VMEM((WIDTH, latents), F32),
            pltpu.SemaphoreType.DMA((2 * YS, 2)),
            pltpu.SemaphoreType.DMA((2 * YS, 2)),
            pltpu.SemaphoreType.DMA,
            pltpu.SemaphoreType.DMA,
        ],
        compiler_params=pltpu.CompilerParams(
            collective_id=1, has_side_effects=True, vmem_limit_bytes=VMEM_BYTES
        ),
    )(*args)


def final_kernel(
    count, lats, grad_q_ref, bias_ref, out_ref, bias_out_ref, arrived, by_lat, by_pts, mine,
    sent_q, got_q, sent_l, got_l, sent_p, got_p,
):
    me, lat = lax.axis_index("pts"), lax.axis_index("lat")
    rows = grad_q_ref.shape[0] // count
    barrier = enter("pts", me, count)
    enter("lat", lat, lats)
    pl.semaphore_wait(barrier, count - 1 + lats - 1)

    def over_pts(src, dst, sent, got, k):
        return pltpu.make_async_remote_copy(
            src_ref=src,
            dst_ref=dst,
            send_sem=sent.at[k],
            recv_sem=got.at[k],
            device_id={"pts": lax.rem(me + k, count)},
            device_id_type=MESH,
        )

    def q_copy(k):
        there = lax.rem(me + k, count)
        return over_pts(grad_q_ref.at[pl.ds(there * rows, rows)], arrived.at[me], sent_q, got_q, k)

    def bias_copy(k):
        return over_pts(mine, by_pts.at[me], sent_p, got_p, k)

    def lat_copy(k):
        return pltpu.make_async_remote_copy(
            src_ref=bias_ref,
            dst_ref=by_lat.at[lat],
            send_sem=sent_l.at[k],
            recv_sem=got_l.at[k],
            device_id={"lat": lax.rem(lat + k, lats)},
            device_id_type=MESH,
        )

    def every(stop, action):
        def step(k, unused):
            action(k)
            return unused

        lax.fori_loop(1, stop, step, 0)

    every(lats, lambda k: lat_copy(k).start())
    every(count, lambda k: q_copy(k).start())
    by_lat[lat] = bias_ref[...]
    arrived[me] = grad_q_ref[pl.ds(me * rows, rows)]
    every(lats, lambda k: lat_copy(k).wait_recv())
    mine[...] = jnp.sum(by_lat[...], axis=0)
    every(count, lambda k: bias_copy(k).start())
    by_pts[me] = mine[...]
    every(count, lambda k: q_copy(k).wait_recv())
    out_ref[...] = jnp.sum(arrived[...], axis=0)
    every(count, lambda k: bias_copy(k).wait_recv())
    bias_out_ref[...] = jnp.sum(by_pts[...], axis=0)
    every(lats, lambda k: lat_copy(k).wait_send())
    every(count, lambda k: q_copy(k).wait_send())
    every(count, lambda k: bias_copy(k).wait_send())


def final_sums(grad_q, bias, count, lats):
    rows = grad_q.shape[0] // count
    return pl.pallas_call(
        functools.partial(final_kernel, count, lats),
        out_shape=[
            jax.ShapeDtypeStruct((rows, WIDTH), F32),
            jax.ShapeDtypeStruct((SWEEPS, 128), F32),
        ],
        in_specs=vmem_specs(2),
        out_specs=vmem_specs(2),
        scratch_shapes=[
            pltpu.VMEM((count, rows, WIDTH), F32),
            pltpu.VMEM((lats, SWEEPS, 128), F32),
            pltpu.VMEM((count, SWEEPS, 128), F32),
            pltpu.VMEM((SWEEPS, 128), F32),
            pltpu.SemaphoreType.DMA((count,)),
            pltpu.SemaphoreType.DMA((count,)),
            pltpu.SemaphoreType.DMA((lats,)),
            pltpu.SemaphoreType.DMA((lats,)),
            pltpu.SemaphoreType.DMA((count,)),
            pltpu.SemaphoreType.DMA((count,)),
        ],
        compiler_params=pltpu.CompilerParams(collective_id=2, has_side_effects=True),
    )(grad_q, bias)


def per_device(count, lats, latents, keys, values, sweep, sweep_bias, grad_out):
    rows, points = latents.shape[0], keys.shape[0]
    swept = sweep[:, None]
    column = jnp.arange(WIDTH, dtype=jnp.int32)[None, :]
    marked = (column < ONES_ROW) & (lax.rem(column, SWEEPS) == swept)
    aux = (marked | ((column >= ONES_ROW) & (column < ONES_ROW + 3))).astype(BF)
    onehot_t = (jnp.arange(SWEEPS, dtype=jnp.int32)[:, None] == sweep[None, :]).astype(BF)
    k_t, q_t, g_t = keys.T, latents.T, grad_out.T
    ones_rows = jnp.zeros((HEADS, 16, points), BF).at[:, 0].set(1.0)
    value_rows = jnp.concatenate([values.T.reshape(HEADS, HEAD_DIM, points), ones_rows], axis=1)
    raw = sweep_bias / SCALE
    hi = lax.reduce_precision(raw, 8, 7)
    mid = lax.reduce_precision(raw - hi, 8, 7)
    low = raw - hi - mid
    pieces = jnp.concatenate([hi, mid, low, jnp.zeros((HEADS, 16), F32)], axis=1).astype(BF)
    bias_rows = jnp.broadcast_to(pieces[:, :, None], (HEADS, 64, rows))

    stats = local_stats(keys, aux, value_rows, q_t, g_t, bias_rows)
    stats = combined_stats(stats, count)
    grad_k, grad_v, grad_q, bias = gradients(
        keys, values, aux, onehot_t, k_t, q_t, g_t, latents, grad_out, bias_rows, stats
    )
    grad_q, bias = final_sums(grad_q, bias, count, lats)
    return grad_q, grad_k, grad_v, bias[:, :HEADS].T


def solution(mesh):
    return jax.shard_map(
        functools.partial(per_device, mesh.shape["pts"], mesh.shape["lat"]),
        mesh=mesh,
        in_specs=(P("lat", None), P("pts", None), P("pts", None), P("pts"), P(), P("lat", None)),
        out_specs=(P(("lat", "pts"), None), P(("pts", "lat"), None), P(("pts", "lat"), None), P()),
        check_vma=False,
    )
```

```python
import functools
import math

import jax
import jax.numpy as jnp
from jax import lax
from jax.experimental import pallas as pl
from jax.experimental.pallas import tpu as pltpu
from jax.sharding import PartitionSpec as P

HEADS = 4
HEAD_DIM = 32
WIDTH = HEADS * HEAD_DIM
SWEEPS = 16
SCALE = HEAD_DIM**-0.5
LOG2E = math.log2(math.e)
TO_LOG2 = SCALE * LOG2E
YS = 4
ONES_ROW = 3 * SWEEPS
BF = jnp.bfloat16
F32 = jnp.float32
MESH = pl.DeviceIdType.MESH
VMEM_BYTES = 56 * 1024 * 1024


def dot(a, b):
    return jnp.dot(a, b, preferred_element_type=F32)


def three_pieces(x):
    hi = x.astype(BF)
    rest = x - hi.astype(F32)
    mid = rest.astype(BF)
    low = (rest - mid.astype(F32)).astype(BF)
    return hi, mid, low


def vmem_specs(count):
    return [pl.BlockSpec(memory_space=pltpu.VMEM)] * count


def whole_kernel(
    count,
    lats,
    latents_ref,
    keys_ref,
    values_ref,
    sweep_ref,
    sweep_bias_ref,
    grad_out_ref,
    grad_k_ref,
    grad_v_ref,
    small_ref,
    k_aux,
    value_rows,
    onehot_t,
    g_t,
    q_feat,
    g_feat,
    q_stack,
    g_stack,
    scores_0,
    scores_1,
    stats,
    arrived,
    mine,
    final,
    k_stage,
    v_stage,
    probs,
    scaled,
    part_sum,
    from_ring,
    from_z,
    grad_q_t,
    bias_sum,
    q_parts,
    from_core,
    by_lat,
    q_mine,
    by_chip,
    sent_1,
    got_1,
    sent_2,
    got_2,
    sent_ring,
    got_ring,
    sent_z,
    got_z,
    sent_core,
    got_core,
    sent_bias,
    got_bias,
    sent_chip,
    got_chip,
):
    points, latents = keys_ref.shape[0], latents_ref.shape[0]
    span = latents // 2
    cols = min(256, span)
    per_span = span // cols
    tiles = HEADS * 2 * per_span
    pairs = tiles // 2
    chunk = min(512, points)
    chunks = points // chunk
    block = points // (2 * YS)
    half = block // 2
    chips = count // 2
    share = stats.shape[0] // count
    rows_out = latents // count

    me = lax.axis_index("pts")
    lat = lax.axis_index("lat")
    core = lax.rem(me, 2)
    chip = me // 2
    z, y = lat // YS, lax.rem(lat, YS)
    up = z * YS + lax.rem(y + 1, YS)
    down = z * YS + lax.rem(y + YS - 1, YS)
    across = (1 - z) * YS + y

    def every(start, stop, action):
        def step(k, unused):
            action(k)
            return unused

        lax.fori_loop(start, stop, step, 0)

    def others(start, stop, action):
        def guarded(k):
            @pl.when(k != me)
            def _():
                action(k)

        every(start, stop, guarded)

    barrier = pltpu.get_barrier_semaphore()

    def bias_peer(k):
        there = lax.rem(lat * 2 + core + k, 2 * lats)
        return {"pts": chip * 2 + lax.rem(there, 2), "lat": there // 2}

    def greet_pts(k):
        pl.semaphore_signal(
            barrier, inc=1, device_id={"pts": lax.rem(me + k, count)}, device_id_type=MESH
        )

    def greet_lat(k):
        pl.semaphore_signal(barrier, inc=1, device_id=bias_peer(k), device_id_type=MESH)

    every(1, count, greet_pts)
    every(1, 2 * lats, greet_lat)

    k_aux[:, :WIDTH] = keys_ref[...]

    def build(c):
        rows = pl.ds(pl.multiple_of(c * chunk, chunk), chunk)
        swept = sweep_ref[:, rows]
        row = lax.broadcasted_iota(jnp.int32, (WIDTH, chunk), 0)
        marked = (row < ONES_ROW) & (lax.rem(row, SWEEPS) == swept)
        ones = (row >= ONES_ROW) & (row < ONES_ROW + 3)
        aux_t = jnp.where(marked | ones, 1.0, 0.0)
        onehot_t[:, rows] = aux_t[:SWEEPS].astype(BF)
        k_aux[rows, WIDTH:] = aux_t.T.astype(BF)
        value_t = values_ref[rows, :].T
        for h in range(HEADS):
            value_rows[h, :HEAD_DIM, rows] = value_t[h * HEAD_DIM : (h + 1) * HEAD_DIM, :]
            value_rows[h, HEAD_DIM:, rows] = jnp.where(row[:16] == 0, 1.0, 0.0).astype(BF)

    every(0, chunks, build)
    q_t = latents_ref[...].T
    g_t[...] = grad_out_ref[...].T
    lane = lax.broadcasted_iota(jnp.int32, (span, WIDTH), 1)
    eye = lax.broadcasted_iota(jnp.int32, (SWEEPS, SWEEPS), 0) == lax.broadcasted_iota(
        jnp.int32, (SWEEPS, SWEEPS), 1
    )
    for h in range(HEADS):
        rows = slice(h * HEAD_DIM, (h + 1) * HEAD_DIM)
        column = jnp.sum(
            jnp.where(eye, sweep_bias_ref[h : h + 1, :], 0.0), axis=1, keepdims=True
        ) * (1.0 / SCALE)
        bias_pieces = three_pieces(jnp.broadcast_to(column, (SWEEPS, span)))
        mine_lanes = (lane >= h * HEAD_DIM) & (lane < (h + 1) * HEAD_DIM)
        for s in range(2):
            n = s * HEADS + h
            here = slice(s * span, (s + 1) * span)
            for source, stack in ((latents_ref, q_stack), (grad_out_ref, g_stack)):
                stack[n] = jnp.where(mine_lanes, source[here, :].astype(F32), 0.0).astype(BF)
            q_feat[n] = jnp.zeros((2 * WIDTH, span), BF)
            g_feat[n] = jnp.zeros((2 * WIDTH, span), BF)
            q_feat[n, rows, :] = q_t[rows, here]
            g_feat[n, rows, :] = g_t[rows, here]
            for index, piece in enumerate(bias_pieces):
                q_feat[n, WIDTH + index * SWEEPS : WIDTH + (index + 1) * SWEEPS, :] = piece
    grad_q_t[...] = jnp.zeros_like(grad_q_t)
    bias_sum[...] = jnp.zeros_like(bias_sum)
    pl.semaphore_wait(barrier, count - 1 + 2 * lats - 1)

    def piece(owner):
        return pltpu.make_async_remote_copy(
            src_ref=stats.at[pl.ds(owner * share, share)],
            dst_ref=arrived.at[me],
            send_sem=sent_1.at[owner],
            recv_sem=got_1.at[me],
            device_id={"pts": owner},
            device_id_type=MESH,
        )

    def piece_from(source):
        return pltpu.make_async_remote_copy(
            src_ref=mine,
            dst_ref=arrived.at[source],
            send_sem=sent_1.at[source],
            recv_sem=got_1.at[source],
            device_id={"pts": source},
            device_id_type=MESH,
        )

    def result(there):
        return pltpu.make_async_remote_copy(
            src_ref=mine,
            dst_ref=final.at[me],
            send_sem=sent_2.at[there],
            recv_sem=got_2.at[me],
            device_id={"pts": there},
            device_id_type=MESH,
        )

    def result_from(owner):
        return pltpu.make_async_remote_copy(
            src_ref=mine,
            dst_ref=final.at[owner],
            send_sem=sent_2.at[owner],
            recv_sem=got_2.at[owner],
            device_id={"pts": owner},
            device_id_type=MESH,
        )

    def owners(s):
        return s * (count // 2), (s + 1) * (count // 2)

    def send_pieces(s):
        others(*owners(s), lambda k: piece(k).start())

    def combine(s):
        first, last = owners(s)

        @pl.when((me >= first) & (me < last))
        def _():
            arrived[me] = stats[pl.ds(me * share, share)]
            others(0, count, lambda k: piece_from(k).wait_recv())
            for part in range(share):
                top = arrived[:, part, 0, :]
                best = jnp.max(top, axis=0, keepdims=True)
                weight = jnp.exp2(top - best)
                total = jnp.sum(weight * arrived[:, part, 1, :], axis=0, keepdims=True)
                weighted = jnp.sum(weight * arrived[:, part, 2, :], axis=0, keepdims=True)
                rounded_total = jnp.sum(weight * arrived[:, part, 3, :], axis=0, keepdims=True)
                offset = (best + jnp.log(total) * LOG2E) * (-1.0 / TO_LOG2)
                row = lax.broadcasted_iota(jnp.int32, (8, 128), 0)
                mine[part] = jnp.where(row == 0, offset, -(weighted / rounded_total))
            others(0, count, lambda k: result(k).start())
            final[me] = mine[...]

    def take_results(s):
        others(*owners(s), lambda k: result_from(k).wait_recv())
        row16 = lax.broadcasted_iota(jnp.int32, (16, 128), 0)
        per_tile = cols // 128
        for n in range(tiles // 2):
            it, h = n // HEADS, n % HEADS
            for part in range(per_tile):
                number = s * (tiles // 2) * per_tile + n * per_tile + part
                tile = final[number // share, number % share]
                left = it * cols + part * 128
                for index, feat in ((0, q_feat), (1, g_feat)):
                    hi, mid, low = three_pieces(tile[index : index + 1, :])
                    feat[
                        s * HEADS + h,
                        WIDTH + ONES_ROW : WIDTH + ONES_ROW + 16,
                        left : left + 128,
                    ] = jnp.where(
                        row16 == 0,
                        hi.astype(F32),
                        jnp.where(
                            row16 == 1, mid.astype(F32), jnp.where(row16 == 2, low.astype(F32), 0.0)
                        ),
                    ).astype(BF)

    lowest = jnp.full((32, cols), -jnp.inf, F32)

    def feature_of(n):
        it = n // HEADS
        return (
            (it // per_span) * HEADS + lax.rem(n, HEADS),
            pl.ds(pl.multiple_of(lax.rem(it, per_span) * cols, cols), cols),
        )

    def score_chunk(n, into, c, top):
        index, lanes = feature_of(n)
        rows = pl.ds(c * chunk, chunk)
        s = dot(k_aux[rows, :], q_feat[index, :, lanes]) * TO_LOG2
        into[rows, :] = s
        return jnp.maximum(top, jnp.max(s.reshape(chunk // 32, 32, cols), axis=0))

    def tile_sums(n, scores, top_rows, following, into):
        top = jnp.max(top_rows, axis=0, keepdims=True)
        head = lax.rem(n, HEADS)
        next_top = lowest
        total = jnp.zeros((32, cols), F32)
        out = jnp.zeros((48, cols), F32)
        for c in range(chunks):
            rows = pl.ds(c * chunk, chunk)
            e = jnp.exp2(scores[rows, :] - top)
            total = total + jnp.sum(e.reshape(chunk // 32, 32, cols), axis=0)
            out = out + dot(value_rows[head, :, rows], e.astype(BF))
            next_top = score_chunk(following, into, c, next_top)
        total = jnp.sum(total, axis=0, keepdims=True)
        g = g_t[
            pl.ds(pl.multiple_of(head * HEAD_DIM, HEAD_DIM), HEAD_DIM),
            pl.ds(pl.multiple_of((n // HEADS) * cols, cols), cols),
        ].astype(F32)
        weighted = jnp.sum(out[:HEAD_DIM] * g, axis=0, keepdims=True)
        rounded_total = out[HEAD_DIM : HEAD_DIM + 1]
        row = lax.broadcasted_iota(jnp.int32, (8, cols), 0)
        tile = jnp.where(
            row == 0, top, jnp.where(row == 1, total, jnp.where(row == 2, weighted, rounded_total))
        )
        for part in range(cols // 128):
            stats[n * (cols // 128) + part] = tile[:, part * 128 : (part + 1) * 128]
        return next_top

    first_top = lowest
    for c in range(chunks):
        first_top = score_chunk(0, scores_0, c, first_top)

    def per_pair(pair, top_rows):
        n = pair * 2
        top_rows = tile_sums(n, scores_0, top_rows, n + 1, scores_1)
        top_rows = tile_sums(n + 1, scores_1, top_rows, lax.rem(n + 2, tiles), scores_0)

        @pl.when(pair == pairs // 2 - 1)
        def _():
            send_pieces(0)

        @pl.when(pair == pairs - 2)
        def _():
            combine(0)

        return top_rows

    lax.fori_loop(0, pairs, per_pair, first_top)
    send_pieces(1)
    take_results(0)

    lane_row = lax.broadcasted_iota(jnp.int32, (block, 128), 1)

    def compute(step, s):
        turn = lax.rem(step, YS)
        owner_z = jnp.where(step < YS, 1 - z, z)
        at_up = (owner_z * YS + lax.rem(y + 2 * YS - 1 - turn, YS)) * block
        at_down = (owner_z * YS + lax.rem(y + 1 + turn, YS)) * block + half
        marks = []
        for row, at in ((0, at_up), (half, at_down)):
            source = pl.ds(pl.multiple_of(at, half), half)
            rows = pl.ds(row, half)
            k_stage[rows, :] = k_aux[source, :]
            v_stage[rows, :WIDTH] = values_ref[source, :]
            v_stage[rows, WIDTH:] = k_aux[source, WIDTH:]
            marks.append(onehot_t[:, source])
        k_t = k_stage[:, :WIDTH].T
        row_sums = jnp.zeros((block, 128), F32)
        grad_k = jnp.zeros((block, WIDTH), F32)
        grad_v = jnp.zeros((block, WIDTH), F32)
        lanes = pl.ds(pl.multiple_of(s * span, span), span)
        for h in range(HEADS):
            n = s * HEADS + h
            rows = slice(h * HEAD_DIM, (h + 1) * HEAD_DIM)
            p = jnp.exp2(dot(k_stage[...], q_feat[n]) * TO_LOG2)
            score_grad = p * dot(v_stage[...], g_feat[n])
            probs[h] = p.astype(BF)
            scaled[h] = (score_grad * SCALE).astype(BF)
            folded = score_grad[:, :128]
            for part in range(1, span // 128):
                folded = folded + score_grad[:, part * 128 : (part + 1) * 128]
            row_sums = row_sums + jnp.where(
                lane_row == h, jnp.sum(folded, axis=1, keepdims=True), 0.0
            )
            grad_v = grad_v + dot(probs[h], g_stack[n])
            grad_k = grad_k + dot(scaled[h], q_stack[n])
            grad_q_t[rows, lanes] += dot(k_t[rows, :], scaled[h])

        @pl.when(s == 0)
        def _():
            part_sum[step, :, :WIDTH] = grad_k
            part_sum[step, :, WIDTH:] = grad_v

        @pl.when(s == 1)
        def _():
            part_sum[step, :, :WIDTH] += grad_k
            part_sum[step, :, WIDTH:] += grad_v

        for piece in three_pieces(row_sums):
            for part in range(2):
                bias_sum[:SWEEPS, :] += dot(marks[part], piece[part * half : (part + 1) * half])

    def ring(step, upwards):
        rows = pl.ds(0, half) if upwards else pl.ds(half, half)
        return pltpu.make_async_remote_copy(
            src_ref=part_sum.at[step, rows],
            dst_ref=from_ring.at[step, rows],
            send_sem=sent_ring.at[step, 0 if upwards else 1],
            recv_sem=got_ring.at[step, 0 if upwards else 1],
            device_id={"lat": up if upwards else down},
            device_id_type=MESH,
        )

    over = pltpu.make_async_remote_copy(
        src_ref=part_sum.at[YS - 1],
        dst_ref=from_z,
        send_sem=sent_z,
        recv_sem=got_z,
        device_id={"lat": across},
        device_id_type=MESH,
    )

    def finish(step):
        turn = lax.rem(step, YS)

        @pl.when(turn > 0)
        def _():
            for upwards in (True, False):
                ring(step - 1, upwards).wait_recv()
            part_sum[step] += from_ring[step - 1]

        @pl.when(turn < YS - 1)
        def _():
            for upwards in (True, False):
                ring(step, upwards).start()

        @pl.when(step == YS - 1)
        def _():
            over.start()

    def per_item(t, unused):
        odd = lax.rem(t, 2)
        second = (t >= 14) | ((t >= 3) & (odd == 1))
        step = jnp.where(
            t < 3, t, jnp.where(t >= 14, t - 8, jnp.where(odd == 1, (t - 3) // 2, t // 2 + 1))
        )

        @pl.when(t == 3)
        def _():
            take_results(1)

        compute(step, jnp.where(second, 1, 0))

        @pl.when(t == 1)
        def _():
            combine(1)

        @pl.when(second & (step < 2 * YS - 1))
        def _():
            finish(step)

        return unused

    lax.fori_loop(0, 4 * YS, per_item, 0)

    swap = pltpu.make_async_remote_copy(
        src_ref=q_parts.at[1 - core],
        dst_ref=from_core,
        send_sem=sent_core,
        recv_sem=got_core,
        device_id={"pts": chip * 2 + 1 - core},
        device_id_type=MESH,
    )

    def bias_copy(k):
        return pltpu.make_async_remote_copy(
            src_ref=bias_sum.at[pl.ds(0, SWEEPS)],
            dst_ref=by_lat.at[lat * 2 + core],
            send_sem=sent_bias.at[k],
            recv_sem=got_bias.at[k],
            device_id=bias_peer(k),
            device_id_type=MESH,
        )

    def chip_copy(k):
        there = lax.rem(chip + k, chips)
        return pltpu.make_async_remote_copy(
            src_ref=q_mine.at[there],
            dst_ref=by_chip.at[chip],
            send_sem=sent_chip.at[k],
            recv_sem=got_chip.at[k],
            device_id={"pts": there * 2 + core},
            device_id_type=MESH,
        )

    every(1, 2 * lats, lambda k: bias_copy(k).start())
    grad_q = grad_q_t[...].T
    for p in range(count):
        q_parts[p % 2, p // 2] = grad_q[p * rows_out : (p + 1) * rows_out]
    swap.start()
    by_lat[lat * 2 + core] = bias_sum[:SWEEPS, :]
    every(1, 2 * lats, lambda k: bias_copy(k).wait_recv())
    bias = jnp.sum(by_lat[...], axis=0)
    swap.wait_recv()
    q_mine[:, :rows_out, :] = q_parts[core] + from_core[...]
    q_mine[:, rows_out:, :] = jnp.broadcast_to(bias, (chips, SWEEPS, 128))
    every(1, chips, lambda k: chip_copy(k).start())
    by_chip[chip] = q_mine[chip]
    finish(2 * YS - 1)
    over.wait_recv()
    done = part_sum[2 * YS - 1] + from_z[...]
    grad_k_ref[...] = done[:, :WIDTH]
    grad_v_ref[...] = done[:, WIDTH:]
    every(1, chips, lambda k: chip_copy(k).wait_recv())
    small_ref[...] = jnp.sum(by_chip[...], axis=0)

    others(0, count, lambda k: piece(k).wait_send())
    others(0, count, lambda k: result(k).wait_send())
    for step in range(2 * YS):
        if step % YS < YS - 1:
            for upwards in (True, False):
                ring(step, upwards).wait_send()
    over.wait_send()
    swap.wait_send()
    every(1, 2 * lats, lambda k: bias_copy(k).wait_send())
    every(1, chips, lambda k: chip_copy(k).wait_send())


def whole(latents, keys, values, sweep, sweep_bias, grad_out, count, lats):
    rows, points = latents.shape[0], keys.shape[0]
    block, span, chips = points // (2 * YS), rows // 2, count // 2
    cols = min(256, span)
    stat_tiles = HEADS * rows // 128
    share = stat_tiles // count
    rows_out = rows // count
    dma = pltpu.SemaphoreType.DMA
    return pl.pallas_call(
        functools.partial(whole_kernel, count, lats),
        out_shape=[
            jax.ShapeDtypeStruct((block, WIDTH), F32),
            jax.ShapeDtypeStruct((block, WIDTH), F32),
            jax.ShapeDtypeStruct((rows_out + SWEEPS, WIDTH), F32),
        ],
        in_specs=vmem_specs(6),
        out_specs=vmem_specs(3),
        scratch_shapes=[
            pltpu.VMEM((points, 2 * WIDTH), BF),
            pltpu.VMEM((HEADS, 48, points), BF),
            pltpu.VMEM((SWEEPS, points), BF),
            pltpu.VMEM((WIDTH, rows), BF),
            pltpu.VMEM((2 * HEADS, 2 * WIDTH, span), BF),
            pltpu.VMEM((2 * HEADS, 2 * WIDTH, span), BF),
            pltpu.VMEM((2 * HEADS, span, WIDTH), BF),
            pltpu.VMEM((2 * HEADS, span, WIDTH), BF),
            pltpu.VMEM((points, cols), F32),
            pltpu.VMEM((points, cols), F32),
            pltpu.VMEM((stat_tiles, 8, 128), F32),
            pltpu.VMEM((count, share, 8, 128), F32),
            pltpu.VMEM((share, 8, 128), F32),
            pltpu.VMEM((count, share, 8, 128), F32),
            pltpu.VMEM((block, 2 * WIDTH), BF),
            pltpu.VMEM((block, 2 * WIDTH), BF),
            pltpu.VMEM((HEADS, block, span), BF),
            pltpu.VMEM((HEADS, block, span), BF),
            pltpu.VMEM((2 * YS, block, 2 * WIDTH), F32),
            pltpu.VMEM((2 * YS, block, 2 * WIDTH), F32),
            pltpu.VMEM((block, 2 * WIDTH), F32),
            pltpu.VMEM((WIDTH, rows), F32),
            pltpu.VMEM((128, 128), F32),
            pltpu.VMEM((2, chips, rows_out, WIDTH), F32),
            pltpu.VMEM((chips, rows_out, WIDTH), F32),
            pltpu.VMEM((2 * lats, SWEEPS, 128), F32),
            pltpu.VMEM((chips, rows_out + SWEEPS, WIDTH), F32),
            pltpu.VMEM((chips, rows_out + SWEEPS, WIDTH), F32),
            dma((count,)),
            dma((count,)),
            dma((count,)),
            dma((count,)),
            dma((2 * YS, 2)),
            dma((2 * YS, 2)),
            dma,
            dma,
            dma,
            dma,
            dma((2 * lats,)),
            dma((2 * lats,)),
            dma((chips,)),
            dma((chips,)),
        ],
        compiler_params=pltpu.CompilerParams(
            collective_id=0, has_side_effects=True, vmem_limit_bytes=VMEM_BYTES
        ),
    )(latents, keys, values, sweep, sweep_bias, grad_out)


def deliver_kernel(small_ref, grad_k_ref, grad_v_ref, q_out, k_out, v_out, bias_out, square):
    rows_out = q_out.shape[0]
    q_out[...] = small_ref[:rows_out, :]
    k_out[...] = grad_k_ref[...]
    v_out[...] = grad_v_ref[...]
    square[...] = jnp.zeros_like(square)
    square[:SWEEPS, :] = small_ref[rows_out:, :]
    bias_out[...] = square[...].T[:HEADS, :SWEEPS]


def deliver(small, grad_k, grad_v):
    return pl.pallas_call(
        deliver_kernel,
        out_shape=[
            jax.ShapeDtypeStruct((small.shape[0] - SWEEPS, WIDTH), F32),
            jax.ShapeDtypeStruct(grad_k.shape, F32),
            jax.ShapeDtypeStruct(grad_v.shape, F32),
            jax.ShapeDtypeStruct((HEADS, SWEEPS), F32),
        ],
        in_specs=vmem_specs(3),
        out_specs=vmem_specs(4),
        scratch_shapes=[pltpu.VMEM((128, 128), F32)],
    )(small, grad_k, grad_v)


def per_device(count, lats, latents, keys, values, sweep, sweep_bias, grad_out):
    grad_k, grad_v, small = whole(
        latents, keys, values, sweep.reshape(1, -1), sweep_bias, grad_out, count, lats
    )
    return tuple(deliver(small, grad_k, grad_v))


def solution(mesh):
    return jax.shard_map(
        functools.partial(per_device, mesh.shape["pts"], mesh.shape["lat"]),
        mesh=mesh,
        in_specs=(P("lat", None), P("pts", None), P("pts", None), P("pts"), P(), P("lat", None)),
        out_specs=(P(("lat", "pts"), None), P(("pts", "lat"), None), P(("pts", "lat"), None), P()),
        check_vma=False,
    )
```

```python
import functools
import math

import jax
import jax.numpy as jnp
from jax import lax
from jax.experimental import pallas as pl
from jax.experimental.pallas import tpu as pltpu
from jax.sharding import PartitionSpec as P

HEADS = 4
HEAD_DIM = 32
WIDTH = HEADS * HEAD_DIM
SWEEPS = 16
SCALE = HEAD_DIM**-0.5
LOG2E = math.log2(math.e)
TO_LOG2 = SCALE * LOG2E
YS = 4
ONES_ROW = 3 * SWEEPS
BF = jnp.bfloat16
F32 = jnp.float32
MESH = pl.DeviceIdType.MESH
VMEM_BYTES = 56 * 1024 * 1024


def dot(a, b):
    return jnp.dot(a, b, preferred_element_type=F32)


def three_pieces(x):
    hi = x.astype(BF)
    rest = x - hi.astype(F32)
    mid = rest.astype(BF)
    low = (rest - mid.astype(F32)).astype(BF)
    return hi, mid, low


def vmem_specs(count):
    return [pl.BlockSpec(memory_space=pltpu.VMEM)] * count


def whole_kernel(
    count,
    lats,
    latents_ref,
    keys_ref,
    values_ref,
    sweep_ref,
    sweep_bias_ref,
    grad_out_ref,
    grad_k_ref,
    grad_v_ref,
    small_ref,
    k_aux,
    value_rows,
    onehot_t,
    lat_rows,
    out_rows,
    g_t,
    q_feat,
    g_feat,
    q_stack,
    g_stack,
    scores_0,
    scores_1,
    stats,
    arrived,
    mine,
    final,
    k_stage,
    v_stage,
    probs,
    scaled,
    mark_stage,
    part_sum,
    from_ring,
    relay,
    from_z,
    grad_q_t,
    bias_sum,
    q_parts,
    from_core,
    by_lat,
    bias_mine,
    by_bias,
    q_mine,
    by_chip,
    sent_1,
    got_1,
    sent_2,
    got_2,
    sent_ring,
    got_ring,
    sent_near,
    got_near,
    sent_far,
    got_far,
    sent_core,
    got_core,
    sent_bias,
    got_bias,
    sent_all,
    got_all,
    sent_chip,
    got_chip,
):
    points, latents = keys_ref.shape[0], latents_ref.shape[0]
    span = latents // 2
    cols = min(256, span)
    per_span = span // cols
    tiles = HEADS * 2 * per_span
    pairs = tiles // 2
    chunk = min(512, points)
    chunks = points // chunk
    block = points // (2 * YS)
    half = block // 2
    quarter = block // 4
    chips = count // 2
    near_z = 4 if chips % 4 == 0 else chips
    share = stats.shape[0] // count
    rows_out = latents // count

    me = lax.axis_index("pts")
    lat = lax.axis_index("lat")
    core = lax.rem(me, 2)
    chip = me // 2
    z, y = lat // YS, lax.rem(lat, YS)
    up = z * YS + lax.rem(y + 1, YS)
    down = z * YS + lax.rem(y + YS - 1, YS)
    height = z * near_z + lax.rem(chip, near_z)

    def at_height(shift):
        there = lax.rem(height + shift + 2 * near_z, 2 * near_z)
        return {
            "pts": ((chip // near_z) * near_z + lax.rem(there, near_z)) * 2 + core,
            "lat": (there // near_z) * YS + y,
        }

    def every(start, stop, action):
        def step(k, unused):
            action(k)
            return unused

        lax.fori_loop(start, stop, step, 0)

    def others(start, stop, action):
        def guarded(k):
            @pl.when(k != me)
            def _():
                action(k)

        every(start, stop, guarded)

    barrier = pltpu.get_barrier_semaphore()

    def bias_peer(k):
        there = lax.rem(lat * 2 + core + k, 2 * lats)
        return {"pts": chip * 2 + lax.rem(there, 2), "lat": there // 2}

    def greet_pts(k):
        pl.semaphore_signal(
            barrier, inc=1, device_id={"pts": lax.rem(me + k, count)}, device_id_type=MESH
        )

    def greet_lat(k):
        pl.semaphore_signal(barrier, inc=1, device_id=bias_peer(k), device_id_type=MESH)

    every(1, count, greet_pts)
    every(1, 2 * lats, greet_lat)
    for shift in (1, -1, near_z - 1, 1 - near_z):
        pl.semaphore_signal(barrier, inc=1, device_id=at_height(shift), device_id_type=MESH)

    k_aux[:, :WIDTH] = keys_ref[...]

    def build(c):
        rows = pl.ds(pl.multiple_of(c * chunk, chunk), chunk)
        swept = sweep_ref[:, rows]
        row = lax.broadcasted_iota(jnp.int32, (WIDTH, chunk), 0)
        marked = (row < ONES_ROW) & (lax.rem(row, SWEEPS) == swept)
        ones = (row >= ONES_ROW) & (row < ONES_ROW + 3)
        aux_t = jnp.where(marked | ones, 1.0, 0.0)
        onehot_t[:, rows] = aux_t[:SWEEPS].astype(BF)
        k_aux[rows, WIDTH:] = aux_t.T.astype(BF)
        value_t = values_ref[rows, :].T
        for h in range(HEADS):
            value_rows[h, :HEAD_DIM, rows] = value_t[h * HEAD_DIM : (h + 1) * HEAD_DIM, :]
            value_rows[h, HEAD_DIM:, rows] = jnp.where(row[:16] == 0, 1.0, 0.0).astype(BF)

    every(0, chunks, build)
    order = [p for parity in range(2) for p in range(count) if (p // 2) % 2 == parity]
    for at, p in enumerate(order):
        to, of = slice(at * rows_out, (at + 1) * rows_out), slice(p * rows_out, (p + 1) * rows_out)
        lat_rows[to, :] = latents_ref[of, :]
        out_rows[to, :] = grad_out_ref[of, :]
    q_t = lat_rows[...].T
    g_t[...] = out_rows[...].T
    lane = lax.broadcasted_iota(jnp.int32, (span, WIDTH), 1)
    eye = lax.broadcasted_iota(jnp.int32, (SWEEPS, SWEEPS), 0) == lax.broadcasted_iota(
        jnp.int32, (SWEEPS, SWEEPS), 1
    )
    for h in range(HEADS):
        rows = slice(h * HEAD_DIM, (h + 1) * HEAD_DIM)
        column = jnp.sum(
            jnp.where(eye, sweep_bias_ref[h : h + 1, :], 0.0), axis=1, keepdims=True
        ) * (1.0 / SCALE)
        bias_pieces = three_pieces(jnp.broadcast_to(column, (SWEEPS, span)))
        mine_lanes = (lane >= h * HEAD_DIM) & (lane < (h + 1) * HEAD_DIM)
        for s in range(2):
            n = s * HEADS + h
            here = slice(s * span, (s + 1) * span)
            for source, stack in ((lat_rows, q_stack), (out_rows, g_stack)):
                stack[n] = jnp.where(mine_lanes, source[here, :].astype(F32), 0.0).astype(BF)
            q_feat[n] = jnp.zeros((2 * WIDTH, span), BF)
            g_feat[n] = jnp.zeros((2 * WIDTH, span), BF)
            q_feat[n, rows, :] = q_t[rows, here]
            g_feat[n, rows, :] = g_t[rows, here]
            for index, piece in enumerate(bias_pieces):
                q_feat[n, WIDTH + index * SWEEPS : WIDTH + (index + 1) * SWEEPS, :] = piece
    grad_q_t[...] = jnp.zeros_like(grad_q_t)
    bias_sum[...] = jnp.zeros_like(bias_sum)

    def piece(owner):
        return pltpu.make_async_remote_copy(
            src_ref=stats.at[pl.ds(owner * share, share)],
            dst_ref=arrived.at[me],
            send_sem=sent_1.at[owner],
            recv_sem=got_1.at[me],
            device_id={"pts": owner},
            device_id_type=MESH,
        )

    def piece_from(source):
        return pltpu.make_async_remote_copy(
            src_ref=mine,
            dst_ref=arrived.at[source],
            send_sem=sent_1.at[source],
            recv_sem=got_1.at[source],
            device_id={"pts": source},
            device_id_type=MESH,
        )

    def result(there):
        return pltpu.make_async_remote_copy(
            src_ref=mine,
            dst_ref=final.at[me],
            send_sem=sent_2.at[there],
            recv_sem=got_2.at[me],
            device_id={"pts": there},
            device_id_type=MESH,
        )

    def result_from(owner):
        return pltpu.make_async_remote_copy(
            src_ref=mine,
            dst_ref=final.at[owner],
            send_sem=sent_2.at[owner],
            recv_sem=got_2.at[owner],
            device_id={"pts": owner},
            device_id_type=MESH,
        )

    def owners(s):
        return s * (count // 2), (s + 1) * (count // 2)

    def send_pieces(s):
        others(*owners(s), lambda k: piece(k).start())

    def combine(s):
        first, last = owners(s)

        @pl.when((me >= first) & (me < last))
        def _():
            arrived[me] = stats[pl.ds(me * share, share)]
            others(0, count, lambda k: piece_from(k).wait_recv())
            for part in range(share):
                top = arrived[:, part, 0, :]
                best = jnp.max(top, axis=0, keepdims=True)
                weight = jnp.exp2(top - best)
                total = jnp.sum(weight * arrived[:, part, 1, :], axis=0, keepdims=True)
                weighted = jnp.sum(weight * arrived[:, part, 2, :], axis=0, keepdims=True)
                rounded_total = jnp.sum(weight * arrived[:, part, 3, :], axis=0, keepdims=True)
                offset = (best + jnp.log(total) * LOG2E) * (-1.0 / TO_LOG2)
                row = lax.broadcasted_iota(jnp.int32, (8, 128), 0)
                mine[part] = jnp.where(row == 0, offset, -(weighted / rounded_total))
            others(0, count, lambda k: result(k).start())
            final[me] = mine[...]

    def take_results(s):
        others(*owners(s), lambda k: result_from(k).wait_recv())
        row16 = lax.broadcasted_iota(jnp.int32, (16, 128), 0)
        per_tile = cols // 128
        for n in range(tiles // 2):
            it, h = n // HEADS, n % HEADS
            for part in range(per_tile):
                number = s * (tiles // 2) * per_tile + n * per_tile + part
                tile = final[number // share, number % share]
                left = it * cols + part * 128
                for index, feat in ((0, q_feat), (1, g_feat)):
                    hi, mid, low = three_pieces(tile[index : index + 1, :])
                    feat[
                        s * HEADS + h,
                        WIDTH + ONES_ROW : WIDTH + ONES_ROW + 16,
                        left : left + 128,
                    ] = jnp.where(
                        row16 == 0,
                        hi.astype(F32),
                        jnp.where(
                            row16 == 1, mid.astype(F32), jnp.where(row16 == 2, low.astype(F32), 0.0)
                        ),
                    ).astype(BF)

    lowest = jnp.full((32, cols), -jnp.inf, F32)

    def feature_of(n):
        it = n // HEADS
        return (
            (it // per_span) * HEADS + lax.rem(n, HEADS),
            pl.ds(pl.multiple_of(lax.rem(it, per_span) * cols, cols), cols),
        )

    def score_chunk(n, into, c, top):
        index, lanes = feature_of(n)
        rows = pl.ds(c * chunk, chunk)
        s = dot(k_aux[rows, :], q_feat[index, :, lanes]) * TO_LOG2
        into[rows, :] = s
        return jnp.maximum(top, jnp.max(s.reshape(chunk // 32, 32, cols), axis=0))

    def tile_sums(n, scores, top_rows, following, into):
        top = jnp.max(top_rows, axis=0, keepdims=True)
        head = lax.rem(n, HEADS)
        next_top = lowest
        total = jnp.zeros((32, cols), F32)
        out = jnp.zeros((48, cols), F32)
        for c in range(chunks):
            rows = pl.ds(c * chunk, chunk)
            e = jnp.exp2(scores[rows, :] - top)
            total = total + jnp.sum(e.reshape(chunk // 32, 32, cols), axis=0)
            out = out + dot(value_rows[head, :, rows], e.astype(BF))
            next_top = score_chunk(following, into, c, next_top)
        total = jnp.sum(total, axis=0, keepdims=True)
        g = g_t[
            pl.ds(pl.multiple_of(head * HEAD_DIM, HEAD_DIM), HEAD_DIM),
            pl.ds(pl.multiple_of((n // HEADS) * cols, cols), cols),
        ].astype(F32)
        weighted = jnp.sum(out[:HEAD_DIM] * g, axis=0, keepdims=True)
        rounded_total = out[HEAD_DIM : HEAD_DIM + 1]
        row = lax.broadcasted_iota(jnp.int32, (8, cols), 0)
        tile = jnp.where(
            row == 0, top, jnp.where(row == 1, total, jnp.where(row == 2, weighted, rounded_total))
        )
        for part in range(cols // 128):
            stats[n * (cols // 128) + part] = tile[:, part * 128 : (part + 1) * 128]
        return next_top

    first_top = lowest
    for c in range(chunks):
        first_top = score_chunk(0, scores_0, c, first_top)

    def per_pair(pair, top_rows):
        n = pair * 2
        top_rows = tile_sums(n, scores_0, top_rows, n + 1, scores_1)
        top_rows = tile_sums(n + 1, scores_1, top_rows, lax.rem(n + 2, tiles), scores_0)

        @pl.when(pair == pairs // 2 - 1)
        def _():
            pl.semaphore_wait(barrier, count - 1 + 2 * lats - 1 + 4)
            send_pieces(0)

        @pl.when(pair == pairs - 2)
        def _():
            combine(0)

        return top_rows

    lax.fori_loop(0, pairs, per_pair, first_top)
    send_pieces(1)
    take_results(0)

    lane_row = lax.broadcasted_iota(jnp.int32, (block, 128), 1)

    def compute(item, s):
        owner_z = jnp.where(item < YS, 1 - z, z)
        sub = lax.rem(item // 2, 2)
        for part in range(2):
            turn = lax.rem(item, 2) * 2 + part
            y_up = lax.rem(y + 2 * YS - 1 - turn, YS)
            y_down = lax.rem(y + 1 + turn, YS)
            for place, at in (
                (0, (owner_z * YS + y_up) * block + sub * quarter),
                (1, (owner_z * YS + y_down) * block + half + sub * quarter),
            ):
                source = pl.ds(pl.multiple_of(at, quarter), quarter)
                row = (part * 2 + place) * quarter
                rows = pl.ds(row, quarter)
                k_stage[rows, :] = k_aux[source, :]
                v_stage[rows, :WIDTH] = values_ref[source, :]
                v_stage[rows, WIDTH:] = k_aux[source, WIDTH:]
                mark_stage[:, row : row + quarter] = onehot_t[:, source]
        k_t = k_stage[:, :WIDTH].T
        row_sums = jnp.zeros((block, 128), F32)
        grad_k = jnp.zeros((block, WIDTH), F32)
        grad_v = jnp.zeros((block, WIDTH), F32)
        lanes = pl.ds(pl.multiple_of(s * span, span), span)
        for h in range(HEADS):
            n = s * HEADS + h
            rows = slice(h * HEAD_DIM, (h + 1) * HEAD_DIM)
            p = jnp.exp2(dot(k_stage[...], q_feat[n]) * TO_LOG2)
            score_grad = p * dot(v_stage[...], g_feat[n])
            probs[h] = p.astype(BF)
            scaled[h] = (score_grad * SCALE).astype(BF)
            folded = score_grad[:, :128]
            for part in range(1, span // 128):
                folded = folded + score_grad[:, part * 128 : (part + 1) * 128]
            row_sums = row_sums + jnp.where(
                lane_row == h, jnp.sum(folded, axis=1, keepdims=True), 0.0
            )
            grad_v = grad_v + dot(probs[h], g_stack[n])
            grad_k = grad_k + dot(scaled[h], q_stack[n])
            grad_q_t[rows, lanes] += dot(k_t[rows, :], scaled[h])

        for part in range(2):
            rows = slice(part * half, (part + 1) * half)
            unit = item * 2 + part

            @pl.when(s == 0)
            def _():
                part_sum[unit, :, :WIDTH] = grad_k[rows]
                part_sum[unit, :, WIDTH:] = grad_v[rows]

            @pl.when(s == 1)
            def _():
                part_sum[unit, :, :WIDTH] += grad_k[rows]
                part_sum[unit, :, WIDTH:] += grad_v[rows]

        for piece in three_pieces(row_sums):
            bias_sum[:SWEEPS, :] += dot(mark_stage[...], piece)

    def ring(unit, way):
        rows = pl.ds(way * quarter, quarter)
        return pltpu.make_async_remote_copy(
            src_ref=part_sum.at[unit, rows],
            dst_ref=from_ring.at[unit, rows],
            send_sem=sent_ring.at[unit, way],
            recv_sem=got_ring.at[unit, way],
            device_id={"lat": down if way else up},
            device_id_type=MESH,
        )

    def near(sub, way):
        return pltpu.make_async_remote_copy(
            src_ref=part_sum.at[sub * YS + YS - 1, pl.ds(way * quarter, quarter)],
            dst_ref=relay.at[sub, way],
            send_sem=sent_near.at[sub, way],
            recv_sem=got_near.at[sub, way],
            device_id=at_height(-1 if way else 1),
            device_id_type=MESH,
        )

    def far(sub, way):
        return pltpu.make_async_remote_copy(
            src_ref=relay.at[sub, way],
            dst_ref=from_z.at[sub, pl.ds(way * quarter, quarter)],
            send_sem=sent_far.at[sub, way],
            recv_sem=got_far.at[sub, way],
            device_id=at_height(1 - near_z if way else near_z - 1),
            device_id_type=MESH,
        )

    def finish(unit):
        turn = lax.rem(unit, YS)

        @pl.when(turn > 0)
        def _():
            for way in range(2):
                ring(unit - 1, way).wait_recv()
            part_sum[unit] += from_ring[unit - 1]

        @pl.when(turn < YS - 1)
        def _():
            for way in range(2):
                ring(unit, way).start()

        @pl.when((turn == YS - 1) & (unit < 2 * YS))
        def _():
            for way in range(2):
                near(unit // YS, way).start()

    def swap(s):
        return pltpu.make_async_remote_copy(
            src_ref=q_parts.at[s, 1 - core],
            dst_ref=from_core.at[s],
            send_sem=sent_core.at[s],
            recv_sem=got_core.at[s],
            device_id={"pts": chip * 2 + 1 - core},
            device_id_type=MESH,
        )

    def start_swap(s):
        grad_q = grad_q_t[:, s * span : (s + 1) * span].T
        for part in range(chips):
            q_parts[s, part % 2, part // 2] = grad_q[part * rows_out : (part + 1) * rows_out]
        swap(s).start()

    def per_item(t, unused):
        swapped = (t == 1) | (t == 2)
        item = jnp.where(swapped, 2 - t, t // 2)
        s = jnp.where(swapped, t - 1, lax.rem(t, 2))

        @pl.when(t == 2)
        def _():
            take_results(1)

        compute(item, s)

        @pl.when(t == 0)
        def _():
            combine(1)

        @pl.when(t >= 2)
        def _():
            finish(jnp.where(t < 6, t - 2, t - 1))

        @pl.when(t == 5)
        def _():
            finish(4)

        for sub, when in ((0, 7), (1, 10)):

            @pl.when(t == when)
            def _():
                for way in range(2):
                    near(sub, way).wait_recv()
                    far(sub, way).start()

        @pl.when(t == 4 * YS - 2)
        def _():
            start_swap(0)

        return unused

    lax.fori_loop(0, 4 * YS, per_item, 0)

    def bias_copy(k):
        return pltpu.make_async_remote_copy(
            src_ref=bias_sum.at[pl.ds(0, SWEEPS)],
            dst_ref=by_lat.at[lat * 2 + core],
            send_sem=sent_bias.at[k],
            recv_sem=got_bias.at[k],
            device_id=bias_peer(k),
            device_id_type=MESH,
        )

    def bias_all(k):
        return pltpu.make_async_remote_copy(
            src_ref=bias_mine,
            dst_ref=by_bias.at[chip],
            send_sem=sent_all.at[k],
            recv_sem=got_all.at[k],
            device_id={"pts": lax.rem(chip + k, chips) * 2 + core},
            device_id_type=MESH,
        )

    def chip_copy(s, m):
        there = 2 * m + s
        return pltpu.make_async_remote_copy(
            src_ref=q_mine.at[s, m],
            dst_ref=by_chip.at[chip],
            send_sem=sent_chip.at[there],
            recv_sem=got_chip.at[chip],
            device_id={"pts": there * 2 + core},
            device_id_type=MESH,
        )

    def chip_from(source):
        return pltpu.make_async_remote_copy(
            src_ref=q_mine.at[0, 0],
            dst_ref=by_chip.at[source],
            send_sem=sent_chip.at[source],
            recv_sem=got_chip.at[source],
            device_id={"pts": source * 2 + core},
            device_id_type=MESH,
        )

    def chips_of(s, action):
        def guarded(m):
            @pl.when(2 * m + s != chip)
            def _():
                action(m)

        every(0, chips // 2, guarded)

    def send_chips(s):
        swap(s).wait_recv()
        q_mine[s] = q_parts[s, core] + from_core[s]
        chips_of(s, lambda m: chip_copy(s, m).start())

    every(1, 2 * lats, lambda k: bias_copy(k).start())
    start_swap(1)
    send_chips(0)
    by_lat[lat * 2 + core] = bias_sum[:SWEEPS, :]
    every(1, 2 * lats, lambda k: bias_copy(k).wait_recv())
    bias_mine[...] = jnp.sum(by_lat[...], axis=0)
    every(1, chips, lambda k: bias_all(k).start())
    send_chips(1)
    by_bias[chip] = bias_mine[...]
    by_chip[chip] = q_mine[lax.rem(chip, 2), chip // 2]
    finish(4 * YS - 1)
    for sub in range(2):
        for way in range(2):
            far(sub, way).wait_recv()
        done = part_sum[(2 + sub) * YS + YS - 1] + from_z[sub]
        for way in range(2):
            source = slice(way * quarter, (way + 1) * quarter)
            rows = slice(way * half + sub * quarter, way * half + (sub + 1) * quarter)
            grad_k_ref[rows, :] = done[source, :WIDTH]
            grad_v_ref[rows, :] = done[source, WIDTH:]

    def got_from(c):
        @pl.when(c != chip)
        def _():
            chip_from(c).wait_recv()

    every(0, chips, got_from)
    small_ref[:rows_out, :] = jnp.sum(by_chip[...], axis=0)
    every(1, chips, lambda k: bias_all(k).wait_recv())
    small_ref[rows_out:, :] = jnp.sum(by_bias[...], axis=0)

    others(0, count, lambda k: piece(k).wait_send())
    others(0, count, lambda k: result(k).wait_send())
    for unit in range(4 * YS):
        if unit % YS < YS - 1:
            for way in range(2):
                ring(unit, way).wait_send()
    for sub in range(2):
        for way in range(2):
            near(sub, way).wait_send()
            far(sub, way).wait_send()
        swap(sub).wait_send()
        chips_of(sub, lambda m: chip_copy(sub, m).wait_send())
    every(1, 2 * lats, lambda k: bias_copy(k).wait_send())
    every(1, chips, lambda k: bias_all(k).wait_send())


def whole(latents, keys, values, sweep, sweep_bias, grad_out, count, lats):
    rows, points = latents.shape[0], keys.shape[0]
    block, span, chips = points // (2 * YS), rows // 2, count // 2
    cols = min(256, span)
    stat_tiles = HEADS * rows // 128
    share = stat_tiles // count
    rows_out = rows // count
    dma = pltpu.SemaphoreType.DMA
    return pl.pallas_call(
        functools.partial(whole_kernel, count, lats),
        out_shape=[
            jax.ShapeDtypeStruct((block, WIDTH), F32),
            jax.ShapeDtypeStruct((block, WIDTH), F32),
            jax.ShapeDtypeStruct((rows_out + SWEEPS, WIDTH), F32),
        ],
        in_specs=vmem_specs(6),
        out_specs=vmem_specs(3),
        scratch_shapes=[
            pltpu.VMEM((points, 2 * WIDTH), BF),
            pltpu.VMEM((HEADS, 48, points), BF),
            pltpu.VMEM((SWEEPS, points), BF),
            pltpu.VMEM((rows, WIDTH), BF),
            pltpu.VMEM((rows, WIDTH), BF),
            pltpu.VMEM((WIDTH, rows), BF),
            pltpu.VMEM((2 * HEADS, 2 * WIDTH, span), BF),
            pltpu.VMEM((2 * HEADS, 2 * WIDTH, span), BF),
            pltpu.VMEM((2 * HEADS, span, WIDTH), BF),
            pltpu.VMEM((2 * HEADS, span, WIDTH), BF),
            pltpu.VMEM((points, cols), F32),
            pltpu.VMEM((points, cols), F32),
            pltpu.VMEM((stat_tiles, 8, 128), F32),
            pltpu.VMEM((count, share, 8, 128), F32),
            pltpu.VMEM((share, 8, 128), F32),
            pltpu.VMEM((count, share, 8, 128), F32),
            pltpu.VMEM((block, 2 * WIDTH), BF),
            pltpu.VMEM((block, 2 * WIDTH), BF),
            pltpu.VMEM((HEADS, block, span), BF),
            pltpu.VMEM((HEADS, block, span), BF),
            pltpu.VMEM((SWEEPS, block), BF),
            pltpu.VMEM((4 * YS, block // 2, 2 * WIDTH), F32),
            pltpu.VMEM((4 * YS, block // 2, 2 * WIDTH), F32),
            pltpu.VMEM((2, 2, block // 4, 2 * WIDTH), F32),
            pltpu.VMEM((2, block // 2, 2 * WIDTH), F32),
            pltpu.VMEM((WIDTH, rows), F32),
            pltpu.VMEM((128, 128), F32),
            pltpu.VMEM((2, 2, chips // 2, rows_out, WIDTH), F32),
            pltpu.VMEM((2, chips // 2, rows_out, WIDTH), F32),
            pltpu.VMEM((2 * lats, SWEEPS, 128), F32),
            pltpu.VMEM((SWEEPS, 128), F32),
            pltpu.VMEM((chips, SWEEPS, 128), F32),
            pltpu.VMEM((2, chips // 2, rows_out, WIDTH), F32),
            pltpu.VMEM((chips, rows_out, WIDTH), F32),
            dma((count,)),
            dma((count,)),
            dma((count,)),
            dma((count,)),
            dma((4 * YS, 2)),
            dma((4 * YS, 2)),
            dma((2, 2)),
            dma((2, 2)),
            dma((2, 2)),
            dma((2, 2)),
            dma((2,)),
            dma((2,)),
            dma((2 * lats,)),
            dma((2 * lats,)),
            dma((chips,)),
            dma((chips,)),
            dma((chips,)),
            dma((chips,)),
        ],
        compiler_params=pltpu.CompilerParams(
            collective_id=0, has_side_effects=True, vmem_limit_bytes=VMEM_BYTES
        ),
    )(latents, keys, values, sweep, sweep_bias, grad_out)


def deliver_kernel(small_ref, grad_k_ref, grad_v_ref, q_out, k_out, v_out, bias_out, square):
    rows_out = q_out.shape[0]
    q_out[...] = small_ref[:rows_out, :]
    k_out[...] = grad_k_ref[...]
    v_out[...] = grad_v_ref[...]
    square[...] = jnp.zeros_like(square)
    square[:SWEEPS, :] = small_ref[rows_out:, :]
    bias_out[...] = square[...].T[:HEADS, :SWEEPS]


def deliver(small, grad_k, grad_v):
    return pl.pallas_call(
        deliver_kernel,
        out_shape=[
            jax.ShapeDtypeStruct((small.shape[0] - SWEEPS, WIDTH), F32),
            jax.ShapeDtypeStruct(grad_k.shape, F32),
            jax.ShapeDtypeStruct(grad_v.shape, F32),
            jax.ShapeDtypeStruct((HEADS, SWEEPS), F32),
        ],
        in_specs=vmem_specs(3),
        out_specs=vmem_specs(4),
        scratch_shapes=[pltpu.VMEM((128, 128), F32)],
    )(small, grad_k, grad_v)


def per_device(count, lats, latents, keys, values, sweep, sweep_bias, grad_out):
    grad_k, grad_v, small = whole(
        latents, keys, values, sweep.reshape(1, -1), sweep_bias, grad_out, count, lats
    )
    return tuple(deliver(small, grad_k, grad_v))


def solution(mesh):
    return jax.shard_map(
        functools.partial(per_device, mesh.shape["pts"], mesh.shape["lat"]),
        mesh=mesh,
        in_specs=(P("lat", None), P("pts", None), P("pts", None), P("pts"), P(), P("lat", None)),
        out_specs=(P(("lat", "pts"), None), P(("pts", "lat"), None), P(("pts", "lat"), None), P()),
        check_vma=False,
    )
```

```python
import functools
import math

import jax
import jax.numpy as jnp
from jax import lax
from jax.experimental import pallas as pl
from jax.experimental.pallas import tpu as pltpu
from jax.sharding import PartitionSpec as P

HEADS = 4
HEAD_DIM = 32
WIDTH = HEADS * HEAD_DIM
SWEEPS = 16
SCALE = HEAD_DIM**-0.5
LOG2E = math.log2(math.e)
TO_LOG2 = SCALE * LOG2E
YS = 4
ONES_ROW = 3 * SWEEPS
BF = jnp.bfloat16
F32 = jnp.float32
MESH = pl.DeviceIdType.MESH
VMEM_BYTES = 56 * 1024 * 1024


def dot(a, b):
    return jnp.dot(a, b, preferred_element_type=F32)


def three_pieces(x):
    hi = x.astype(BF)
    rest = x - hi.astype(F32)
    mid = rest.astype(BF)
    low = (rest - mid.astype(F32)).astype(BF)
    return hi, mid, low


def vmem_specs(count):
    return [pl.BlockSpec(memory_space=pltpu.VMEM)] * count


def whole_kernel(
    count,
    lats,
    latents_ref,
    keys_ref,
    values_ref,
    sweep_ref,
    sweep_bias_ref,
    grad_out_ref,
    grad_k_ref,
    grad_v_ref,
    small_ref,
    k_aux,
    value_rows,
    onehot_t,
    g_t,
    q_feat,
    g_feat,
    q_stack,
    g_stack,
    scores_0,
    scores_1,
    stats,
    from_sibling,
    stats_1,
    stats_x,
    stats_2,
    stats_z,
    k_stage,
    v_stage,
    mark_stage,
    probs,
    scaled,
    part_sum,
    from_ring,
    relay,
    from_z,
    grad_q_t,
    bias_sum,
    q_parts,
    from_core,
    bias_1,
    q_x,
    got_q_x,
    q_z,
    got_q_z,
    bias_2,
    bias_z,
    sent_s1,
    got_s1,
    sent_sx,
    got_sx,
    sent_sz,
    got_sz,
    sent_ring,
    got_ring,
    sent_near,
    got_near,
    sent_far,
    got_far,
    sent_core,
    got_core,
    sent_b1,
    got_b1,
    sent_qx,
    got_qx,
    sent_qz,
    got_qz,
    sent_b2,
    got_b2,
):
    points, latents = keys_ref.shape[0], latents_ref.shape[0]
    span = latents // 2
    cols = min(256, span)
    per_span = span // cols
    tiles = HEADS * 2 * per_span
    pairs = tiles // 2
    chunk = min(512, points)
    chunks = points // chunk
    block = points // (2 * YS)
    half = block // 2
    quarter = block // 4
    chips = count // 2
    nz = 4 if chips % 4 == 0 else chips
    nx = chips // nz
    heights = 2 * nz
    rows_out = latents // count

    me = lax.axis_index("pts")
    lat = lax.axis_index("lat")
    core = lax.rem(me, 2)
    chip = me // 2
    z, y = lat // YS, lax.rem(lat, YS)
    up = z * YS + lax.rem(y + 1, YS)
    down = z * YS + lax.rem(y + YS - 1, YS)
    x, zl = chip // nz, lax.rem(chip, nz)
    height = z * nz + zl

    def x_peer(k):
        return {"pts": (lax.rem(x + k, nx) * nz + zl) * 2 + core}

    def z_peer(k):
        return {"pts": (x * nz + lax.rem(zl + k, nz)) * 2 + core}

    def y_peer(k):
        there = lax.rem(y * 2 + core + k, 2 * YS)
        return {"pts": chip * 2 + lax.rem(there, 2), "lat": z * YS + there // 2}

    def at_height(shift):
        there = lax.rem(height + shift + heights, heights)
        return {"pts": (x * nz + lax.rem(there, nz)) * 2 + core, "lat": (there // nz) * YS + y}

    def remote(src, dst, sent, got, device):
        return pltpu.make_async_remote_copy(
            src_ref=src,
            dst_ref=dst,
            send_sem=sent,
            recv_sem=got,
            device_id=device,
            device_id_type=MESH,
        )

    def every(start, stop, action):
        def step(k, unused):
            action(k)
            return unused

        lax.fori_loop(start, stop, step, 0)

    barrier = pltpu.get_barrier_semaphore()
    greeted = (
        [x_peer(k) for k in range(1, nx)]
        + [at_height(k) for k in range(1, heights)]
        + [y_peer(k) for k in range(1, 2 * YS)]
    )
    for device in greeted:
        pl.semaphore_signal(barrier, inc=1, device_id=device, device_id_type=MESH)

    k_aux[:, :WIDTH] = keys_ref[...]

    def build(c):
        rows = pl.ds(pl.multiple_of(c * chunk, chunk), chunk)
        swept = sweep_ref[:, rows]
        row = lax.broadcasted_iota(jnp.int32, (WIDTH, chunk), 0)
        marked = (row < ONES_ROW) & (lax.rem(row, SWEEPS) == swept)
        ones = (row >= ONES_ROW) & (row < ONES_ROW + 3)
        aux_t = jnp.where(marked | ones, 1.0, 0.0)
        onehot_t[:, rows] = aux_t[:SWEEPS].astype(BF)
        k_aux[rows, WIDTH:] = aux_t.T.astype(BF)
        value_t = values_ref[rows, :].T
        for h in range(HEADS):
            value_rows[h, :HEAD_DIM, rows] = value_t[h * HEAD_DIM : (h + 1) * HEAD_DIM, :]
            value_rows[h, HEAD_DIM:, rows] = jnp.where(row[:16] == 0, 1.0, 0.0).astype(BF)

    every(0, chunks, build)
    q_t = latents_ref[...].T
    g_t[...] = grad_out_ref[...].T
    lane = lax.broadcasted_iota(jnp.int32, (span, WIDTH), 1)
    eye = lax.broadcasted_iota(jnp.int32, (SWEEPS, SWEEPS), 0) == lax.broadcasted_iota(
        jnp.int32, (SWEEPS, SWEEPS), 1
    )
    for h in range(HEADS):
        rows = slice(h * HEAD_DIM, (h + 1) * HEAD_DIM)
        column = jnp.sum(
            jnp.where(eye, sweep_bias_ref[h : h + 1, :], 0.0), axis=1, keepdims=True
        ) * (1.0 / SCALE)
        bias_pieces = three_pieces(jnp.broadcast_to(column, (SWEEPS, span)))
        mine_lanes = (lane >= h * HEAD_DIM) & (lane < (h + 1) * HEAD_DIM)
        for s in range(2):
            n = s * HEADS + h
            here = slice(s * span, (s + 1) * span)
            for source, stack in ((latents_ref, q_stack), (grad_out_ref, g_stack)):
                stack[n] = jnp.where(mine_lanes, source[here, :].astype(F32), 0.0).astype(BF)
            q_feat[n] = jnp.zeros((2 * WIDTH, span), BF)
            g_feat[n] = jnp.zeros((2 * WIDTH, span), BF)
            q_feat[n, rows, :] = q_t[rows, here]
            g_feat[n, rows, :] = g_t[rows, here]
            for index, piece in enumerate(bias_pieces):
                q_feat[n, WIDTH + index * SWEEPS : WIDTH + (index + 1) * SWEEPS, :] = piece
    grad_q_t[...] = jnp.zeros_like(grad_q_t)
    bias_sum[...] = jnp.zeros_like(bias_sum)

    def merge(parts):
        best = functools.reduce(jnp.maximum, [part[0] for part in parts])
        weights = [jnp.exp2(part[0] - best) for part in parts]
        sums = [sum(w * part[kind] for w, part in zip(weights, parts)) for kind in (1, 2, 3)]
        return [best] + sums

    def keep(ref, merged):
        for kind, value in enumerate(merged):
            ref[kind] = value

    def to_sibling(s):
        return remote(
            stats.at[s], from_sibling.at[s], sent_s1.at[s], got_s1.at[s], {"pts": me + 1 - 2 * core}
        )

    def along_x(s, k):
        return remote(
            stats_1.at[s], stats_x.at[s, x], sent_sx.at[s, k], got_sx.at[s, k], x_peer(k)
        )

    def along_z(s, k):
        return remote(
            stats_2.at[s], stats_z.at[s, zl], sent_sz.at[s, k], got_sz.at[s, k], z_peer(k)
        )

    def exchange_x(s):
        to_sibling(s).wait_recv()
        merged = merge([stats[s], from_sibling[s]])
        keep(stats_1.at[s], merged)
        for k in range(1, nx):
            along_x(s, k).start()
        keep(stats_x.at[s, x], merged)

    def exchange_z(s):
        for k in range(1, nx):
            along_x(s, k).wait_recv()
        merged = merge([stats_x[s, i] for i in range(nx)])
        keep(stats_2.at[s], merged)
        for k in range(1, nz):
            along_z(s, k).start()
        keep(stats_z.at[s, zl], merged)

    def take_results(s):
        for k in range(1, nz):
            along_z(s, k).wait_recv()
        best, total, weighted, rounded_total = merge([stats_z[s, i] for i in range(nz)])
        offset = (best + jnp.log(total) * LOG2E) * (-1.0 / TO_LOG2)
        delta = -(weighted / rounded_total)
        row16 = lax.broadcasted_iota(jnp.int32, (16, 128), 0)
        per_tile = cols // 128
        for n in range(tiles // 2):
            it, h = n // HEADS, n % HEADS
            for part in range(per_tile):
                line = n * per_tile + part
                left = it * cols + part * 128
                for value, feat in ((offset, q_feat), (delta, g_feat)):
                    hi, mid, low = three_pieces(value[line : line + 1, :])
                    feat[
                        s * HEADS + h,
                        WIDTH + ONES_ROW : WIDTH + ONES_ROW + 16,
                        left : left + 128,
                    ] = jnp.where(
                        row16 == 0,
                        hi.astype(F32),
                        jnp.where(
                            row16 == 1, mid.astype(F32), jnp.where(row16 == 2, low.astype(F32), 0.0)
                        ),
                    ).astype(BF)

    lowest = jnp.full((32, cols), -jnp.inf, F32)

    def feature_of(n):
        it = n // HEADS
        return (
            (it // per_span) * HEADS + lax.rem(n, HEADS),
            pl.ds(pl.multiple_of(lax.rem(it, per_span) * cols, cols), cols),
        )

    def score_chunk(n, into, c, top):
        index, lanes = feature_of(n)
        rows = pl.ds(c * chunk, chunk)
        s = dot(k_aux[rows, :], q_feat[index, :, lanes]) * TO_LOG2
        into[rows, :] = s
        return jnp.maximum(top, jnp.max(s.reshape(chunk // 32, 32, cols), axis=0))

    def tile_sums(n, scores, top_rows, following, into):
        top = jnp.max(top_rows, axis=0, keepdims=True)
        head = lax.rem(n, HEADS)
        next_top = lowest
        total = jnp.zeros((32, cols), F32)
        out = jnp.zeros((48, cols), F32)
        for c in range(chunks):
            rows = pl.ds(c * chunk, chunk)
            e = jnp.exp2(scores[rows, :] - top)
            total = total + jnp.sum(e.reshape(chunk // 32, 32, cols), axis=0)
            out = out + dot(value_rows[head, :, rows], e.astype(BF))
            next_top = score_chunk(following, into, c, next_top)
        total = jnp.sum(total, axis=0, keepdims=True)
        g = g_t[
            pl.ds(pl.multiple_of(head * HEAD_DIM, HEAD_DIM), HEAD_DIM),
            pl.ds(pl.multiple_of((n // HEADS) * cols, cols), cols),
        ].astype(F32)
        weighted = jnp.sum(out[:HEAD_DIM] * g, axis=0, keepdims=True)
        rounded_total = out[HEAD_DIM : HEAD_DIM + 1]
        per_tile = cols // 128
        for kind, value in enumerate((top, total, weighted, rounded_total)):
            for part in range(per_tile):
                line = lax.rem(n, tiles // 2) * per_tile + part
                stats[n // (tiles // 2), kind, pl.ds(line, 1), :] = value[
                    :, part * 128 : (part + 1) * 128
                ]
        return next_top

    first_top = lowest
    for c in range(chunks):
        first_top = score_chunk(0, scores_0, c, first_top)

    def per_pair(pair, top_rows):
        n = pair * 2
        top_rows = tile_sums(n, scores_0, top_rows, n + 1, scores_1)
        top_rows = tile_sums(n + 1, scores_1, top_rows, lax.rem(n + 2, tiles), scores_0)

        @pl.when(pair == pairs // 2 - 1)
        def _():
            pl.semaphore_wait(barrier, len(greeted))
            to_sibling(0).start()

        @pl.when(pair == pairs // 2)
        def _():
            exchange_x(0)

        @pl.when(pair == pairs // 2 + 1)
        def _():
            exchange_z(0)

        return top_rows

    lax.fori_loop(0, pairs, per_pair, first_top)
    to_sibling(1).start()
    take_results(0)

    lane_row = lax.broadcasted_iota(jnp.int32, (block, 128), 1)

    def compute(step, s):
        turn = lax.rem(step, YS)
        owner_z = jnp.where(step < YS, 1 - z, z)
        at_up = (owner_z * YS + lax.rem(y + 2 * YS - 1 - turn, YS)) * block
        at_down = (owner_z * YS + lax.rem(y + 1 + turn, YS)) * block + half
        for row, at in ((0, at_up), (half, at_down)):
            source = pl.ds(pl.multiple_of(at, half), half)
            rows = pl.ds(row, half)
            k_stage[rows, :] = k_aux[source, :]
            v_stage[rows, :WIDTH] = values_ref[source, :]
            v_stage[rows, WIDTH:] = k_aux[source, WIDTH:]
            mark_stage[:, row : row + half] = onehot_t[:, source]
        k_t = k_stage[:, :WIDTH].T
        row_sums = jnp.zeros((block, 128), F32)
        grad_k = jnp.zeros((block, WIDTH), F32)
        grad_v = jnp.zeros((block, WIDTH), F32)
        lanes = pl.ds(pl.multiple_of(s * span, span), span)
        for h in range(HEADS):
            n = s * HEADS + h
            rows = slice(h * HEAD_DIM, (h + 1) * HEAD_DIM)
            p = jnp.exp2(dot(k_stage[...], q_feat[n]) * TO_LOG2)
            score_grad = p * dot(v_stage[...], g_feat[n])
            probs[h] = p.astype(BF)
            scaled[h] = (score_grad * SCALE).astype(BF)
            folded = score_grad[:, :128]
            for part in range(1, span // 128):
                folded = folded + score_grad[:, part * 128 : (part + 1) * 128]
            row_sums = row_sums + jnp.where(
                lane_row == h, jnp.sum(folded, axis=1, keepdims=True), 0.0
            )
            grad_v = grad_v + dot(probs[h], g_stack[n])
            grad_k = grad_k + dot(scaled[h], q_stack[n])
            grad_q_t[rows, lanes] += dot(k_t[rows, :], scaled[h])

        @pl.when(s == 0)
        def _():
            part_sum[step, :, :WIDTH] = grad_k
            part_sum[step, :, WIDTH:] = grad_v

        @pl.when(s == 1)
        def _():
            part_sum[step, :, :WIDTH] += grad_k
            part_sum[step, :, WIDTH:] += grad_v

        for piece in three_pieces(row_sums):
            bias_sum[:SWEEPS, :] += dot(mark_stage[...], piece)

    def rows_of(part, way):
        return pl.ds(way * half + part * quarter, quarter)

    def ring(step, part, way):
        rows = rows_of(part, way)
        return remote(
            part_sum.at[step, rows],
            from_ring.at[step, rows],
            sent_ring.at[step, part, way],
            got_ring.at[step, part, way],
            {"lat": down if way else up},
        )

    def near(part, way):
        return remote(
            part_sum.at[YS - 1, rows_of(part, way)],
            relay.at[part, way],
            sent_near.at[part, way],
            got_near.at[part, way],
            at_height(-1 if way else 1),
        )

    def far(part, way):
        return remote(
            relay.at[part, way],
            from_z.at[rows_of(part, way)],
            sent_far.at[part, way],
            got_far.at[part, way],
            at_height(1 - nz if way else nz - 1),
        )

    def finish(step, part):
        turn = lax.rem(step, YS)

        @pl.when(turn > 0)
        def _():
            for way in range(2):
                ring(step - 1, part, way).wait_recv()
                rows = rows_of(part, way)
                part_sum[step, rows, :] += from_ring[step - 1, rows, :]

        @pl.when(turn < YS - 1)
        def _():
            for way in range(2):
                ring(step, part, way).start()

        @pl.when(step == YS - 1)
        def _():
            for way in range(2):
                near(part, way).start()

    def per_item(t, unused):
        step = t // 2
        for when, value in ((1, 1), (2, 2), (3, 0), (4, 1), (5, 3), (6, 2)):
            step = jnp.where(t == when, value, step)
        s = jnp.where((t < 3) | (t == 5), 0, jnp.where(t < 8, 1, lax.rem(t, 2)))

        @pl.when(t == 3)
        def _():
            take_results(1)

        compute(step, s)

        @pl.when(t == 0)
        def _():
            exchange_x(1)

        @pl.when(t == 1)
        def _():
            exchange_z(1)

        @pl.when(t >= 3)
        def _():
            finish(jnp.where(t < 11, (t - 3) // 2, (t - 1) // 2), lax.rem(t + 1, 2))

        @pl.when((t == 9) | (t == 10))
        def _():
            finish(YS, t - 9)

        for part in range(2):

            @pl.when(t == 11 + part)
            def _():
                for way in range(2):
                    near(part, way).wait_recv()
                    far(part, way).start()

        return unused

    lax.fori_loop(0, 4 * YS, per_item, 0)

    swap = remote(q_parts.at[1 - core], from_core, sent_core, got_core, {"pts": me + 1 - 2 * core})

    def bias_y(k):
        return remote(
            bias_sum.at[pl.ds(0, SWEEPS)],
            bias_1.at[y * 2 + core],
            sent_b1.at[k],
            got_b1.at[k],
            y_peer(k),
        )

    def q_along_x(k):
        return remote(
            q_x.at[lax.rem(x + k, nx)], got_q_x.at[x], sent_qx.at[k], got_qx.at[k], x_peer(k)
        )

    def q_along_z(k):
        return remote(
            q_z.at[lax.rem(zl + k, nz)], got_q_z.at[zl], sent_qz.at[k], got_qz.at[k], z_peer(k)
        )

    def bias_along_z(k):
        return remote(bias_2, bias_z.at[height], sent_b2.at[k], got_b2.at[k], at_height(k))

    bias_copies = [bias_y(k) for k in range(1, 2 * YS)]
    x_copies = [q_along_x(k) for k in range(1, nx)]
    z_copies = [q_along_z(k) for k in range(1, nz)]
    bias_z_copies = [bias_along_z(k) for k in range(1, heights)]

    for copy in bias_copies:
        copy.start()
    grad_q = grad_q_t[...].T
    for p in range(count):
        q_parts[p % 2, p // 2] = grad_q[p * rows_out : (p + 1) * rows_out]
    swap.start()
    bias_1[y * 2 + core] = bias_sum[:SWEEPS, :]
    for copy in bias_copies:
        copy.wait_recv()
    bias = jnp.sum(bias_1[...], axis=0)
    swap.wait_recv()
    for i in range(nx):
        for j in range(nz):
            q_x[i, j * rows_out : (j + 1) * rows_out, :] = (
                q_parts[core, i * nz + j] + from_core[i * nz + j]
            )
        q_x[i, nz * rows_out :, :] = bias
    for copy in x_copies:
        copy.start()
    got_q_x[x] = q_x[x]
    finish(2 * YS - 1, 1)
    for copy in x_copies:
        copy.wait_recv()
    summed = jnp.sum(got_q_x[...], axis=0)
    bias_2[...] = summed[nz * rows_out :]
    for j in range(nz):
        q_z[j] = summed[j * rows_out : (j + 1) * rows_out]
    for copy in bias_z_copies + z_copies:
        copy.start()
    got_q_z[zl] = q_z[zl]
    bias_z[height] = bias_2[...]
    for part in range(2):
        for way in range(2):
            far(part, way).wait_recv()
    done = part_sum[2 * YS - 1] + from_z[...]
    grad_k_ref[...] = done[:, :WIDTH]
    grad_v_ref[...] = done[:, WIDTH:]
    for copy in bias_z_copies + z_copies:
        copy.wait_recv()
    small_ref[:rows_out, :] = jnp.sum(got_q_z[...], axis=0)
    small_ref[rows_out:, :] = jnp.sum(bias_z[...], axis=0)

    for s in range(2):
        to_sibling(s).wait_send()
        for k in range(1, nx):
            along_x(s, k).wait_send()
        for k in range(1, nz):
            along_z(s, k).wait_send()
    for part in range(2):
        for way in range(2):
            for step in range(2 * YS):
                if step % YS < YS - 1:
                    ring(step, part, way).wait_send()
            near(part, way).wait_send()
            far(part, way).wait_send()
    swap.wait_send()
    for copy in bias_copies + x_copies + z_copies + bias_z_copies:
        copy.wait_send()


def whole(latents, keys, values, sweep, sweep_bias, grad_out, count, lats):
    rows, points = latents.shape[0], keys.shape[0]
    block, span, chips = points // (2 * YS), rows // 2, count // 2
    cols = min(256, span)
    lines = HEADS * rows // 256
    nz = 4 if chips % 4 == 0 else chips
    nx = chips // nz
    heights = 2 * nz
    rows_out = rows // count
    dma = pltpu.SemaphoreType.DMA
    return pl.pallas_call(
        functools.partial(whole_kernel, count, lats),
        out_shape=[
            jax.ShapeDtypeStruct((block, WIDTH), F32),
            jax.ShapeDtypeStruct((block, WIDTH), F32),
            jax.ShapeDtypeStruct((rows_out + SWEEPS, WIDTH), F32),
        ],
        in_specs=vmem_specs(6),
        out_specs=vmem_specs(3),
        scratch_shapes=[
            pltpu.VMEM((points, 2 * WIDTH), BF),
            pltpu.VMEM((HEADS, 48, points), BF),
            pltpu.VMEM((SWEEPS, points), BF),
            pltpu.VMEM((WIDTH, rows), BF),
            pltpu.VMEM((2 * HEADS, 2 * WIDTH, span), BF),
            pltpu.VMEM((2 * HEADS, 2 * WIDTH, span), BF),
            pltpu.VMEM((2 * HEADS, span, WIDTH), BF),
            pltpu.VMEM((2 * HEADS, span, WIDTH), BF),
            pltpu.VMEM((points, cols), F32),
            pltpu.VMEM((points, cols), F32),
            pltpu.VMEM((2, 4, lines, 128), F32),
            pltpu.VMEM((2, 4, lines, 128), F32),
            pltpu.VMEM((2, 4, lines, 128), F32),
            pltpu.VMEM((2, nx, 4, lines, 128), F32),
            pltpu.VMEM((2, 4, lines, 128), F32),
            pltpu.VMEM((2, nz, 4, lines, 128), F32),
            pltpu.VMEM((block, 2 * WIDTH), BF),
            pltpu.VMEM((block, 2 * WIDTH), BF),
            pltpu.VMEM((SWEEPS, block), BF),
            pltpu.VMEM((HEADS, block, span), BF),
            pltpu.VMEM((HEADS, block, span), BF),
            pltpu.VMEM((2 * YS, block, 2 * WIDTH), F32),
            pltpu.VMEM((2 * YS, block, 2 * WIDTH), F32),
            pltpu.VMEM((2, 2, block // 4, 2 * WIDTH), F32),
            pltpu.VMEM((block, 2 * WIDTH), F32),
            pltpu.VMEM((WIDTH, rows), F32),
            pltpu.VMEM((128, 128), F32),
            pltpu.VMEM((2, chips, rows_out, WIDTH), F32),
            pltpu.VMEM((chips, rows_out, WIDTH), F32),
            pltpu.VMEM((2 * YS, SWEEPS, 128), F32),
            pltpu.VMEM((nx, nz * rows_out + SWEEPS, WIDTH), F32),
            pltpu.VMEM((nx, nz * rows_out + SWEEPS, WIDTH), F32),
            pltpu.VMEM((nz, rows_out, WIDTH), F32),
            pltpu.VMEM((nz, rows_out, WIDTH), F32),
            pltpu.VMEM((SWEEPS, 128), F32),
            pltpu.VMEM((heights, SWEEPS, 128), F32),
            dma((2,)),
            dma((2,)),
            dma((2, nx)),
            dma((2, nx)),
            dma((2, nz)),
            dma((2, nz)),
            dma((2 * YS, 2, 2)),
            dma((2 * YS, 2, 2)),
            dma((2, 2)),
            dma((2, 2)),
            dma((2, 2)),
            dma((2, 2)),
            dma,
            dma,
            dma((2 * YS,)),
            dma((2 * YS,)),
            dma((nx,)),
            dma((nx,)),
            dma((nz,)),
            dma((nz,)),
            dma((heights,)),
            dma((heights,)),
        ],
        compiler_params=pltpu.CompilerParams(
            collective_id=0, has_side_effects=True, vmem_limit_bytes=VMEM_BYTES
        ),
    )(latents, keys, values, sweep, sweep_bias, grad_out)


def deliver_kernel(small_ref, grad_k_ref, grad_v_ref, q_out, k_out, v_out, bias_out, square):
    rows_out = q_out.shape[0]
    q_out[...] = small_ref[:rows_out, :]
    k_out[...] = grad_k_ref[...]
    v_out[...] = grad_v_ref[...]
    square[...] = jnp.zeros_like(square)
    square[:SWEEPS, :] = small_ref[rows_out:, :]
    bias_out[...] = square[...].T[:HEADS, :SWEEPS]


def deliver(small, grad_k, grad_v):
    return pl.pallas_call(
        deliver_kernel,
        out_shape=[
            jax.ShapeDtypeStruct((small.shape[0] - SWEEPS, WIDTH), F32),
            jax.ShapeDtypeStruct(grad_k.shape, F32),
            jax.ShapeDtypeStruct(grad_v.shape, F32),
            jax.ShapeDtypeStruct((HEADS, SWEEPS), F32),
        ],
        in_specs=vmem_specs(3),
        out_specs=vmem_specs(4),
        scratch_shapes=[pltpu.VMEM((128, 128), F32)],
    )(small, grad_k, grad_v)


def per_device(count, lats, latents, keys, values, sweep, sweep_bias, grad_out):
    grad_k, grad_v, small = whole(
        latents, keys, values, sweep.reshape(1, -1), sweep_bias, grad_out, count, lats
    )
    return tuple(deliver(small, grad_k, grad_v))


def solution(mesh):
    return jax.shard_map(
        functools.partial(per_device, mesh.shape["pts"], mesh.shape["lat"]),
        mesh=mesh,
        in_specs=(P("lat", None), P("pts", None), P("pts", None), P("pts"), P(), P("lat", None)),
        out_specs=(P(("lat", "pts"), None), P(("pts", "lat"), None), P(("pts", "lat"), None), P()),
        check_vma=False,
    )
```

```python
import functools
import math

import jax
import jax.numpy as jnp
from jax import lax
from jax.experimental import pallas as pl
from jax.experimental.pallas import tpu as pltpu
from jax.sharding import PartitionSpec as P

HEADS = 4
HEAD_DIM = 32
WIDTH = HEADS * HEAD_DIM
SWEEPS = 16
SCALE = HEAD_DIM**-0.5
LOG2E = math.log2(math.e)
TO_LOG2 = SCALE * LOG2E
YS = 4
ONES_ROW = 3 * SWEEPS
BF = jnp.bfloat16
F32 = jnp.float32
MESH = pl.DeviceIdType.MESH
VMEM_BYTES = 56 * 1024 * 1024


def dot(a, b):
    return jnp.dot(a, b, preferred_element_type=F32)


def dot_transposed(a, b):
    return lax.dot_general(a, b, (((1,), (1,)), ((), ())), preferred_element_type=F32)


def three_pieces(x):
    hi = x.astype(BF)
    rest = x - hi.astype(F32)
    mid = rest.astype(BF)
    low = (rest - mid.astype(F32)).astype(BF)
    return hi, mid, low


def vmem_specs(count):
    return [pl.BlockSpec(memory_space=pltpu.VMEM)] * count


def whole_kernel(
    count,
    lats,
    latents_ref,
    keys_ref,
    values_ref,
    sweep_ref,
    sweep_bias_ref,
    grad_out_ref,
    grads_ref,
    small_ref,
    k_aux,
    value_rows,
    onehot_t,
    g_t,
    q_feat,
    g_feat,
    scores_0,
    scores_1,
    stats,
    from_sibling,
    stats_1,
    stats_x,
    stats_2,
    stats_z,
    k_stage,
    v_stage,
    mark_stage,
    probs,
    scaled,
    part_sum,
    from_ring,
    relay,
    from_z,
    grad_q_t,
    bias_sum,
    q_parts,
    from_core,
    bias_1,
    q_x,
    got_q_x,
    q_z,
    got_q_z,
    bias_2,
    bias_z,
    sent_s1,
    got_s1,
    sent_sx,
    got_sx,
    sent_sz,
    got_sz,
    sent_ring,
    got_ring,
    sent_near,
    got_near,
    sent_far,
    got_far,
    sent_core,
    got_core,
    sent_b1,
    got_b1,
    sent_qx,
    got_qx,
    sent_qz,
    got_qz,
    sent_b2,
    got_b2,
):
    points, latents = keys_ref.shape[0], latents_ref.shape[0]
    span = latents // 2
    cols = min(256, span)
    per_span = span // cols
    tiles = HEADS * 2 * per_span
    pairs = tiles // 2
    chunk = min(512, points)
    chunks = points // chunk
    block = points // (2 * YS)
    half = block // 2
    quarter = block // 4
    chips = count // 2
    nz = 4 if chips % 4 == 0 else chips
    nx = chips // nz
    heights = 2 * nz
    rows_out = latents // count

    me = lax.axis_index("pts")
    lat = lax.axis_index("lat")
    core = lax.rem(me, 2)
    chip = me // 2
    z, y = lat // YS, lax.rem(lat, YS)
    up = z * YS + lax.rem(y + 1, YS)
    down = z * YS + lax.rem(y + YS - 1, YS)
    x, zl = chip // nz, lax.rem(chip, nz)
    height = z * nz + zl

    def x_peer(k):
        return {"pts": (lax.rem(x + k, nx) * nz + zl) * 2 + core}

    def z_peer(k):
        return {"pts": (x * nz + lax.rem(zl + k, nz)) * 2 + core}

    def y_peer(k):
        there = lax.rem(y * 2 + core + k, 2 * YS)
        return {"pts": chip * 2 + lax.rem(there, 2), "lat": z * YS + there // 2}

    def at_height(shift):
        there = lax.rem(height + shift + heights, heights)
        return {"pts": (x * nz + lax.rem(there, nz)) * 2 + core, "lat": (there // nz) * YS + y}

    def remote(src, dst, sent, got, device):
        return pltpu.make_async_remote_copy(
            src_ref=src,
            dst_ref=dst,
            send_sem=sent,
            recv_sem=got,
            device_id=device,
            device_id_type=MESH,
        )

    def every(start, stop, action):
        def step(k, unused):
            action(k)
            return unused

        lax.fori_loop(start, stop, step, 0)

    barrier = pltpu.get_barrier_semaphore()
    greeted = (
        [x_peer(k) for k in range(1, nx)]
        + [at_height(k) for k in range(1, heights)]
        + [y_peer(k) for k in range(1, 2 * YS)]
    )
    for device in greeted:
        pl.semaphore_signal(barrier, inc=1, device_id=device, device_id_type=MESH)

    k_aux[:, :WIDTH] = keys_ref[...]

    def build(c):
        rows = pl.ds(pl.multiple_of(c * chunk, chunk), chunk)
        swept = sweep_ref[:, rows]
        row = lax.broadcasted_iota(jnp.int32, (WIDTH, chunk), 0)
        marked = (row < ONES_ROW) & (lax.rem(row, SWEEPS) == swept)
        ones = (row >= ONES_ROW) & (row < ONES_ROW + 3)
        aux_t = jnp.where(marked | ones, 1.0, 0.0)
        onehot_t[:, rows] = aux_t[:SWEEPS].astype(BF)
        k_aux[rows, WIDTH:] = aux_t.T.astype(BF)
        value_t = values_ref[rows, :].T
        for h in range(HEADS):
            value_rows[h, :HEAD_DIM, rows] = value_t[h * HEAD_DIM : (h + 1) * HEAD_DIM, :]
            value_rows[h, HEAD_DIM:, rows] = jnp.where(row[:16] == 0, 1.0, 0.0).astype(BF)

    every(0, chunks, build)
    q_t = latents_ref[...].T
    g_t[...] = grad_out_ref[...].T
    eye = lax.broadcasted_iota(jnp.int32, (SWEEPS, SWEEPS), 0) == lax.broadcasted_iota(
        jnp.int32, (SWEEPS, SWEEPS), 1
    )
    for h in range(HEADS):
        rows = slice(h * HEAD_DIM, (h + 1) * HEAD_DIM)
        column = jnp.sum(
            jnp.where(eye, sweep_bias_ref[h : h + 1, :], 0.0), axis=1, keepdims=True
        ) * (1.0 / SCALE)
        bias_pieces = three_pieces(jnp.broadcast_to(column, (SWEEPS, span)))
        for s in range(2):
            n = s * HEADS + h
            here = slice(s * span, (s + 1) * span)
            q_feat[n] = jnp.zeros((2 * WIDTH, span), BF)
            g_feat[n] = jnp.zeros((2 * WIDTH, span), BF)
            q_feat[n, rows, :] = q_t[rows, here]
            g_feat[n, rows, :] = g_t[rows, here]
            for index, piece in enumerate(bias_pieces):
                q_feat[n, WIDTH + index * SWEEPS : WIDTH + (index + 1) * SWEEPS, :] = piece
    grad_q_t[...] = jnp.zeros_like(grad_q_t)
    bias_sum[...] = jnp.zeros_like(bias_sum)
    part_sum[...] = jnp.zeros_like(part_sum)

    def merge(parts):
        best = functools.reduce(jnp.maximum, [part[0] for part in parts])
        weights = [jnp.exp2(part[0] - best) for part in parts]
        sums = [sum(w * part[kind] for w, part in zip(weights, parts)) for kind in (1, 2)]
        return [best] + sums

    def keep(ref, merged):
        for kind, value in enumerate(merged):
            ref[kind] = value

    def to_sibling(s):
        return remote(
            stats.at[s], from_sibling.at[s], sent_s1.at[s], got_s1.at[s], {"pts": me + 1 - 2 * core}
        )

    def along_x(s, k):
        return remote(
            stats_1.at[s], stats_x.at[s, x], sent_sx.at[s, k], got_sx.at[s, k], x_peer(k)
        )

    def along_z(s, k):
        return remote(
            stats_2.at[s], stats_z.at[s, zl], sent_sz.at[s, k], got_sz.at[s, k], z_peer(k)
        )

    def exchange_x(s):
        to_sibling(s).wait_recv()
        merged = merge([stats[s], from_sibling[s]])
        keep(stats_1.at[s], merged)
        for k in range(1, nx):
            along_x(s, k).start()
        keep(stats_x.at[s, x], merged)

    def exchange_z(s):
        for k in range(1, nx):
            along_x(s, k).wait_recv()
        merged = merge([stats_x[s, i] for i in range(nx)])
        keep(stats_2.at[s], merged)
        for k in range(1, nz):
            along_z(s, k).start()
        keep(stats_z.at[s, zl], merged)

    def take_results(s):
        for k in range(1, nz):
            along_z(s, k).wait_recv()
        best, total, weighted = merge([stats_z[s, i] for i in range(nz)])
        offset = (best + jnp.log(total) * LOG2E) * (-1.0 / TO_LOG2)
        delta = -(weighted / total)
        row16 = lax.broadcasted_iota(jnp.int32, (16, 128), 0)
        per_tile = cols // 128
        for n in range(tiles // 2):
            it, h = n // HEADS, n % HEADS
            for part in range(per_tile):
                line = n * per_tile + part
                left = it * cols + part * 128
                for value, feat in ((offset, q_feat), (delta, g_feat)):
                    hi, mid, low = three_pieces(value[line : line + 1, :])
                    feat[
                        s * HEADS + h,
                        WIDTH + ONES_ROW : WIDTH + ONES_ROW + 16,
                        left : left + 128,
                    ] = jnp.where(
                        row16 == 0,
                        hi.astype(F32),
                        jnp.where(
                            row16 == 1, mid.astype(F32), jnp.where(row16 == 2, low.astype(F32), 0.0)
                        ),
                    ).astype(BF)

    lowest = jnp.full((32, cols), -jnp.inf, F32)

    def feature_of(n):
        it = n // HEADS
        return (
            (it // per_span) * HEADS + lax.rem(n, HEADS),
            pl.ds(pl.multiple_of(lax.rem(it, per_span) * cols, cols), cols),
        )

    def score_chunk(n, into, c, top):
        index, lanes = feature_of(n)
        rows = pl.ds(c * chunk, chunk)
        s = dot(k_aux[rows, :], q_feat[index, :, lanes]) * TO_LOG2
        into[rows, :] = s
        return jnp.maximum(top, jnp.max(s.reshape(chunk // 32, 32, cols), axis=0))

    def tile_sums(n, scores, top_rows, following, into):
        top = jnp.max(top_rows, axis=0, keepdims=True)
        head = lax.rem(n, HEADS)
        next_top = lowest
        out = jnp.zeros((48, cols), F32)
        for c in range(chunks):
            rows = pl.ds(c * chunk, chunk)
            e = jnp.exp2(scores[rows, :] - top)
            out = out + dot(value_rows[head, :, rows], e.astype(BF))
            next_top = score_chunk(following, into, c, next_top)
        g = g_t[
            pl.ds(pl.multiple_of(head * HEAD_DIM, HEAD_DIM), HEAD_DIM),
            pl.ds(pl.multiple_of((n // HEADS) * cols, cols), cols),
        ].astype(F32)
        weighted = jnp.sum(out[:HEAD_DIM] * g, axis=0, keepdims=True)
        total = out[HEAD_DIM : HEAD_DIM + 1]
        per_tile = cols // 128
        for kind, value in enumerate((top, total, weighted)):
            for part in range(per_tile):
                line = lax.rem(n, tiles // 2) * per_tile + part
                stats[n // (tiles // 2), kind, pl.ds(line, 1), :] = value[
                    :, part * 128 : (part + 1) * 128
                ]
        return next_top

    first_top = lowest
    for c in range(chunks):
        first_top = score_chunk(0, scores_0, c, first_top)

    def per_pair(pair, top_rows):
        n = pair * 2
        top_rows = tile_sums(n, scores_0, top_rows, n + 1, scores_1)
        top_rows = tile_sums(n + 1, scores_1, top_rows, lax.rem(n + 2, tiles), scores_0)

        @pl.when(pair == pairs // 2 - 1)
        def _():
            pl.semaphore_wait(barrier, len(greeted))
            to_sibling(0).start()

        @pl.when(pair == pairs // 2)
        def _():
            exchange_x(0)

        @pl.when(pair == pairs // 2 + 1)
        def _():
            exchange_z(0)

        return top_rows

    lax.fori_loop(0, pairs, per_pair, first_top)
    to_sibling(1).start()
    take_results(0)

    lane_row = lax.broadcasted_iota(jnp.int32, (block, 128), 1)

    def compute(step, s):
        turn = lax.rem(step, YS)
        owner_z = jnp.where(step < YS, 1 - z, z)
        at_up = (owner_z * YS + lax.rem(y + 2 * YS - 1 - turn, YS)) * block
        at_down = (owner_z * YS + lax.rem(y + 1 + turn, YS)) * block + half
        for row, at in ((0, at_up), (half, at_down)):
            source = pl.ds(pl.multiple_of(at, half), half)
            rows = pl.ds(row, half)
            k_stage[rows, :] = k_aux[source, :]
            v_stage[rows, :WIDTH] = values_ref[source, :]
            v_stage[rows, WIDTH:] = k_aux[source, WIDTH:]
            mark_stage[:, row : row + half] = onehot_t[:, source]
        k_t = k_stage[:, :WIDTH].T
        row_sums = jnp.zeros((block, 128), F32)
        lanes = pl.ds(pl.multiple_of(s * span, span), span)
        for h in range(HEADS):
            n = s * HEADS + h
            rows = slice(h * HEAD_DIM, (h + 1) * HEAD_DIM)
            p = jnp.exp2(dot(k_stage[...], q_feat[n]) * TO_LOG2)
            score_grad = p * dot(v_stage[...], g_feat[n])
            probs[h] = p.astype(BF)
            scaled[h] = (score_grad * SCALE).astype(BF)
            folded = score_grad[:, :128]
            for part in range(1, span // 128):
                folded = folded + score_grad[:, part * 128 : (part + 1) * 128]
            row_sums = row_sums + jnp.where(
                lane_row == h, jnp.sum(folded, axis=1, keepdims=True), 0.0
            )
            part_sum[step, rows, :] += dot_transposed(q_feat[n, rows, :], scaled[h])
            part_sum[step, WIDTH + h * HEAD_DIM : WIDTH + (h + 1) * HEAD_DIM, :] += dot_transposed(
                g_feat[n, rows, :], probs[h]
            )
            grad_q_t[rows, lanes] += dot(k_t[rows, :], scaled[h])

        for piece in three_pieces(row_sums):
            bias_sum[:SWEEPS, :] += dot(mark_stage[...], piece)

    def lanes_of(part, way):
        return pl.ds(pl.multiple_of(way * half + part * quarter, quarter), quarter)

    def ring(step, part, way):
        here = lanes_of(part, way)
        return remote(
            part_sum.at[step, :, here],
            from_ring.at[step, :, here],
            sent_ring.at[step, part, way],
            got_ring.at[step, part, way],
            {"lat": down if way else up},
        )

    def near(part, way):
        return remote(
            part_sum.at[YS - 1, :, lanes_of(part, way)],
            relay.at[part, way],
            sent_near.at[part, way],
            got_near.at[part, way],
            at_height(-1 if way else 1),
        )

    def far(part, way):
        return remote(
            relay.at[part, way],
            from_z.at[:, lanes_of(part, way)],
            sent_far.at[part, way],
            got_far.at[part, way],
            at_height(1 - nz if way else nz - 1),
        )

    def finish(step, part):
        turn = lax.rem(step, YS)

        @pl.when(turn > 0)
        def _():
            for way in range(2):
                ring(step - 1, part, way).wait_recv()
                here = lanes_of(part, way)
                part_sum[step, :, here] += from_ring[step - 1, :, here]

        @pl.when(turn < YS - 1)
        def _():
            for way in range(2):
                ring(step, part, way).start()

        @pl.when(step == YS - 1)
        def _():
            for way in range(2):
                near(part, way).start()

    def per_item(t, unused):
        step = t // 2
        for when, value in ((1, 1), (2, 2), (3, 0), (4, 1), (5, 3), (6, 2)):
            step = jnp.where(t == when, value, step)
        s = jnp.where((t < 3) | (t == 5), 0, jnp.where(t < 8, 1, lax.rem(t, 2)))

        @pl.when(t == 3)
        def _():
            take_results(1)

        compute(step, s)

        @pl.when(t == 0)
        def _():
            exchange_x(1)

        @pl.when(t == 1)
        def _():
            exchange_z(1)

        @pl.when(t >= 3)
        def _():
            finish(jnp.where(t < 11, (t - 3) // 2, (t - 1) // 2), lax.rem(t + 1, 2))

        @pl.when((t == 9) | (t == 10))
        def _():
            finish(YS, t - 9)

        for part in range(2):

            @pl.when(t == 11 + part)
            def _():
                for way in range(2):
                    near(part, way).wait_recv()
                    far(part, way).start()

        return unused

    lax.fori_loop(0, 4 * YS, per_item, 0)

    swap = remote(q_parts.at[1 - core], from_core, sent_core, got_core, {"pts": me + 1 - 2 * core})

    def bias_y(k):
        return remote(
            bias_sum.at[pl.ds(0, SWEEPS)],
            bias_1.at[y * 2 + core],
            sent_b1.at[k],
            got_b1.at[k],
            y_peer(k),
        )

    def q_along_x(k):
        return remote(
            q_x.at[lax.rem(x + k, nx)], got_q_x.at[x], sent_qx.at[k], got_qx.at[k], x_peer(k)
        )

    def q_along_z(k):
        return remote(
            q_z.at[lax.rem(zl + k, nz)], got_q_z.at[zl], sent_qz.at[k], got_qz.at[k], z_peer(k)
        )

    def bias_along_z(k):
        return remote(bias_2, bias_z.at[height], sent_b2.at[k], got_b2.at[k], at_height(k))

    bias_copies = [bias_y(k) for k in range(1, 2 * YS)]
    x_copies = [q_along_x(k) for k in range(1, nx)]
    z_copies = [q_along_z(k) for k in range(1, nz)]
    bias_z_copies = [bias_along_z(k) for k in range(1, heights)]

    for copy in bias_copies:
        copy.start()
    grad_q = grad_q_t[...].T
    for p in range(count):
        q_parts[p % 2, p // 2] = grad_q[p * rows_out : (p + 1) * rows_out]
    swap.start()
    bias_1[y * 2 + core] = bias_sum[:SWEEPS, :]
    for copy in bias_copies:
        copy.wait_recv()
    bias = jnp.sum(bias_1[...], axis=0)
    swap.wait_recv()
    for i in range(nx):
        for j in range(nz):
            q_x[i, j * rows_out : (j + 1) * rows_out, :] = (
                q_parts[core, i * nz + j] + from_core[i * nz + j]
            )
        q_x[i, nz * rows_out :, :] = bias
    for copy in x_copies:
        copy.start()
    got_q_x[x] = q_x[x]
    finish(2 * YS - 1, 1)
    for copy in x_copies:
        copy.wait_recv()
    summed = jnp.sum(got_q_x[...], axis=0)
    bias_2[...] = summed[nz * rows_out :]
    for j in range(nz):
        q_z[j] = summed[j * rows_out : (j + 1) * rows_out]
    for copy in bias_z_copies + z_copies:
        copy.start()
    got_q_z[zl] = q_z[zl]
    bias_z[height] = bias_2[...]
    for part in range(2):
        for way in range(2):
            far(part, way).wait_recv()
    grads_ref[...] = part_sum[2 * YS - 1] + from_z[...]
    for copy in bias_z_copies + z_copies:
        copy.wait_recv()
    small_ref[:rows_out, :] = jnp.sum(got_q_z[...], axis=0)
    small_ref[rows_out:, :] = jnp.sum(bias_z[...], axis=0)

    for s in range(2):
        to_sibling(s).wait_send()
        for k in range(1, nx):
            along_x(s, k).wait_send()
        for k in range(1, nz):
            along_z(s, k).wait_send()
    for part in range(2):
        for way in range(2):
            for step in range(2 * YS):
                if step % YS < YS - 1:
                    ring(step, part, way).wait_send()
            near(part, way).wait_send()
            far(part, way).wait_send()
    swap.wait_send()
    for copy in bias_copies + x_copies + z_copies + bias_z_copies:
        copy.wait_send()


def whole(latents, keys, values, sweep, sweep_bias, grad_out, count, lats):
    rows, points = latents.shape[0], keys.shape[0]
    block, span, chips = points // (2 * YS), rows // 2, count // 2
    cols = min(256, span)
    lines = HEADS * rows // 256
    nz = 4 if chips % 4 == 0 else chips
    nx = chips // nz
    heights = 2 * nz
    rows_out = rows // count
    dma = pltpu.SemaphoreType.DMA
    return pl.pallas_call(
        functools.partial(whole_kernel, count, lats),
        out_shape=[
            jax.ShapeDtypeStruct((2 * WIDTH, block), F32),
            jax.ShapeDtypeStruct((rows_out + SWEEPS, WIDTH), F32),
        ],
        in_specs=vmem_specs(6),
        out_specs=vmem_specs(2),
        scratch_shapes=[
            pltpu.VMEM((points, 2 * WIDTH), BF),
            pltpu.VMEM((HEADS, 48, points), BF),
            pltpu.VMEM((SWEEPS, points), BF),
            pltpu.VMEM((WIDTH, rows), BF),
            pltpu.VMEM((2 * HEADS, 2 * WIDTH, span), BF),
            pltpu.VMEM((2 * HEADS, 2 * WIDTH, span), BF),
            pltpu.VMEM((points, cols), F32),
            pltpu.VMEM((points, cols), F32),
            pltpu.VMEM((2, 3, lines, 128), F32),
            pltpu.VMEM((2, 3, lines, 128), F32),
            pltpu.VMEM((2, 3, lines, 128), F32),
            pltpu.VMEM((2, nx, 3, lines, 128), F32),
            pltpu.VMEM((2, 3, lines, 128), F32),
            pltpu.VMEM((2, nz, 3, lines, 128), F32),
            pltpu.VMEM((block, 2 * WIDTH), BF),
            pltpu.VMEM((block, 2 * WIDTH), BF),
            pltpu.VMEM((SWEEPS, block), BF),
            pltpu.VMEM((HEADS, block, span), BF),
            pltpu.VMEM((HEADS, block, span), BF),
            pltpu.VMEM((2 * YS, 2 * WIDTH, block), F32),
            pltpu.VMEM((2 * YS, 2 * WIDTH, block), F32),
            pltpu.VMEM((2, 2, 2 * WIDTH, block // 4), F32),
            pltpu.VMEM((2 * WIDTH, block), F32),
            pltpu.VMEM((WIDTH, rows), F32),
            pltpu.VMEM((128, 128), F32),
            pltpu.VMEM((2, chips, rows_out, WIDTH), F32),
            pltpu.VMEM((chips, rows_out, WIDTH), F32),
            pltpu.VMEM((2 * YS, SWEEPS, 128), F32),
            pltpu.VMEM((nx, nz * rows_out + SWEEPS, WIDTH), F32),
            pltpu.VMEM((nx, nz * rows_out + SWEEPS, WIDTH), F32),
            pltpu.VMEM((nz, rows_out, WIDTH), F32),
            pltpu.VMEM((nz, rows_out, WIDTH), F32),
            pltpu.VMEM((SWEEPS, 128), F32),
            pltpu.VMEM((heights, SWEEPS, 128), F32),
            dma((2,)),
            dma((2,)),
            dma((2, nx)),
            dma((2, nx)),
            dma((2, nz)),
            dma((2, nz)),
            dma((2 * YS, 2, 2)),
            dma((2 * YS, 2, 2)),
            dma((2, 2)),
            dma((2, 2)),
            dma((2, 2)),
            dma((2, 2)),
            dma,
            dma,
            dma((2 * YS,)),
            dma((2 * YS,)),
            dma((nx,)),
            dma((nx,)),
            dma((nz,)),
            dma((nz,)),
            dma((heights,)),
            dma((heights,)),
        ],
        compiler_params=pltpu.CompilerParams(
            collective_id=0, has_side_effects=True, vmem_limit_bytes=VMEM_BYTES
        ),
    )(latents, keys, values, sweep, sweep_bias, grad_out)


def deliver_kernel(small_ref, grads_ref, q_out, k_out, v_out, bias_out, square):
    rows_out = q_out.shape[0]
    q_out[...] = small_ref[:rows_out, :]
    k_out[...] = grads_ref[:WIDTH, :].T
    v_out[...] = grads_ref[WIDTH:, :].T
    square[...] = jnp.zeros_like(square)
    square[:SWEEPS, :] = small_ref[rows_out:, :]
    bias_out[...] = square[...].T[:HEADS, :SWEEPS]


def deliver(small, grads):
    block = grads.shape[1]
    return pl.pallas_call(
        deliver_kernel,
        out_shape=[
            jax.ShapeDtypeStruct((small.shape[0] - SWEEPS, WIDTH), F32),
            jax.ShapeDtypeStruct((block, WIDTH), F32),
            jax.ShapeDtypeStruct((block, WIDTH), F32),
            jax.ShapeDtypeStruct((HEADS, SWEEPS), F32),
        ],
        in_specs=vmem_specs(2),
        out_specs=vmem_specs(4),
        scratch_shapes=[pltpu.VMEM((128, 128), F32)],
    )(small, grads)


def per_device(count, lats, latents, keys, values, sweep, sweep_bias, grad_out):
    grads, small = whole(
        latents, keys, values, sweep.reshape(1, -1), sweep_bias, grad_out, count, lats
    )
    return tuple(deliver(small, grads))


def solution(mesh):
    return jax.shard_map(
        functools.partial(per_device, mesh.shape["pts"], mesh.shape["lat"]),
        mesh=mesh,
        in_specs=(P("lat", None), P("pts", None), P("pts", None), P("pts"), P(), P("lat", None)),
        out_specs=(P(("lat", "pts"), None), P(("pts", "lat"), None), P(("pts", "lat"), None), P()),
        check_vma=False,
    )
```

```python
import functools
import math

import jax
import jax.numpy as jnp
from jax import lax
from jax.experimental import pallas as pl
from jax.experimental.pallas import tpu as pltpu
from jax.sharding import PartitionSpec as P

HEADS = 4
HEAD_DIM = 32
WIDTH = HEADS * HEAD_DIM
SWEEPS = 16
SCALE = HEAD_DIM**-0.5
LOG2E = math.log2(math.e)
TO_LOG2 = SCALE * LOG2E
YS = 4
ONES_ROW = 3 * SWEEPS
BF = jnp.bfloat16
F32 = jnp.float32
MESH = pl.DeviceIdType.MESH
VMEM_BYTES = 56 * 1024 * 1024


def dot(a, b):
    return jnp.dot(a, b, preferred_element_type=F32)


def dot_transposed(a, b):
    return lax.dot_general(a, b, (((1,), (1,)), ((), ())), preferred_element_type=F32)


def three_pieces(x):
    hi = x.astype(BF)
    rest = x - hi.astype(F32)
    mid = rest.astype(BF)
    low = (rest - mid.astype(F32)).astype(BF)
    return hi, mid, low


def vmem_specs(count):
    return [pl.BlockSpec(memory_space=pltpu.VMEM)] * count


def whole_kernel(
    count,
    lats,
    latents_ref,
    keys_ref,
    values_ref,
    sweep_ref,
    sweep_bias_ref,
    grad_out_ref,
    grads_ref,
    small_ref,
    k_aux,
    value_rows,
    onehot_t,
    own_rows,
    other_rows,
    g_t,
    q_feat,
    g_feat,
    scores_0,
    scores_1,
    stats,
    from_sibling,
    stats_1,
    stats_x,
    stats_2,
    stats_z,
    result,
    results,
    k_stage,
    v_stage,
    mark_stage,
    probs,
    scaled,
    part_sum,
    from_ring,
    grad_q_t,
    bias_sum,
    q_parts,
    from_core,
    bias_1,
    q_x,
    got_q_x,
    q_z,
    got_q_z,
    bias_2,
    bias_z,
    sent_lz,
    got_lz,
    sent_lx,
    got_lx,
    sent_lc,
    got_lc,
    sent_s1,
    got_s1,
    sent_sx,
    got_sx,
    sent_sz,
    got_sz,
    sent_sr,
    got_sr,
    sent_ring,
    got_ring,
    sent_core,
    got_core,
    sent_b1,
    got_b1,
    sent_qx,
    got_qx,
    sent_qz,
    got_qz,
    sent_b2,
    got_b2,
):
    latents = latents_ref.shape[0]
    points = keys_ref.shape[0] // 2
    span = latents // 2
    cols = min(256, span)
    per_span = span // cols
    per_tile = cols // 128
    group_tiles = HEADS * per_span
    group_lines = group_tiles * per_tile
    tiles = 4 * group_tiles
    group_pairs = group_tiles // 2
    chunk = min(512, points)
    chunks = points // chunk
    block = points // YS
    half = block // 2
    chips = count // 2
    nz = 4 if chips % 4 == 0 else chips
    nx = chips // nz
    heights = 2 * nz
    near = nz // 2
    rows_out = latents // count
    slice_rows = span // (2 * nx)
    lines = stats.shape[2] // nx

    me = lax.axis_index("pts")
    lat = lax.axis_index("lat")
    core = lax.rem(me, 2)
    chip = me // 2
    z, y = lat // YS, lax.rem(lat, YS)
    up = z * YS + lax.rem(y + 1, YS)
    down = z * YS + lax.rem(y + YS - 1, YS)
    x, zl = chip // nz, lax.rem(chip, nz)
    height = z * nz + zl
    sibling = {"pts": me + 1 - 2 * core}

    def x_peer(k):
        return {"pts": (lax.rem(x + k, nx) * nz + zl) * 2 + core}

    def y_peer(k):
        there = lax.rem(y * 2 + core + k, 2 * YS)
        return {"pts": chip * 2 + lax.rem(there, 2), "lat": z * YS + there // 2}

    def at_height(there):
        return {"pts": (x * nz + lax.rem(there, nz)) * 2 + core, "lat": (there // nz) * YS + y}

    def height_peer(k):
        return at_height(lax.rem(height + k, heights))

    def remote(src, dst, sent, got, device):
        return pltpu.make_async_remote_copy(
            src_ref=src,
            dst_ref=dst,
            send_sem=sent,
            recv_sem=got,
            device_id=device,
            device_id_type=MESH,
        )

    barrier = pltpu.get_barrier_semaphore()
    greeted = (
        [x_peer(k) for k in range(1, nx)]
        + [height_peer(k) for k in range(1, heights)]
        + [y_peer(k) for k in range(1, 2 * YS)]
    )
    for device in greeted:
        pl.semaphore_signal(barrier, inc=1, device_id=device, device_id_type=MESH)

    order = [p for parity in range(2) for p in range(count) if (p // 2) % 2 == parity]
    for at, p in enumerate(order):
        to, of = slice(at * rows_out, (at + 1) * rows_out), slice(p * rows_out, (p + 1) * rows_out)
        own_rows[to, :WIDTH] = latents_ref[of, :].astype(F32)
        own_rows[to, WIDTH:] = grad_out_ref[of, :].astype(F32)

    def other_z(s):
        first = s * span + (core * nx + x) * slice_rows
        return remote(
            own_rows.at[pl.ds(pl.multiple_of(first, slice_rows), slice_rows)],
            other_rows.at[s, core, x],
            sent_lz.at[s],
            got_lz.at[s],
            at_height(heights - 1 - height),
        )

    def other_x(s, k):
        return remote(
            other_rows.at[s, core, x],
            other_rows.at[s, core, x],
            sent_lx.at[s, k],
            got_lx.at[s, k],
            x_peer(k),
        )

    def other_core(s):
        return remote(
            other_rows.at[s, core], other_rows.at[s, core], sent_lc.at[s], got_lc.at[s], sibling
        )

    def forward_x(s):
        other_z(s).wait_recv()
        for k in range(1, nx):
            other_x(s, k).start()

    def forward_core(s):
        for k in range(1, nx):
            other_x(s, k).wait_recv()
        other_core(s).start()

    pl.semaphore_wait(barrier, len(greeted))
    for s in range(2):
        other_z(s).start()

    base = z * points
    k_aux[:, :WIDTH] = keys_ref[pl.ds(pl.multiple_of(base, points), points), :]

    def build(c, unused):
        rows = pl.ds(pl.multiple_of(c * chunk, chunk), chunk)
        source = pl.ds(pl.multiple_of(base + c * chunk, chunk), chunk)
        swept = sweep_ref[:, source]
        row = lax.broadcasted_iota(jnp.int32, (WIDTH, chunk), 0)
        marked = (row < ONES_ROW) & (lax.rem(row, SWEEPS) == swept)
        ones = (row >= ONES_ROW) & (row < ONES_ROW + 3)
        aux_t = jnp.where(marked | ones, 1.0, 0.0)
        onehot_t[:, rows] = aux_t[:SWEEPS].astype(BF)
        k_aux[rows, WIDTH:] = aux_t.T.astype(BF)
        value_t = values_ref[source, :].T
        for h in range(HEADS):
            value_rows[h, :HEAD_DIM, rows] = value_t[h * HEAD_DIM : (h + 1) * HEAD_DIM, :]
            value_rows[h, HEAD_DIM:, rows] = jnp.where(row[:16] == 0, 1.0, 0.0).astype(BF)
        return unused

    lax.fori_loop(0, chunks, build, 0)
    eye = lax.broadcasted_iota(jnp.int32, (SWEEPS, SWEEPS), 0) == lax.broadcasted_iota(
        jnp.int32, (SWEEPS, SWEEPS), 1
    )

    def features(g, both):
        q_t = both[:, :WIDTH].T.astype(BF)
        out_t = both[:, WIDTH:].T.astype(BF)
        g_t[:, g * span : (g + 1) * span] = out_t
        for h in range(HEADS):
            rows = slice(h * HEAD_DIM, (h + 1) * HEAD_DIM)
            column = jnp.sum(
                jnp.where(eye, sweep_bias_ref[h : h + 1, :], 0.0), axis=1, keepdims=True
            ) * (1.0 / SCALE)
            n = g * HEADS + h
            q_feat[n] = jnp.zeros((2 * WIDTH, span), BF)
            g_feat[n] = jnp.zeros((2 * WIDTH, span), BF)
            q_feat[n, rows, :] = q_t[rows]
            g_feat[n, rows, :] = out_t[rows]
            for index, piece in enumerate(
                three_pieces(jnp.broadcast_to(column, (SWEEPS, span)))
            ):
                q_feat[n, WIDTH + index * SWEEPS : WIDTH + (index + 1) * SWEEPS, :] = piece

    def take_other(s):
        other_core(s).wait_recv()
        features(2 + s, other_rows[s].reshape(span, 2 * WIDTH))

    for s in range(2):
        features(s, own_rows[s * span : (s + 1) * span, :])
    forward_x(0)
    grad_q_t[...] = jnp.zeros_like(grad_q_t)
    bias_sum[...] = jnp.zeros_like(bias_sum)
    part_sum[...] = jnp.zeros_like(part_sum)

    def merge(parts):
        best = functools.reduce(jnp.maximum, [part[0] for part in parts])
        weights = [jnp.exp2(part[0] - best) for part in parts]
        sums = [sum(w * part[kind] for w, part in zip(weights, parts)) for kind in (1, 2)]
        return [best] + sums

    def share_of(there):
        return pl.ds(pl.multiple_of(there * lines, lines), lines)

    def to_sibling(s):
        return remote(stats.at[s], from_sibling.at[s], sent_s1.at[s], got_s1.at[s], sibling)

    def along_x(s, k):
        return remote(
            stats_1.at[s, :, share_of(lax.rem(x + k, nx))],
            stats_x.at[s, x],
            sent_sx.at[s, k],
            got_sx.at[s, k],
            x_peer(k),
        )

    def along_z(s, k):
        return remote(
            stats_2.at[s], stats_z.at[s, height], sent_sz.at[s, k], got_sz.at[s, k], height_peer(k)
        )

    def results_x(s, k):
        return remote(
            result.at[s], results.at[s, x], sent_sr.at[s, k], got_sr.at[s, k], x_peer(k)
        )

    def exchange_x(s):
        to_sibling(s).wait_recv()
        merged = merge([stats[s], from_sibling[s]])
        for kind, value in enumerate(merged):
            stats_1[s, kind] = value
        for k in range(1, nx):
            along_x(s, k).start()
        stats_x[s, x] = stats_1[s, :, share_of(x), :]

    def exchange_z(s):
        for k in range(1, nx):
            along_x(s, k).wait_recv()
        for kind, value in enumerate(merge([stats_x[s, i] for i in range(nx)])):
            stats_2[s, kind] = value
        for k in range(1, heights):
            along_z(s, k).start()
        stats_z[s, height] = stats_2[s]

    def exchange_results(s):
        for k in range(1, heights):
            along_z(s, k).wait_recv()
        best, total, weighted = merge([stats_z[s, i] for i in range(heights)])
        result[s, 0] = (best + jnp.log(total) * LOG2E) * (-1.0 / TO_LOG2)
        result[s, 1] = -(weighted / total)
        for k in range(1, nx):
            results_x(s, k).start()
        results[s, x] = result[s]

    def take_results(s):
        for k in range(1, nx):
            results_x(s, k).wait_recv()
        row16 = lax.broadcasted_iota(jnp.int32, (16, 128), 0)
        for side in range(2):
            whose = z if side == 0 else 1 - z
            for n in range(group_tiles):
                it, h = n // HEADS, n % HEADS
                for part in range(per_tile):
                    line = whose * group_lines + n * per_tile + part
                    left = it * cols + part * 128
                    for kind, feat in ((0, q_feat), (1, g_feat)):
                        value = results[s, line // lines, kind, pl.ds(lax.rem(line, lines), 1), :]
                        hi, mid, low = three_pieces(value)
                        feat[
                            (2 * side + s) * HEADS + h,
                            WIDTH + ONES_ROW : WIDTH + ONES_ROW + 16,
                            left : left + 128,
                        ] = jnp.where(
                            row16 == 0,
                            hi.astype(F32),
                            jnp.where(
                                row16 == 1,
                                mid.astype(F32),
                                jnp.where(row16 == 2, low.astype(F32), 0.0),
                            ),
                        ).astype(BF)

    lowest = jnp.full((32, cols), -jnp.inf, F32)

    def tile_lanes(n):
        return pl.ds(pl.multiple_of((lax.rem(n, group_tiles) // HEADS) * cols, cols), cols)

    def score_chunk(n, into, c, top):
        index = (n // group_tiles) * HEADS + lax.rem(n, HEADS)
        rows = pl.ds(c * chunk, chunk)
        s = dot(k_aux[rows, :], q_feat[index, :, tile_lanes(n)]) * TO_LOG2
        into[rows, :] = s
        return jnp.maximum(top, jnp.max(s.reshape(chunk // 32, 32, cols), axis=0))

    def tile_sums(n, scores, top_rows, following, into):
        top = jnp.max(top_rows, axis=0, keepdims=True)
        head = lax.rem(n, HEADS)
        next_top = lowest
        out = jnp.zeros((48, cols), F32)
        for c in range(chunks):
            rows = pl.ds(c * chunk, chunk)
            e = jnp.exp2(scores[rows, :] - top)
            out = out + dot(value_rows[head, :, rows], e.astype(BF))
            next_top = score_chunk(following, into, c, next_top)
        group = n // group_tiles
        g = g_t[
            pl.ds(pl.multiple_of(head * HEAD_DIM, HEAD_DIM), HEAD_DIM),
            pl.ds(
                pl.multiple_of(group * span + (lax.rem(n, group_tiles) // HEADS) * cols, cols), cols
            ),
        ].astype(F32)
        weighted = jnp.sum(out[:HEAD_DIM] * g, axis=0, keepdims=True)
        total = out[HEAD_DIM : HEAD_DIM + 1]
        whose = jnp.where(group < 2, z, 1 - z)
        for kind, value in enumerate((top, total, weighted)):
            for part in range(per_tile):
                line = whose * group_lines + lax.rem(n, group_tiles) * per_tile + part
                stats[lax.rem(group, 2), kind, pl.ds(line, 1), :] = value[
                    :, part * 128 : (part + 1) * 128
                ]
        return next_top

    first_top = lowest
    for c in range(chunks):
        first_top = score_chunk(0, scores_0, c, first_top)

    def per_pair(pair, top_rows):
        n = pair * 2

        @pl.when(pair == 2 * group_pairs - 1)
        def _():
            take_other(0)

        @pl.when(pair == 3 * group_pairs - 1)
        def _():
            take_other(1)

        top_rows = tile_sums(n, scores_0, top_rows, n + 1, scores_1)
        top_rows = tile_sums(n + 1, scores_1, top_rows, lax.rem(n + 2, tiles), scores_0)

        @pl.when(pair == group_pairs // 2 - 1)
        def _():
            forward_x(1)

        @pl.when(pair == group_pairs - 1)
        def _():
            forward_core(0)

        @pl.when(pair == group_pairs + group_pairs // 2)
        def _():
            forward_core(1)

        @pl.when(pair == 3 * group_pairs - 1)
        def _():
            to_sibling(0).start()

        @pl.when(pair == 3 * group_pairs)
        def _():
            exchange_x(0)

        @pl.when(pair == max(3 * group_pairs + 1, 4 * group_pairs - 3))
        def _():
            exchange_z(0)

        @pl.when(pair == 4 * group_pairs - 1)
        def _():
            exchange_results(0)

        return top_rows

    lax.fori_loop(0, 4 * group_pairs, per_pair, first_top)
    to_sibling(1).start()
    take_results(0)

    lane_row = lax.broadcasted_iota(jnp.int32, (block, 128), 1)

    def compute(step, g):
        y_up = lax.rem(y + 2 * YS - 1 - step, YS)
        y_down = lax.rem(y + 1 + step, YS)
        for row, at in ((0, y_up * block), (half, y_down * block + half)):
            here = pl.ds(pl.multiple_of(at, half), half)
            rows = pl.ds(row, half)
            k_stage[rows, :] = k_aux[here, :]
            v_stage[rows, :WIDTH] = values_ref[pl.ds(pl.multiple_of(base + at, half), half), :]
            v_stage[rows, WIDTH:] = k_aux[here, WIDTH:]
            mark_stage[:, row : row + half] = onehot_t[:, here]
        k_t = k_stage[:, :WIDTH].T
        row_sums = jnp.zeros((block, 128), F32)
        lanes = pl.ds(pl.multiple_of(g * span, span), span)
        for h in range(HEADS):
            n = g * HEADS + h
            rows = slice(h * HEAD_DIM, (h + 1) * HEAD_DIM)
            p = jnp.exp2(dot(k_stage[...], q_feat[n]) * TO_LOG2)
            score_grad = p * dot(v_stage[...], g_feat[n])
            probs[h] = p.astype(BF)
            scaled[h] = (score_grad * SCALE).astype(BF)
            folded = score_grad[:, :128]
            for part in range(1, span // 128):
                folded = folded + score_grad[:, part * 128 : (part + 1) * 128]
            row_sums = row_sums + jnp.where(
                lane_row == h, jnp.sum(folded, axis=1, keepdims=True), 0.0
            )
            part_sum[step, rows, :] += dot_transposed(q_feat[n, rows, :], scaled[h])
            part_sum[step, WIDTH + h * HEAD_DIM : WIDTH + (h + 1) * HEAD_DIM, :] += dot_transposed(
                g_feat[n, rows, :], probs[h]
            )
            grad_q_t[rows, lanes] += dot(k_t[rows, :], scaled[h])
        for piece in three_pieces(row_sums):
            bias_sum[:SWEEPS, :] += dot(mark_stage[...], piece)

    def ring(step, way):
        here = pl.ds(way * half, half)
        return remote(
            part_sum.at[step, :, here],
            from_ring.at[step, :, here],
            sent_ring.at[step, way],
            got_ring.at[step, way],
            {"lat": down if way else up},
        )

    def finish(step):
        if step > 0:
            for way in range(2):
                ring(step - 1, way).wait_recv()
            part_sum[step] += from_ring[step - 1]
        if step < YS - 1:
            for way in range(2):
                ring(step, way).start()

    def swap(s):
        return remote(
            q_parts.at[s, 1 - core], from_core.at[s], sent_core.at[s], got_core.at[s], sibling
        )

    def q_along_x(s, k):
        rows = near * 2 * rows_out + s * SWEEPS
        return remote(
            q_x.at[s, lax.rem(x + k, nx), pl.ds(0, rows)],
            got_q_x.at[s, x, pl.ds(0, rows)],
            sent_qx.at[s, k],
            got_qx.at[s, k],
            x_peer(k),
        )

    def start_swap(s):
        for side in range(2):
            g = 2 * side + s
            whose = z if side == 0 else 1 - z
            grad_q = grad_q_t[:, g * span : (g + 1) * span].T
            for j in range(chips):
                m = j // 2
                q_parts[s, j % 2, m // near, whose * near + m % near] = grad_q[
                    j * rows_out : (j + 1) * rows_out
                ]
        swap(s).start()

    def send_x(s, bias):
        swap(s).wait_recv()
        for i in range(nx):
            for j in range(2 * near):
                q_x[s, i, j * rows_out : (j + 1) * rows_out, :] = (
                    q_parts[s, core, i, j] + from_core[s, i, j]
                )
            if bias is not None:
                q_x[s, i, 2 * near * rows_out :, :] = bias
        for k in range(1, nx):
            q_along_x(s, k).start()
        got_q_x[s, x] = q_x[s, x]

    def height_copies(s, action):
        for j in range(2 * near):
            there = (j // near) * nz + 2 * (j % near) + s

            @pl.when(height != there)
            def _():
                action(
                    remote(
                        q_z.at[s, j],
                        got_q_z.at[height],
                        sent_qz.at[there],
                        got_qz.at[height],
                        at_height(there),
                    )
                )

            if action is start:

                @pl.when(height == there)
                def _():
                    got_q_z[height] = q_z[s, j]

    def start(copy):
        copy.start()

    def wait_send(copy):
        copy.wait_send()

    def send_z(s):
        for k in range(1, nx):
            q_along_x(s, k).wait_recv()
        summed = jnp.sum(got_q_x[s, :, : 2 * near * rows_out, :], axis=0)
        for j in range(2 * near):
            q_z[s, j] = summed[j * rows_out : (j + 1) * rows_out]
        height_copies(s, start)

    def per_item(t, unused):
        step = t // 4
        g = lax.rem(t, 4)
        g = jnp.where(g == 1, 2, jnp.where(g == 2, 1, g))
        for when, at, group in (
            (2, 1, 0), (3, 1, 2), (4, 0, 1), (5, 0, 3), (6, 1, 1), (7, 1, 3),
        ):
            step = jnp.where(t == when, at, step)
            g = jnp.where(t == when, group, g)

        @pl.when(t == 4)
        def _():
            take_results(1)

        compute(step, g)

        for when, action in (
            (0, lambda: exchange_x(1)),
            (1, lambda: exchange_z(1)),
            (2, lambda: exchange_results(1)),
            (5, lambda: finish(0)),
            (8, lambda: finish(1)),
            (11, lambda: finish(2)),
            (13, lambda: start_swap(0)),
            (14, lambda: send_x(0, None)),
        ):
            pl.when(t == when)(action)
        return unused

    lax.fori_loop(0, 4 * YS, per_item, 0)

    def bias_y(k):
        return remote(
            bias_sum.at[pl.ds(0, SWEEPS)],
            bias_1.at[y * 2 + core],
            sent_b1.at[k],
            got_b1.at[k],
            y_peer(k),
        )

    def bias_along_z(k):
        return remote(bias_2, bias_z.at[height], sent_b2.at[k], got_b2.at[k], height_peer(k))

    bias_copies = [bias_y(k) for k in range(1, 2 * YS)]
    bias_z_copies = [bias_along_z(k) for k in range(1, heights)]

    for copy in bias_copies:
        copy.start()
    start_swap(1)
    send_z(0)
    bias_1[y * 2 + core] = bias_sum[:SWEEPS, :]
    for copy in bias_copies:
        copy.wait_recv()
    send_x(1, jnp.sum(bias_1[...], axis=0))
    finish(YS - 1)
    grads_ref[...] = part_sum[YS - 1]
    send_z(1)
    bias_2[...] = jnp.sum(got_q_x[1, :, 2 * near * rows_out :, :], axis=0)
    for copy in bias_z_copies:
        copy.start()
    bias_z[height] = bias_2[...]
    for source in range(heights):

        @pl.when(height != source)
        def _():
            remote(
                q_z.at[0, 0],
                got_q_z.at[source],
                sent_qz.at[source],
                got_qz.at[source],
                at_height(source),
            ).wait_recv()

    for copy in bias_z_copies:
        copy.wait_recv()
    small_ref[:rows_out, :] = jnp.sum(got_q_z[...], axis=0)
    small_ref[rows_out:, :] = jnp.sum(bias_z[...], axis=0)

    for s in range(2):
        other_z(s).wait_send()
        other_core(s).wait_send()
        to_sibling(s).wait_send()
        swap(s).wait_send()
        for k in range(1, nx):
            other_x(s, k).wait_send()
            along_x(s, k).wait_send()
            results_x(s, k).wait_send()
            q_along_x(s, k).wait_send()
        for k in range(1, heights):
            along_z(s, k).wait_send()
        height_copies(s, wait_send)
    for step in range(YS - 1):
        for way in range(2):
            ring(step, way).wait_send()
    for copy in bias_copies + bias_z_copies:
        copy.wait_send()


def whole(latents, keys, values, sweep, sweep_bias, grad_out, count, lats):
    rows, points = latents.shape[0], keys.shape[0] // 2
    block, span, chips = points // YS, rows // 2, count // 2
    cols = min(256, span)
    lines = 2 * HEADS * span // 128
    nz = 4 if chips % 4 == 0 else chips
    nx = chips // nz
    heights, near = 2 * nz, nz // 2
    rows_out = rows // count
    x_rows = 2 * near * rows_out
    dma = pltpu.SemaphoreType.DMA
    return pl.pallas_call(
        functools.partial(whole_kernel, count, lats),
        out_shape=[
            jax.ShapeDtypeStruct((2 * WIDTH, block), F32),
            jax.ShapeDtypeStruct((rows_out + SWEEPS, WIDTH), F32),
        ],
        in_specs=vmem_specs(6),
        out_specs=vmem_specs(2),
        scratch_shapes=[
            pltpu.VMEM((points, 2 * WIDTH), BF),
            pltpu.VMEM((HEADS, 48, points), BF),
            pltpu.VMEM((SWEEPS, points), BF),
            pltpu.VMEM((rows, 2 * WIDTH), F32),
            pltpu.VMEM((2, 2, nx, span // (2 * nx), 2 * WIDTH), F32),
            pltpu.VMEM((WIDTH, 4 * span), BF),
            pltpu.VMEM((4 * HEADS, 2 * WIDTH, span), BF),
            pltpu.VMEM((4 * HEADS, 2 * WIDTH, span), BF),
            pltpu.VMEM((points, cols), F32),
            pltpu.VMEM((points, cols), F32),
            pltpu.VMEM((2, 3, lines, 128), F32),
            pltpu.VMEM((2, 3, lines, 128), F32),
            pltpu.VMEM((2, 3, lines, 128), F32),
            pltpu.VMEM((2, nx, 3, lines // nx, 128), F32),
            pltpu.VMEM((2, 3, lines // nx, 128), F32),
            pltpu.VMEM((2, heights, 3, lines // nx, 128), F32),
            pltpu.VMEM((2, 2, lines // nx, 128), F32),
            pltpu.VMEM((2, nx, 2, lines // nx, 128), F32),
            pltpu.VMEM((block, 2 * WIDTH), BF),
            pltpu.VMEM((block, 2 * WIDTH), BF),
            pltpu.VMEM((SWEEPS, block), BF),
            pltpu.VMEM((HEADS, block, span), BF),
            pltpu.VMEM((HEADS, block, span), BF),
            pltpu.VMEM((YS, 2 * WIDTH, block), F32),
            pltpu.VMEM((YS, 2 * WIDTH, block), F32),
            pltpu.VMEM((WIDTH, 4 * span), F32),
            pltpu.VMEM((128, 128), F32),
            pltpu.VMEM((2, 2, nx, 2 * near, rows_out, WIDTH), F32),
            pltpu.VMEM((2, nx, 2 * near, rows_out, WIDTH), F32),
            pltpu.VMEM((2 * YS, SWEEPS, 128), F32),
            pltpu.VMEM((2, nx, x_rows + SWEEPS, WIDTH), F32),
            pltpu.VMEM((2, nx, x_rows + SWEEPS, WIDTH), F32),
            pltpu.VMEM((2, 2 * near, rows_out, WIDTH), F32),
            pltpu.VMEM((heights, rows_out, WIDTH), F32),
            pltpu.VMEM((SWEEPS, 128), F32),
            pltpu.VMEM((heights, SWEEPS, 128), F32),
            dma((2,)),
            dma((2,)),
            dma((2, nx)),
            dma((2, nx)),
            dma((2,)),
            dma((2,)),
            dma((2,)),
            dma((2,)),
            dma((2, nx)),
            dma((2, nx)),
            dma((2, heights)),
            dma((2, heights)),
            dma((2, nx)),
            dma((2, nx)),
            dma((YS, 2)),
            dma((YS, 2)),
            dma((2,)),
            dma((2,)),
            dma((2 * YS,)),
            dma((2 * YS,)),
            dma((2, nx)),
            dma((2, nx)),
            dma((heights,)),
            dma((heights,)),
            dma((heights,)),
            dma((heights,)),
        ],
        compiler_params=pltpu.CompilerParams(
            collective_id=0, has_side_effects=True, vmem_limit_bytes=VMEM_BYTES
        ),
    )(latents, keys, values, sweep, sweep_bias, grad_out)


def deliver_kernel(small_ref, grads_ref, q_out, k_out, v_out, bias_out, square):
    rows_out = q_out.shape[0]
    q_out[...] = small_ref[:rows_out, :]
    k_out[...] = grads_ref[:WIDTH, :].T
    v_out[...] = grads_ref[WIDTH:, :].T
    square[...] = jnp.zeros_like(square)
    square[:SWEEPS, :] = small_ref[rows_out:, :]
    bias_out[...] = square[...].T[:HEADS, :SWEEPS]


def deliver(small, grads):
    block = grads.shape[1]
    return pl.pallas_call(
        deliver_kernel,
        out_shape=[
            jax.ShapeDtypeStruct((small.shape[0] - SWEEPS, WIDTH), F32),
            jax.ShapeDtypeStruct((block, WIDTH), F32),
            jax.ShapeDtypeStruct((block, WIDTH), F32),
            jax.ShapeDtypeStruct((HEADS, SWEEPS), F32),
        ],
        in_specs=vmem_specs(2),
        out_specs=vmem_specs(4),
        scratch_shapes=[pltpu.VMEM((128, 128), F32)],
    )(small, grads)


def per_device(count, lats, latents, keys, values, sweep, sweep_bias, grad_out):
    grads, small = whole(
        latents, keys, values, sweep.reshape(1, -1), sweep_bias, grad_out, count, lats
    )
    return tuple(deliver(small, grads))


def solution(mesh):
    return jax.shard_map(
        functools.partial(per_device, mesh.shape["pts"], mesh.shape["lat"]),
        mesh=mesh,
        in_specs=(P("lat", None), P("pts", None), P("pts", None), P("pts"), P(), P("lat", None)),
        out_specs=(P(("lat", "pts"), None), P(("pts", "lat"), None), P(("pts", "lat"), None), P()),
        check_vma=False,
    )
```

```python
import functools
import math

import jax
import jax.numpy as jnp
from jax import lax
from jax.experimental import pallas as pl
from jax.experimental.pallas import tpu as pltpu
from jax.sharding import PartitionSpec as P

HEADS = 4
HEAD_DIM = 32
WIDTH = HEADS * HEAD_DIM
SWEEPS = 16
SCALE = HEAD_DIM**-0.5
LOG2E = math.log2(math.e)
TO_LOG2 = SCALE * LOG2E
YS = 4
ONES_ROW = 3 * SWEEPS
BF = jnp.bfloat16
F32 = jnp.float32
MESH = pl.DeviceIdType.MESH
VMEM_BYTES = 56 * 1024 * 1024


def dot(a, b):
    return jnp.dot(a, b, preferred_element_type=F32)


def dot_transposed(a, b):
    return lax.dot_general(a, b, (((1,), (1,)), ((), ())), preferred_element_type=F32)


def three_pieces(x):
    hi = x.astype(BF)
    rest = x - hi.astype(F32)
    mid = rest.astype(BF)
    low = (rest - mid.astype(F32)).astype(BF)
    return hi, mid, low


def vmem_specs(count):
    return [pl.BlockSpec(memory_space=pltpu.VMEM)] * count


def whole_kernel(
    count,
    lats,
    latents_ref,
    keys_ref,
    values_ref,
    sweep_ref,
    sweep_bias_ref,
    grad_out_ref,
    grads_ref,
    small_ref,
    k_aux,
    value_rows,
    onehot_t,
    g_t,
    q_feat,
    g_feat,
    scores_0,
    scores_1,
    kept,
    factors,
    g_factored,
    stats,
    from_sibling,
    stats_1,
    stats_x,
    stats_2,
    stats_z,
    k_stage,
    v_stage,
    mark_stage,
    probs,
    scaled,
    part_sum,
    from_ring,
    relay,
    from_z,
    grad_q_t,
    bias_sum,
    q_parts,
    from_core,
    bias_1,
    q_x,
    got_q_x,
    q_z,
    got_q_z,
    bias_2,
    bias_z,
    sent_s1,
    got_s1,
    sent_sx,
    got_sx,
    sent_sz,
    got_sz,
    sent_ring,
    got_ring,
    sent_near,
    got_near,
    sent_far,
    got_far,
    sent_core,
    got_core,
    sent_b1,
    got_b1,
    sent_qx,
    got_qx,
    sent_qz,
    got_qz,
    sent_b2,
    got_b2,
):
    points, latents = keys_ref.shape[0], latents_ref.shape[0]
    span = latents // 2
    cols = min(256, span)
    per_span = span // cols
    tiles = HEADS * 2 * per_span
    pairs = tiles // 2
    chunk = min(512, points)
    chunks = points // chunk
    block = points // (2 * YS)
    half = block // 2
    quarter = block // 4
    chips = count // 2
    nz = 4 if chips % 4 == 0 else chips
    nx = chips // nz
    heights = 2 * nz
    rows_out = latents // count

    me = lax.axis_index("pts")
    lat = lax.axis_index("lat")
    core = lax.rem(me, 2)
    chip = me // 2
    z, y = lat // YS, lax.rem(lat, YS)
    up = z * YS + lax.rem(y + 1, YS)
    down = z * YS + lax.rem(y + YS - 1, YS)
    x, zl = chip // nz, lax.rem(chip, nz)
    height = z * nz + zl

    def x_peer(k):
        return {"pts": (lax.rem(x + k, nx) * nz + zl) * 2 + core}

    def z_peer(k):
        return {"pts": (x * nz + lax.rem(zl + k, nz)) * 2 + core}

    def y_peer(k):
        there = lax.rem(y * 2 + core + k, 2 * YS)
        return {"pts": chip * 2 + lax.rem(there, 2), "lat": z * YS + there // 2}

    def at_height(shift):
        there = lax.rem(height + shift + heights, heights)
        return {"pts": (x * nz + lax.rem(there, nz)) * 2 + core, "lat": (there // nz) * YS + y}

    def remote(src, dst, sent, got, device):
        return pltpu.make_async_remote_copy(
            src_ref=src,
            dst_ref=dst,
            send_sem=sent,
            recv_sem=got,
            device_id=device,
            device_id_type=MESH,
        )

    def every(start, stop, action):
        def step(k, unused):
            action(k)
            return unused

        lax.fori_loop(start, stop, step, 0)

    barrier = pltpu.get_barrier_semaphore()
    greeted = (
        [x_peer(k) for k in range(1, nx)]
        + [at_height(k) for k in range(1, heights)]
        + [y_peer(k) for k in range(1, 2 * YS)]
    )
    for device in greeted:
        pl.semaphore_signal(barrier, inc=1, device_id=device, device_id_type=MESH)

    k_aux[:, :WIDTH] = keys_ref[...]

    def build(c):
        rows = pl.ds(pl.multiple_of(c * chunk, chunk), chunk)
        swept = sweep_ref[:, rows]
        row = lax.broadcasted_iota(jnp.int32, (SWEEPS, chunk), 0)
        marked = jnp.where(row == swept, 1.0, 0.0)
        ones = jnp.where(row < 3, 1.0, 0.0)
        rest = jnp.zeros((WIDTH - 4 * SWEEPS, chunk), F32)
        aux_t = jnp.concatenate([marked, marked, marked, ones, rest], axis=0)
        onehot_t[:, rows] = marked.astype(BF)
        k_aux[rows, WIDTH:] = aux_t.T.astype(BF)
        value_t = values_ref[rows, :].T
        for h in range(HEADS):
            value_rows[h, :HEAD_DIM, rows] = value_t[h * HEAD_DIM : (h + 1) * HEAD_DIM, :]
            value_rows[h, HEAD_DIM:, rows] = jnp.where(row == 0, 1.0, 0.0).astype(BF)

    every(0, chunks, build)
    q_t = latents_ref[...].T
    g_t[...] = grad_out_ref[...].T
    eye = lax.broadcasted_iota(jnp.int32, (SWEEPS, SWEEPS), 0) == lax.broadcasted_iota(
        jnp.int32, (SWEEPS, SWEEPS), 1
    )
    for h in range(HEADS):
        rows = slice(h * HEAD_DIM, (h + 1) * HEAD_DIM)
        column = jnp.sum(
            jnp.where(eye, sweep_bias_ref[h : h + 1, :], 0.0), axis=1, keepdims=True
        ) * (1.0 / SCALE)
        bias_pieces = three_pieces(jnp.broadcast_to(column, (SWEEPS, span)))
        for s in range(2):
            n = s * HEADS + h
            here = slice(s * span, (s + 1) * span)
            q_feat[n] = jnp.zeros((2 * WIDTH, span), BF)
            g_feat[n] = jnp.zeros((2 * WIDTH, span), BF)
            q_feat[n, rows, :] = q_t[rows, here]
            g_feat[n, rows, :] = g_t[rows, here]
            for index, piece in enumerate(bias_pieces):
                q_feat[n, WIDTH + index * SWEEPS : WIDTH + (index + 1) * SWEEPS, :] = piece
    grad_q_t[...] = jnp.zeros_like(grad_q_t)
    bias_sum[...] = jnp.zeros_like(bias_sum)

    def merge(parts):
        best = functools.reduce(jnp.maximum, [part[0] for part in parts])
        weights = [jnp.exp2(part[0] - best) for part in parts]
        sums = [sum(w * part[kind] for w, part in zip(weights, parts)) for kind in (1, 2)]
        return [best] + sums

    def keep(ref, merged):
        for kind, value in enumerate(merged):
            ref[kind] = value

    def to_sibling(s):
        return remote(
            stats.at[s], from_sibling.at[s], sent_s1.at[s], got_s1.at[s], {"pts": me + 1 - 2 * core}
        )

    def along_x(s, k):
        return remote(
            stats_1.at[s], stats_x.at[s, x], sent_sx.at[s, k], got_sx.at[s, k], x_peer(k)
        )

    def along_z(s, k):
        return remote(
            stats_2.at[s], stats_z.at[s, zl], sent_sz.at[s, k], got_sz.at[s, k], z_peer(k)
        )

    def exchange_x(s):
        to_sibling(s).wait_recv()
        merged = merge([stats[s], from_sibling[s]])
        keep(stats_1.at[s], merged)
        for k in range(1, nx):
            along_x(s, k).start()
        keep(stats_x.at[s, x], merged)

    def exchange_z(s):
        for k in range(1, nx):
            along_x(s, k).wait_recv()
        merged = merge([stats_x[s, i] for i in range(nx)])
        keep(stats_2.at[s], merged)
        for k in range(1, nz):
            along_z(s, k).start()
        keep(stats_z.at[s, zl], merged)

    def take_results(s):
        for k in range(1, nz):
            along_z(s, k).wait_recv()
        best, total, weighted = merge([stats_z[s, i] for i in range(nz)])
        if s == 0:
            first = (best + jnp.log(total) * LOG2E) * (-1.0 / TO_LOG2)
        else:
            first = jnp.exp2(stats[s, 0] - best) / total
        delta = -(weighted / total)
        row16 = lax.broadcasted_iota(jnp.int32, (16, 128), 0)
        per_tile = cols // 128
        for n in range(tiles // 2):
            it, h = n // HEADS, n % HEADS
            for part in range(per_tile):
                line = n * per_tile + part
                left = it * cols + part * 128
                if s == 1:
                    factors[h : h + 1, left : left + 128] = first[line : line + 1, :]
                for value, feat in ((first, q_feat), (delta, g_feat))[s:]:
                    hi, mid, low = three_pieces(value[line : line + 1, :])
                    feat[
                        s * HEADS + h,
                        WIDTH + ONES_ROW : WIDTH + ONES_ROW + 16,
                        left : left + 128,
                    ] = jnp.where(
                        row16 == 0,
                        hi.astype(F32),
                        jnp.where(
                            row16 == 1, mid.astype(F32), jnp.where(row16 == 2, low.astype(F32), 0.0)
                        ),
                    ).astype(BF)

        if s == 1:
            for h in range(HEADS):
                rows = slice(h * HEAD_DIM, (h + 1) * HEAD_DIM)
                product = g_t[rows, span:].astype(F32) * factors[h : h + 1, :]
                hi, mid, _ = three_pieces(product)
                g_factored[h, :HEAD_DIM, :] = hi
                g_factored[h, HEAD_DIM:, :] = mid

    lowest = jnp.full((32, cols), -jnp.inf, F32)

    def feature_of(n):
        it = n // HEADS
        return (
            (it // per_span) * HEADS + lax.rem(n, HEADS),
            pl.ds(pl.multiple_of(lax.rem(it, per_span) * cols, cols), cols),
        )

    def score_chunk(n, into, c, top):
        index, lanes = feature_of(n)
        rows = pl.ds(c * chunk, chunk)
        s = dot(k_aux[rows, :], q_feat[index, :, lanes]) * TO_LOG2
        into[rows, :] = s
        return jnp.maximum(top, jnp.max(s.reshape(chunk // 32, 32, cols), axis=0))

    def tile_sums(keep_e, n, scores, top_rows, following, into):
        top = jnp.max(top_rows, axis=0, keepdims=True)
        head = lax.rem(n, HEADS)
        next_top = lowest
        unused_index, lanes = feature_of(n)
        out = jnp.zeros((48, cols), F32)
        for c in range(chunks):
            rows = pl.ds(c * chunk, chunk)
            e = jnp.exp2(scores[rows, :] - top).astype(BF)
            if keep_e:
                kept[head, rows, lanes] = e
            out = out + dot(value_rows[head, :, rows], e)
            next_top = score_chunk(following, into, c, next_top)
        g = g_t[
            pl.ds(pl.multiple_of(head * HEAD_DIM, HEAD_DIM), HEAD_DIM),
            pl.ds(pl.multiple_of((n // HEADS) * cols, cols), cols),
        ].astype(F32)
        weighted = jnp.sum(out[:HEAD_DIM] * g, axis=0, keepdims=True)
        total = out[HEAD_DIM : HEAD_DIM + 1]
        per_tile = cols // 128
        for kind, value in enumerate((top, total, weighted)):
            for part in range(per_tile):
                line = lax.rem(n, tiles // 2) * per_tile + part
                stats[n // (tiles // 2), kind, pl.ds(line, 1), :] = value[
                    :, part * 128 : (part + 1) * 128
                ]
        return next_top

    first_top = lowest
    for c in range(chunks):
        first_top = score_chunk(0, scores_0, c, first_top)

    def per_pair(keep_e, pair, top_rows):
        n = pair * 2
        top_rows = tile_sums(keep_e, n, scores_0, top_rows, n + 1, scores_1)
        top_rows = tile_sums(
            keep_e, n + 1, scores_1, top_rows, lax.rem(n + 2, tiles), scores_0
        )

        @pl.when(pair == pairs // 2 - 1)
        def _():
            pl.semaphore_wait(barrier, len(greeted))
            to_sibling(0).start()

        @pl.when(pair == pairs // 2)
        def _():
            exchange_x(0)

        @pl.when(pair == pairs // 2 + 1)
        def _():
            exchange_z(0)

        return top_rows

    first_top = lax.fori_loop(0, pairs // 2, functools.partial(per_pair, False), first_top)
    lax.fori_loop(pairs // 2, pairs, functools.partial(per_pair, True), first_top)
    to_sibling(1).start()
    take_results(0)

    lane_row = lax.broadcasted_iota(jnp.int32, (block, 128), 1)

    def compute(step, s):
        turn = lax.rem(step, YS)
        owner_z = jnp.where(step < YS, 1 - z, z)
        at_up = (owner_z * YS + lax.rem(y + 2 * YS - 1 - turn, YS)) * block
        at_down = (owner_z * YS + lax.rem(y + 1 + turn, YS)) * block + half
        places = []
        for row, at in ((0, at_up), (half, at_down)):
            source = pl.ds(pl.multiple_of(at, half), half)
            rows = pl.ds(row, half)
            if s == 0:
                k_stage[rows, :] = k_aux[source, :]
            else:
                k_stage[rows, :WIDTH] = keys_ref[source, :]
            v_stage[rows, :WIDTH] = values_ref[source, :]
            v_stage[rows, WIDTH:] = k_aux[source, WIDTH:]
            mark_stage[:, row : row + half] = onehot_t[:, source]
            places.append((slice(row, row + half), source))
        k_t = k_stage[:, :WIDTH].T
        row_sums = jnp.zeros((block, 128), F32)
        lanes = slice(s * span, (s + 1) * span)
        for h in range(HEADS):
            n = s * HEADS + h
            rows = slice(h * HEAD_DIM, (h + 1) * HEAD_DIM)
            rows_v = slice(WIDTH + h * HEAD_DIM, WIDTH + (h + 1) * HEAD_DIM)
            out_prod = dot(v_stage[...], g_feat[n])
            if s == 0:
                p = jnp.exp2(dot(k_stage[...], q_feat[n]) * TO_LOG2)
                low = (p * out_prod) * SCALE
                probs[h] = p.astype(BF)
                part_sum[step, rows_v, :] = dot_transposed(g_feat[n, rows, :], probs[h])
            else:
                out_prod = out_prod * (factors[h : h + 1, :] * SCALE)
                low = jnp.concatenate(
                    [
                        kept[h, source, :].astype(F32) * out_prod[place]
                        for place, source in places
                    ],
                    axis=0,
                )
                for place, source in places:
                    both = dot_transposed(g_factored[h], kept[h, source, :])
                    part_sum[step, rows_v, place] += both[:HEAD_DIM] + both[HEAD_DIM:]
            scaled[h] = low.astype(BF)
            folded = low[:, :128]
            for part in range(1, span // 128):
                folded = folded + low[:, part * 128 : (part + 1) * 128]
            row_sums = row_sums + jnp.where(
                lane_row == h, jnp.sum(folded, axis=1, keepdims=True), 0.0
            )
            grad_k = dot_transposed(q_feat[n, rows, :], scaled[h])
            if s == 0:
                part_sum[step, rows, :] = grad_k
            else:
                part_sum[step, rows, :] += grad_k
            grad_q_t[rows, lanes] += dot(k_t[rows, :], scaled[h])
        for piece in three_pieces(row_sums * (1.0 / SCALE)):
            bias_sum[:SWEEPS, :] += dot(mark_stage[...], piece)

    def lanes_of(part, way):
        return pl.ds(pl.multiple_of(way * half + part * quarter, quarter), quarter)

    def ring(step, part, way):
        here = lanes_of(part, way)
        return remote(
            part_sum.at[step, :, here],
            from_ring.at[step, :, here],
            sent_ring.at[step, part, way],
            got_ring.at[step, part, way],
            {"lat": down if way else up},
        )

    def near(part, way):
        return remote(
            part_sum.at[YS - 1, :, lanes_of(part, way)],
            relay.at[part, way],
            sent_near.at[part, way],
            got_near.at[part, way],
            at_height(-1 if way else 1),
        )

    def far(part, way):
        return remote(
            relay.at[part, way],
            from_z.at[:, lanes_of(part, way)],
            sent_far.at[part, way],
            got_far.at[part, way],
            at_height(1 - nz if way else nz - 1),
        )

    def finish(step, part):
        turn = lax.rem(step, YS)

        @pl.when(turn > 0)
        def _():
            for way in range(2):
                ring(step - 1, part, way).wait_recv()
                here = lanes_of(part, way)
                part_sum[step, :, here] += from_ring[step - 1, :, here]

        @pl.when(turn < YS - 1)
        def _():
            for way in range(2):
                ring(step, part, way).start()

        @pl.when(step == YS - 1)
        def _():
            for way in range(2):
                near(part, way).start()

    def per_item(t, unused):
        step = t // 2
        for when, value in ((1, 1), (2, 2), (3, 0), (4, 1), (5, 3), (6, 2)):
            step = jnp.where(t == when, value, step)
        s = jnp.where((t < 3) | (t == 5), 0, jnp.where(t < 8, 1, lax.rem(t, 2)))

        @pl.when(t == 3)
        def _():
            take_results(1)

        for index in range(2):
            pl.when(s == index)(functools.partial(compute, step, index))

        @pl.when(t == 0)
        def _():
            exchange_x(1)

        @pl.when(t == 1)
        def _():
            exchange_z(1)

        @pl.when(t >= 3)
        def _():
            finish(jnp.where(t < 11, (t - 3) // 2, (t - 1) // 2), lax.rem(t + 1, 2))

        @pl.when((t == 9) | (t == 10))
        def _():
            finish(YS, t - 9)

        for part in range(2):

            @pl.when(t == 11 + part)
            def _():
                for way in range(2):
                    near(part, way).wait_recv()
                    far(part, way).start()

        return unused

    lax.fori_loop(0, 4 * YS, per_item, 0)

    swap = remote(q_parts.at[1 - core], from_core, sent_core, got_core, {"pts": me + 1 - 2 * core})

    def bias_y(k):
        return remote(
            bias_sum.at[pl.ds(0, SWEEPS)],
            bias_1.at[y * 2 + core],
            sent_b1.at[k],
            got_b1.at[k],
            y_peer(k),
        )

    def q_along_x(k):
        return remote(
            q_x.at[lax.rem(x + k, nx)], got_q_x.at[x], sent_qx.at[k], got_qx.at[k], x_peer(k)
        )

    def q_along_z(k):
        return remote(
            q_z.at[lax.rem(zl + k, nz)], got_q_z.at[zl], sent_qz.at[k], got_qz.at[k], z_peer(k)
        )

    def bias_along_z(k):
        return remote(bias_2, bias_z.at[height], sent_b2.at[k], got_b2.at[k], at_height(k))

    bias_copies = [bias_y(k) for k in range(1, 2 * YS)]
    x_copies = [q_along_x(k) for k in range(1, nx)]
    z_copies = [q_along_z(k) for k in range(1, nz)]
    bias_z_copies = [bias_along_z(k) for k in range(1, heights)]

    for copy in bias_copies:
        copy.start()
    grad_q = grad_q_t[...].T
    for p in range(count):
        q_parts[p % 2, p // 2] = grad_q[p * rows_out : (p + 1) * rows_out]
    swap.start()
    bias_1[y * 2 + core] = bias_sum[:SWEEPS, :]
    for copy in bias_copies:
        copy.wait_recv()
    bias = jnp.sum(bias_1[...], axis=0)
    swap.wait_recv()
    for i in range(nx):
        for j in range(nz):
            q_x[i, j * rows_out : (j + 1) * rows_out, :] = (
                q_parts[core, i * nz + j] + from_core[i * nz + j]
            )
        q_x[i, nz * rows_out :, :] = bias
    for copy in x_copies:
        copy.start()
    got_q_x[x] = q_x[x]
    finish(2 * YS - 1, 1)
    for copy in x_copies:
        copy.wait_recv()
    summed = jnp.sum(got_q_x[...], axis=0)
    bias_2[...] = summed[nz * rows_out :]
    for j in range(nz):
        q_z[j] = summed[j * rows_out : (j + 1) * rows_out]
    for copy in bias_z_copies + z_copies:
        copy.start()
    got_q_z[zl] = q_z[zl]
    bias_z[height] = bias_2[...]
    for part in range(2):
        for way in range(2):
            far(part, way).wait_recv()
    grads_ref[...] = part_sum[2 * YS - 1] + from_z[...]
    for copy in bias_z_copies + z_copies:
        copy.wait_recv()
    small_ref[:rows_out, :] = jnp.sum(got_q_z[...], axis=0)
    small_ref[rows_out:, :] = jnp.sum(bias_z[...], axis=0)

    for s in range(2):
        to_sibling(s).wait_send()
        for k in range(1, nx):
            along_x(s, k).wait_send()
        for k in range(1, nz):
            along_z(s, k).wait_send()
    for part in range(2):
        for way in range(2):
            for step in range(2 * YS):
                if step % YS < YS - 1:
                    ring(step, part, way).wait_send()
            near(part, way).wait_send()
            far(part, way).wait_send()
    swap.wait_send()
    for copy in bias_copies + x_copies + z_copies + bias_z_copies:
        copy.wait_send()


def whole(latents, keys, values, sweep, sweep_bias, grad_out, count, lats):
    rows, points = latents.shape[0], keys.shape[0]
    block, span, chips = points // (2 * YS), rows // 2, count // 2
    cols = min(256, span)
    lines = HEADS * rows // 256
    nz = 4 if chips % 4 == 0 else chips
    nx = chips // nz
    heights = 2 * nz
    rows_out = rows // count
    dma = pltpu.SemaphoreType.DMA
    return pl.pallas_call(
        functools.partial(whole_kernel, count, lats),
        out_shape=[
            jax.ShapeDtypeStruct((2 * WIDTH, block), F32),
            jax.ShapeDtypeStruct((rows_out + SWEEPS, WIDTH), F32),
        ],
        in_specs=vmem_specs(6),
        out_specs=vmem_specs(2),
        scratch_shapes=[
            pltpu.VMEM((points, 2 * WIDTH), BF),
            pltpu.VMEM((HEADS, 48, points), BF),
            pltpu.VMEM((SWEEPS, points), BF),
            pltpu.VMEM((WIDTH, rows), BF),
            pltpu.VMEM((2 * HEADS, 2 * WIDTH, span), BF),
            pltpu.VMEM((2 * HEADS, 2 * WIDTH, span), BF),
            pltpu.VMEM((points, cols), F32),
            pltpu.VMEM((points, cols), F32),
            pltpu.VMEM((HEADS, points, span), BF),
            pltpu.VMEM((8, span), F32),
            pltpu.VMEM((HEADS, 2 * HEAD_DIM, span), BF),
            pltpu.VMEM((2, 3, lines, 128), F32),
            pltpu.VMEM((2, 3, lines, 128), F32),
            pltpu.VMEM((2, 3, lines, 128), F32),
            pltpu.VMEM((2, nx, 3, lines, 128), F32),
            pltpu.VMEM((2, 3, lines, 128), F32),
            pltpu.VMEM((2, nz, 3, lines, 128), F32),
            pltpu.VMEM((block, 2 * WIDTH), BF),
            pltpu.VMEM((block, 2 * WIDTH), BF),
            pltpu.VMEM((SWEEPS, block), BF),
            pltpu.VMEM((HEADS, block, span), BF),
            pltpu.VMEM((HEADS, block, span), BF),
            pltpu.VMEM((2 * YS, 2 * WIDTH, block), F32),
            pltpu.VMEM((2 * YS, 2 * WIDTH, block), F32),
            pltpu.VMEM((2, 2, 2 * WIDTH, block // 4), F32),
            pltpu.VMEM((2 * WIDTH, block), F32),
            pltpu.VMEM((WIDTH, rows), F32),
            pltpu.VMEM((128, 128), F32),
            pltpu.VMEM((2, chips, rows_out, WIDTH), F32),
            pltpu.VMEM((chips, rows_out, WIDTH), F32),
            pltpu.VMEM((2 * YS, SWEEPS, 128), F32),
            pltpu.VMEM((nx, nz * rows_out + SWEEPS, WIDTH), F32),
            pltpu.VMEM((nx, nz * rows_out + SWEEPS, WIDTH), F32),
            pltpu.VMEM((nz, rows_out, WIDTH), F32),
            pltpu.VMEM((nz, rows_out, WIDTH), F32),
            pltpu.VMEM((SWEEPS, 128), F32),
            pltpu.VMEM((heights, SWEEPS, 128), F32),
            dma((2,)),
            dma((2,)),
            dma((2, nx)),
            dma((2, nx)),
            dma((2, nz)),
            dma((2, nz)),
            dma((2 * YS, 2, 2)),
            dma((2 * YS, 2, 2)),
            dma((2, 2)),
            dma((2, 2)),
            dma((2, 2)),
            dma((2, 2)),
            dma,
            dma,
            dma((2 * YS,)),
            dma((2 * YS,)),
            dma((nx,)),
            dma((nx,)),
            dma((nz,)),
            dma((nz,)),
            dma((heights,)),
            dma((heights,)),
        ],
        compiler_params=pltpu.CompilerParams(
            collective_id=0, has_side_effects=True, vmem_limit_bytes=VMEM_BYTES
        ),
    )(latents, keys, values, sweep, sweep_bias, grad_out)


def deliver_kernel(small_ref, grads_ref, q_out, k_out, v_out, bias_out, square):
    rows_out = q_out.shape[0]
    q_out[...] = small_ref[:rows_out, :]
    k_out[...] = grads_ref[:WIDTH, :].T
    v_out[...] = grads_ref[WIDTH:, :].T
    square[...] = jnp.zeros_like(square)
    square[:SWEEPS, :] = small_ref[rows_out:, :]
    bias_out[...] = square[...].T[:HEADS, :SWEEPS]


def deliver(small, grads):
    block = grads.shape[1]
    return pl.pallas_call(
        deliver_kernel,
        out_shape=[
            jax.ShapeDtypeStruct((small.shape[0] - SWEEPS, WIDTH), F32),
            jax.ShapeDtypeStruct((block, WIDTH), F32),
            jax.ShapeDtypeStruct((block, WIDTH), F32),
            jax.ShapeDtypeStruct((HEADS, SWEEPS), F32),
        ],
        in_specs=vmem_specs(2),
        out_specs=vmem_specs(4),
        scratch_shapes=[pltpu.VMEM((128, 128), F32)],
    )(small, grads)


def per_device(count, lats, latents, keys, values, sweep, sweep_bias, grad_out):
    grads, small = whole(
        latents, keys, values, sweep.reshape(1, -1), sweep_bias, grad_out, count, lats
    )
    return tuple(deliver(small, grads))


def solution(mesh):
    return jax.shard_map(
        functools.partial(per_device, mesh.shape["pts"], mesh.shape["lat"]),
        mesh=mesh,
        in_specs=(P("lat", None), P("pts", None), P("pts", None), P("pts"), P(), P("lat", None)),
        out_specs=(P(("lat", "pts"), None), P(("pts", "lat"), None), P(("pts", "lat"), None), P()),
        check_vma=False,
    )
```

```python
import functools
import math

import jax
import jax.numpy as jnp
from jax import lax
from jax.experimental import pallas as pl
from jax.experimental.pallas import tpu as pltpu
from jax.sharding import PartitionSpec as P

HEADS = 4
HEAD_DIM = 32
WIDTH = HEADS * HEAD_DIM
SWEEPS = 16
SCALE = HEAD_DIM**-0.5
LOG2E = math.log2(math.e)
TO_LOG2 = SCALE * LOG2E
YS = 4
ONES_ROW = 3 * SWEEPS
BF = jnp.bfloat16
F32 = jnp.float32
MESH = pl.DeviceIdType.MESH
VMEM_BYTES = 56 * 1024 * 1024


def dot(a, b):
    return jnp.dot(a, b, preferred_element_type=F32)


def dot_transposed(a, b):
    return lax.dot_general(a, b, (((1,), (1,)), ((), ())), preferred_element_type=F32)


def three_pieces(x):
    hi = x.astype(BF)
    rest = x - hi.astype(F32)
    mid = rest.astype(BF)
    low = (rest - mid.astype(F32)).astype(BF)
    return hi, mid, low


def vmem_specs(count):
    return [pl.BlockSpec(memory_space=pltpu.VMEM)] * count


def whole_kernel(
    count,
    lats,
    latents_ref,
    keys_ref,
    values_ref,
    sweep_ref,
    sweep_bias_ref,
    grad_out_ref,
    grads_ref,
    small_ref,
    k_aux,
    value_rows,
    onehot_t,
    g_t,
    q_feat,
    g_feat,
    scores_0,
    scores_1,
    kept,
    factors,
    g_factored,
    stats,
    from_sibling,
    stats_1,
    stats_x,
    stats_2,
    stats_z,
    k_stage,
    v_stage,
    mark_stage,
    probs,
    scaled,
    part_sum,
    from_ring,
    relay,
    from_z,
    grad_q_t,
    bias_sum,
    q_parts,
    from_core,
    bias_1,
    q_x,
    got_q_x,
    q_z,
    got_q_z,
    bias_2,
    bias_z,
    sent_s1,
    got_s1,
    sent_sx,
    got_sx,
    sent_sz,
    got_sz,
    sent_ring,
    got_ring,
    sent_near,
    got_near,
    sent_far,
    got_far,
    sent_core,
    got_core,
    sent_b1,
    got_b1,
    sent_qx,
    got_qx,
    sent_qz,
    got_qz,
    sent_b2,
    got_b2,
):
    points, latents = keys_ref.shape[0], latents_ref.shape[0]
    span = latents // 2
    cols = min(256, span)
    per_span = span // cols
    tiles = HEADS * 2 * per_span
    pairs = tiles // 2
    chunk = min(512, points)
    chunks = points // chunk
    block = points // (2 * YS)
    half = block // 2
    quarter = block // 4
    chips = count // 2
    nz = 4 if chips % 4 == 0 else chips
    nx = chips // nz
    heights = 2 * nz
    rows_out = latents // count

    me = lax.axis_index("pts")
    lat = lax.axis_index("lat")
    core = lax.rem(me, 2)
    chip = me // 2
    z, y = lat // YS, lax.rem(lat, YS)
    up = z * YS + lax.rem(y + 1, YS)
    down = z * YS + lax.rem(y + YS - 1, YS)
    x, zl = chip // nz, lax.rem(chip, nz)
    height = z * nz + zl

    def x_peer(k):
        return {"pts": (lax.rem(x + k, nx) * nz + zl) * 2 + core}

    def z_peer(k):
        return {"pts": (x * nz + lax.rem(zl + k, nz)) * 2 + core}

    def y_peer(k):
        there = lax.rem(y * 2 + core + k, 2 * YS)
        return {"pts": chip * 2 + lax.rem(there, 2), "lat": z * YS + there // 2}

    def at_height(shift):
        there = lax.rem(height + shift + heights, heights)
        return {"pts": (x * nz + lax.rem(there, nz)) * 2 + core, "lat": (there // nz) * YS + y}

    def remote(src, dst, sent, got, device):
        return pltpu.make_async_remote_copy(
            src_ref=src,
            dst_ref=dst,
            send_sem=sent,
            recv_sem=got,
            device_id=device,
            device_id_type=MESH,
        )

    def every(start, stop, action):
        def step(k, unused):
            action(k)
            return unused

        lax.fori_loop(start, stop, step, 0)

    barrier = pltpu.get_barrier_semaphore()
    greeted = (
        [x_peer(k) for k in range(1, nx)]
        + [at_height(k) for k in range(1, heights)]
        + [y_peer(k) for k in range(1, 2 * YS)]
    )
    for device in greeted:
        pl.semaphore_signal(barrier, inc=1, device_id=device, device_id_type=MESH)

    k_aux[:, :WIDTH] = keys_ref[...]

    def build(c):
        rows = pl.ds(pl.multiple_of(c * chunk, chunk), chunk)
        swept = sweep_ref[:, rows]
        row = lax.broadcasted_iota(jnp.int32, (SWEEPS, chunk), 0)
        marked = jnp.where(row == swept, 1.0, 0.0)
        ones = jnp.where(row < 3, 1.0, 0.0)
        rest = jnp.zeros((WIDTH - 4 * SWEEPS, chunk), F32)
        aux_t = jnp.concatenate([marked, marked, marked, ones, rest], axis=0)
        onehot_t[:, rows] = marked.astype(BF)
        k_aux[rows, WIDTH:] = aux_t.T.astype(BF)
        value_t = values_ref[rows, :].T
        for h in range(HEADS):
            value_rows[h, :HEAD_DIM, rows] = value_t[h * HEAD_DIM : (h + 1) * HEAD_DIM, :]
            value_rows[h, HEAD_DIM:, rows] = jnp.where(row == 0, 1.0, 0.0).astype(BF)

    every(0, chunks, build)
    q_t = latents_ref[...].T
    g_t[...] = grad_out_ref[...].T
    eye = lax.broadcasted_iota(jnp.int32, (SWEEPS, SWEEPS), 0) == lax.broadcasted_iota(
        jnp.int32, (SWEEPS, SWEEPS), 1
    )
    for h in range(HEADS):
        rows = slice(h * HEAD_DIM, (h + 1) * HEAD_DIM)
        column = jnp.sum(
            jnp.where(eye, sweep_bias_ref[h : h + 1, :], 0.0), axis=1, keepdims=True
        ) * (1.0 / SCALE)
        bias_pieces = three_pieces(jnp.broadcast_to(column, (SWEEPS, span)))
        for s in range(2):
            n = s * HEADS + h
            here = slice(s * span, (s + 1) * span)
            q_feat[n] = jnp.zeros((2 * WIDTH, span), BF)
            g_feat[n] = jnp.zeros((2 * WIDTH, span), BF)
            q_feat[n, rows, :] = q_t[rows, here]
            g_feat[n, rows, :] = g_t[rows, here]
            for index, piece in enumerate(bias_pieces):
                q_feat[n, WIDTH + index * SWEEPS : WIDTH + (index + 1) * SWEEPS, :] = piece
    grad_q_t[...] = jnp.zeros_like(grad_q_t)
    bias_sum[...] = jnp.zeros_like(bias_sum)

    def merge(parts):
        best = functools.reduce(jnp.maximum, [part[0] for part in parts])
        weights = [jnp.exp2(part[0] - best) for part in parts]
        sums = [sum(w * part[kind] for w, part in zip(weights, parts)) for kind in (1, 2)]
        return [best] + sums

    def keep(ref, merged):
        for kind, value in enumerate(merged):
            ref[kind] = value

    def to_sibling(s):
        return remote(
            stats.at[s], from_sibling.at[s], sent_s1.at[s], got_s1.at[s], {"pts": me + 1 - 2 * core}
        )

    def along_x(s, k):
        return remote(
            stats_1.at[s], stats_x.at[s, x], sent_sx.at[s, k], got_sx.at[s, k], x_peer(k)
        )

    def along_z(s, k):
        return remote(
            stats_2.at[s], stats_z.at[s, zl], sent_sz.at[s, k], got_sz.at[s, k], z_peer(k)
        )

    def exchange_x(s):
        to_sibling(s).wait_recv()
        merged = merge([stats[s], from_sibling[s]])
        keep(stats_1.at[s], merged)
        for k in range(1, nx):
            along_x(s, k).start()
        keep(stats_x.at[s, x], merged)

    def exchange_z(s):
        for k in range(1, nx):
            along_x(s, k).wait_recv()
        merged = merge([stats_x[s, i] for i in range(nx)])
        keep(stats_2.at[s], merged)
        for k in range(1, nz):
            along_z(s, k).start()
        keep(stats_z.at[s, zl], merged)

    def take_results(s):
        for k in range(1, nz):
            along_z(s, k).wait_recv()
        best, total, weighted = merge([stats_z[s, i] for i in range(nz)])
        if s == 0:
            first = (best + jnp.log(total) * LOG2E) * (-1.0 / TO_LOG2)
        else:
            first = jnp.exp2(stats[s, 0] - best) / total
        delta = -(weighted / total)
        row16 = lax.broadcasted_iota(jnp.int32, (16, 128), 0)
        per_tile = cols // 128
        for n in range(tiles // 2):
            it, h = n // HEADS, n % HEADS
            for part in range(per_tile):
                line = n * per_tile + part
                left = it * cols + part * 128
                if s == 1:
                    factors[h : h + 1, left : left + 128] = first[line : line + 1, :]
                for value, feat in ((first, q_feat), (delta, g_feat))[s:]:
                    hi, mid, low = three_pieces(value[line : line + 1, :])
                    feat[
                        s * HEADS + h,
                        WIDTH + ONES_ROW : WIDTH + ONES_ROW + 16,
                        left : left + 128,
                    ] = jnp.where(
                        row16 == 0,
                        hi.astype(F32),
                        jnp.where(
                            row16 == 1, mid.astype(F32), jnp.where(row16 == 2, low.astype(F32), 0.0)
                        ),
                    ).astype(BF)

        if s == 1:
            for h in range(HEADS):
                rows = slice(h * HEAD_DIM, (h + 1) * HEAD_DIM)
                product = g_t[rows, span:].astype(F32) * factors[h : h + 1, :]
                hi, mid, _ = three_pieces(product)
                g_factored[h, :HEAD_DIM, :] = hi
                g_factored[h, HEAD_DIM:, :] = mid

    lowest = jnp.full((32, cols), -jnp.inf, F32)

    def feature_of(n):
        it = n // HEADS
        return (
            (it // per_span) * HEADS + lax.rem(n, HEADS),
            pl.ds(pl.multiple_of(lax.rem(it, per_span) * cols, cols), cols),
        )

    def score_chunk(n, into, c, top):
        index, lanes = feature_of(n)
        rows = pl.ds(c * chunk, chunk)
        s = dot(k_aux[rows, :], q_feat[index, :, lanes]) * TO_LOG2
        into[rows, :] = s
        return jnp.maximum(top, jnp.max(s.reshape(chunk // 32, 32, cols), axis=0))

    def tile_sums(keep_e, n, scores, top_rows, following, into):
        top = jnp.max(top_rows, axis=0, keepdims=True)
        head = lax.rem(n, HEADS)
        next_top = lowest
        unused_index, lanes = feature_of(n)
        out = jnp.zeros((48, cols), F32)
        for c in range(chunks):
            rows = pl.ds(c * chunk, chunk)
            e = jnp.exp2(scores[rows, :] - top).astype(BF)
            if keep_e:
                kept[head, rows, lanes] = e
            out = out + dot(value_rows[head, :, rows], e)
            next_top = score_chunk(following, into, c, next_top)
        g = g_t[
            pl.ds(pl.multiple_of(head * HEAD_DIM, HEAD_DIM), HEAD_DIM),
            pl.ds(pl.multiple_of((n // HEADS) * cols, cols), cols),
        ].astype(F32)
        weighted = jnp.sum(out[:HEAD_DIM] * g, axis=0, keepdims=True)
        total = out[HEAD_DIM : HEAD_DIM + 1]
        per_tile = cols // 128
        for kind, value in enumerate((top, total, weighted)):
            for part in range(per_tile):
                line = lax.rem(n, tiles // 2) * per_tile + part
                stats[n // (tiles // 2), kind, pl.ds(line, 1), :] = value[
                    :, part * 128 : (part + 1) * 128
                ]
        return next_top

    first_top = lowest
    for c in range(chunks):
        first_top = score_chunk(0, scores_0, c, first_top)

    def per_pair(keep_e, pair, top_rows):
        n = pair * 2
        top_rows = tile_sums(keep_e, n, scores_0, top_rows, n + 1, scores_1)
        top_rows = tile_sums(
            keep_e, n + 1, scores_1, top_rows, lax.rem(n + 2, tiles), scores_0
        )

        @pl.when(pair == pairs // 2 - 1)
        def _():
            pl.semaphore_wait(barrier, len(greeted))
            to_sibling(0).start()

        @pl.when(pair == pairs // 2)
        def _():
            exchange_x(0)

        @pl.when(pair == pairs // 2 + 1)
        def _():
            exchange_z(0)

        return top_rows

    first_top = lax.fori_loop(0, pairs // 2, functools.partial(per_pair, False), first_top)
    lax.fori_loop(pairs // 2, pairs, functools.partial(per_pair, True), first_top)
    to_sibling(1).start()
    take_results(0)
    exchange_x(1)

    lane_row = lax.broadcasted_iota(jnp.int32, (block, 128), 1)

    def compute(step, s):
        turn = lax.rem(step, YS)
        owner_z = jnp.where(step < YS, 1 - z, z)
        at_up = (owner_z * YS + lax.rem(y + 2 * YS - 1 - turn, YS)) * block
        at_down = (owner_z * YS + lax.rem(y + 1 + turn, YS)) * block + half
        places = []
        for row, at in ((0, at_up), (half, at_down)):
            source = pl.ds(pl.multiple_of(at, half), half)
            rows = pl.ds(row, half)
            if s == 0:
                k_stage[rows, :] = k_aux[source, :]
            else:
                k_stage[rows, :WIDTH] = keys_ref[source, :]
            v_stage[rows, :WIDTH] = values_ref[source, :]
            v_stage[rows, WIDTH:] = k_aux[source, WIDTH:]
            mark_stage[:, row : row + half] = onehot_t[:, source]
            places.append((slice(row, row + half), source))
        k_t = k_stage[:, :WIDTH].T
        row_sums = jnp.zeros((block, 128), F32)
        lanes = slice(s * span, (s + 1) * span)
        for h in range(HEADS):
            n = s * HEADS + h
            rows = slice(h * HEAD_DIM, (h + 1) * HEAD_DIM)
            rows_v = slice(WIDTH + h * HEAD_DIM, WIDTH + (h + 1) * HEAD_DIM)
            out_prod = dot(v_stage[...], g_feat[n])
            if s == 0:
                p = jnp.exp2(dot(k_stage[...], q_feat[n]) * TO_LOG2)
                low = (p * out_prod) * SCALE
                probs[h] = p.astype(BF)
                part_sum[step, rows_v, :] = dot_transposed(g_feat[n, rows, :], probs[h])
            else:
                out_prod = out_prod * (factors[h : h + 1, :] * SCALE)
                low = jnp.concatenate(
                    [
                        kept[h, source, :].astype(F32) * out_prod[place]
                        for place, source in places
                    ],
                    axis=0,
                )
                for place, source in places:
                    both = dot_transposed(g_factored[h], kept[h, source, :])
                    part_sum[step, rows_v, place] += both[:HEAD_DIM] + both[HEAD_DIM:]
            scaled[h] = low.astype(BF)
            folded = low[:, :128]
            for part in range(1, span // 128):
                folded = folded + low[:, part * 128 : (part + 1) * 128]
            row_sums = row_sums + jnp.where(
                lane_row == h, jnp.sum(folded, axis=1, keepdims=True), 0.0
            )
            grad_k = dot_transposed(q_feat[n, rows, :], scaled[h])
            if s == 0:
                part_sum[step, rows, :] = grad_k
            else:
                part_sum[step, rows, :] += grad_k
            grad_q_t[rows, lanes] += dot(k_t[rows, :], scaled[h])
        for piece in three_pieces(row_sums * (1.0 / SCALE)):
            bias_sum[:SWEEPS, :] += dot(mark_stage[...], piece)

    def lanes_of(part, way):
        return pl.ds(pl.multiple_of(way * half + part * quarter, quarter), quarter)

    def ring(step, part, way):
        here = lanes_of(part, way)
        return remote(
            part_sum.at[step, :, here],
            from_ring.at[step, :, here],
            sent_ring.at[step, part, way],
            got_ring.at[step, part, way],
            {"lat": down if way else up},
        )

    def near(part, way):
        return remote(
            part_sum.at[YS - 1, :, lanes_of(part, way)],
            relay.at[part, way],
            sent_near.at[part, way],
            got_near.at[part, way],
            at_height(-1 if way else 1),
        )

    def far(part, way):
        return remote(
            relay.at[part, way],
            from_z.at[:, lanes_of(part, way)],
            sent_far.at[part, way],
            got_far.at[part, way],
            at_height(1 - nz if way else nz - 1),
        )

    def finish(step, part):
        turn = lax.rem(step, YS)

        @pl.when(turn > 0)
        def _():
            for way in range(2):
                ring(step - 1, part, way).wait_recv()
                here = lanes_of(part, way)
                part_sum[step, :, here] += from_ring[step - 1, :, here]

        @pl.when(turn < YS - 1)
        def _():
            for way in range(2):
                ring(step, part, way).start()

        @pl.when(step == YS - 1)
        def _():
            for way in range(2):
                near(part, way).start()

    def per_item(t, unused):
        swapped = (t == 1) | (t == 2)
        step = jnp.where(swapped, 2 - t, t // 2)
        s = jnp.where(swapped, t - 1, lax.rem(t, 2))

        @pl.when(t == 2)
        def _():
            take_results(1)

        for index in range(2):
            pl.when(s == index)(functools.partial(compute, step, index))

        @pl.when(t == 0)
        def _():
            exchange_z(1)

        @pl.when((t >= 2) & (t != 10))
        def _():
            finish(
                jnp.where(t < 10, (t - 2) // 2, (t - 1) // 2),
                jnp.where(t < 10, lax.rem(t, 2), lax.rem(t + 1, 2)),
            )

        @pl.when((t == 9) | (t == 10))
        def _():
            finish(YS, t - 9)

        for part in range(2):

            @pl.when(t == 10 + part)
            def _():
                for way in range(2):
                    near(part, way).wait_recv()
                    far(part, way).start()

        return unused

    lax.fori_loop(0, 4 * YS, per_item, 0)

    swap = remote(q_parts.at[1 - core], from_core, sent_core, got_core, {"pts": me + 1 - 2 * core})

    def bias_y(k):
        return remote(
            bias_sum.at[pl.ds(0, SWEEPS)],
            bias_1.at[y * 2 + core],
            sent_b1.at[k],
            got_b1.at[k],
            y_peer(k),
        )

    def q_along_x(k):
        return remote(
            q_x.at[lax.rem(x + k, nx)], got_q_x.at[x], sent_qx.at[k], got_qx.at[k], x_peer(k)
        )

    def q_along_z(k):
        return remote(
            q_z.at[lax.rem(zl + k, nz)], got_q_z.at[zl], sent_qz.at[k], got_qz.at[k], z_peer(k)
        )

    def bias_along_z(k):
        return remote(bias_2, bias_z.at[height], sent_b2.at[k], got_b2.at[k], at_height(k))

    bias_copies = [bias_y(k) for k in range(1, 2 * YS)]
    x_copies = [q_along_x(k) for k in range(1, nx)]
    z_copies = [q_along_z(k) for k in range(1, nz)]
    bias_z_copies = [bias_along_z(k) for k in range(1, heights)]

    for copy in bias_copies:
        copy.start()
    grad_q = grad_q_t[...].T
    for p in range(count):
        q_parts[p % 2, p // 2] = grad_q[p * rows_out : (p + 1) * rows_out]
    swap.start()
    bias_1[y * 2 + core] = bias_sum[:SWEEPS, :]
    for copy in bias_copies:
        copy.wait_recv()
    bias = jnp.sum(bias_1[...], axis=0)
    swap.wait_recv()
    for i in range(nx):
        for j in range(nz):
            q_x[i, j * rows_out : (j + 1) * rows_out, :] = (
                q_parts[core, i * nz + j] + from_core[i * nz + j]
            )
        q_x[i, nz * rows_out :, :] = bias
    for copy in x_copies:
        copy.start()
    got_q_x[x] = q_x[x]
    finish(2 * YS - 1, 1)
    for s in range(2):
        to_sibling(s).wait_send()
        for k in range(1, nx):
            along_x(s, k).wait_send()
        for k in range(1, nz):
            along_z(s, k).wait_send()
    for part in range(2):
        for way in range(2):
            for step in range(2 * YS):
                if step % YS < YS - 1:
                    ring(step, part, way).wait_send()
            near(part, way).wait_send()
    for copy in x_copies:
        copy.wait_recv()
    summed = jnp.sum(got_q_x[...], axis=0)
    bias_2[...] = summed[nz * rows_out :]
    for j in range(nz):
        q_z[j] = summed[j * rows_out : (j + 1) * rows_out]
    for copy in bias_z_copies + z_copies:
        copy.start()
    got_q_z[zl] = q_z[zl]
    bias_z[height] = bias_2[...]
    swap.wait_send()
    for copy in bias_copies + x_copies:
        copy.wait_send()
    for part in range(2):
        for way in range(2):
            far(part, way).wait_send()
            far(part, way).wait_recv()
    grads_ref[...] = part_sum[2 * YS - 1] + from_z[...]
    for copy in bias_z_copies + z_copies:
        copy.wait_recv()
    small_ref[:rows_out, :] = jnp.sum(got_q_z[...], axis=0)
    small_ref[rows_out:, :] = jnp.sum(bias_z[...], axis=0)

    for copy in z_copies + bias_z_copies:
        copy.wait_send()


def whole(latents, keys, values, sweep, sweep_bias, grad_out, count, lats):
    rows, points = latents.shape[0], keys.shape[0]
    block, span, chips = points // (2 * YS), rows // 2, count // 2
    cols = min(256, span)
    lines = HEADS * rows // 256
    nz = 4 if chips % 4 == 0 else chips
    nx = chips // nz
    heights = 2 * nz
    rows_out = rows // count
    dma = pltpu.SemaphoreType.DMA
    return pl.pallas_call(
        functools.partial(whole_kernel, count, lats),
        out_shape=[
            jax.ShapeDtypeStruct((2 * WIDTH, block), F32),
            jax.ShapeDtypeStruct((rows_out + SWEEPS, WIDTH), F32),
        ],
        in_specs=vmem_specs(6),
        out_specs=vmem_specs(2),
        scratch_shapes=[
            pltpu.VMEM((points, 2 * WIDTH), BF),
            pltpu.VMEM((HEADS, 48, points), BF),
            pltpu.VMEM((SWEEPS, points), BF),
            pltpu.VMEM((WIDTH, rows), BF),
            pltpu.VMEM((2 * HEADS, 2 * WIDTH, span), BF),
            pltpu.VMEM((2 * HEADS, 2 * WIDTH, span), BF),
            pltpu.VMEM((points, cols), F32),
            pltpu.VMEM((points, cols), F32),
            pltpu.VMEM((HEADS, points, span), BF),
            pltpu.VMEM((8, span), F32),
            pltpu.VMEM((HEADS, 2 * HEAD_DIM, span), BF),
            pltpu.VMEM((2, 3, lines, 128), F32),
            pltpu.VMEM((2, 3, lines, 128), F32),
            pltpu.VMEM((2, 3, lines, 128), F32),
            pltpu.VMEM((2, nx, 3, lines, 128), F32),
            pltpu.VMEM((2, 3, lines, 128), F32),
            pltpu.VMEM((2, nz, 3, lines, 128), F32),
            pltpu.VMEM((block, 2 * WIDTH), BF),
            pltpu.VMEM((block, 2 * WIDTH), BF),
            pltpu.VMEM((SWEEPS, block), BF),
            pltpu.VMEM((HEADS, block, span), BF),
            pltpu.VMEM((HEADS, block, span), BF),
            pltpu.VMEM((2 * YS, 2 * WIDTH, block), F32),
            pltpu.VMEM((2 * YS, 2 * WIDTH, block), F32),
            pltpu.VMEM((2, 2, 2 * WIDTH, block // 4), F32),
            pltpu.VMEM((2 * WIDTH, block), F32),
            pltpu.VMEM((WIDTH, rows), F32),
            pltpu.VMEM((128, 128), F32),
            pltpu.VMEM((2, chips, rows_out, WIDTH), F32),
            pltpu.VMEM((chips, rows_out, WIDTH), F32),
            pltpu.VMEM((2 * YS, SWEEPS, 128), F32),
            pltpu.VMEM((nx, nz * rows_out + SWEEPS, WIDTH), F32),
            pltpu.VMEM((nx, nz * rows_out + SWEEPS, WIDTH), F32),
            pltpu.VMEM((nz, rows_out, WIDTH), F32),
            pltpu.VMEM((nz, rows_out, WIDTH), F32),
            pltpu.VMEM((SWEEPS, 128), F32),
            pltpu.VMEM((heights, SWEEPS, 128), F32),
            dma((2,)),
            dma((2,)),
            dma((2, nx)),
            dma((2, nx)),
            dma((2, nz)),
            dma((2, nz)),
            dma((2 * YS, 2, 2)),
            dma((2 * YS, 2, 2)),
            dma((2, 2)),
            dma((2, 2)),
            dma((2, 2)),
            dma((2, 2)),
            dma,
            dma,
            dma((2 * YS,)),
            dma((2 * YS,)),
            dma((nx,)),
            dma((nx,)),
            dma((nz,)),
            dma((nz,)),
            dma((heights,)),
            dma((heights,)),
        ],
        compiler_params=pltpu.CompilerParams(
            collective_id=0, has_side_effects=True, vmem_limit_bytes=VMEM_BYTES
        ),
    )(latents, keys, values, sweep, sweep_bias, grad_out)


def deliver_kernel(small_ref, grads_ref, q_out, k_out, v_out, bias_out, square):
    rows_out = q_out.shape[0]
    q_out[...] = small_ref[:rows_out, :]
    k_out[...] = grads_ref[:WIDTH, :].T
    v_out[...] = grads_ref[WIDTH:, :].T
    square[...] = jnp.zeros_like(square)
    square[:SWEEPS, :] = small_ref[rows_out:, :]
    bias_out[...] = square[...].T[:HEADS, :SWEEPS]


def deliver(small, grads):
    block = grads.shape[1]
    return pl.pallas_call(
        deliver_kernel,
        out_shape=[
            jax.ShapeDtypeStruct((small.shape[0] - SWEEPS, WIDTH), F32),
            jax.ShapeDtypeStruct((block, WIDTH), F32),
            jax.ShapeDtypeStruct((block, WIDTH), F32),
            jax.ShapeDtypeStruct((HEADS, SWEEPS), F32),
        ],
        in_specs=vmem_specs(2),
        out_specs=vmem_specs(4),
        scratch_shapes=[pltpu.VMEM((128, 128), F32)],
    )(small, grads)


def per_device(count, lats, latents, keys, values, sweep, sweep_bias, grad_out):
    grads, small = whole(
        latents, keys, values, sweep.reshape(1, -1), sweep_bias, grad_out, count, lats
    )
    return tuple(deliver(small, grads))


def solution(mesh):
    return jax.shard_map(
        functools.partial(per_device, mesh.shape["pts"], mesh.shape["lat"]),
        mesh=mesh,
        in_specs=(P("lat", None), P("pts", None), P("pts", None), P("pts"), P(), P("lat", None)),
        out_specs=(P(("lat", "pts"), None), P(("pts", "lat"), None), P(("pts", "lat"), None), P()),
        check_vma=False,
    )
```

```python
import functools
import math

import jax
import jax.numpy as jnp
from jax import lax
from jax.experimental import pallas as pl
from jax.experimental.pallas import tpu as pltpu
from jax.sharding import PartitionSpec as P

HEADS = 4
HEAD_DIM = 32
WIDTH = HEADS * HEAD_DIM
SWEEPS = 16
SCALE = HEAD_DIM**-0.5
LOG2E = math.log2(math.e)
TO_LOG2 = SCALE * LOG2E
YS = 4
ONES_ROW = 3 * SWEEPS
BF = jnp.bfloat16
F32 = jnp.float32
MESH = pl.DeviceIdType.MESH
VMEM_BYTES = 56 * 1024 * 1024


def dot(a, b):
    return jnp.dot(a, b, preferred_element_type=F32)


def dot_transposed(a, b):
    return lax.dot_general(a, b, (((1,), (1,)), ((), ())), preferred_element_type=F32)


def three_pieces(x):
    hi = x.astype(BF)
    rest = x - hi.astype(F32)
    mid = rest.astype(BF)
    low = (rest - mid.astype(F32)).astype(BF)
    return hi, mid, low


def vmem_specs(count):
    return [pl.BlockSpec(memory_space=pltpu.VMEM)] * count


def whole_kernel(
    count,
    lats,
    latents_ref,
    keys_ref,
    values_ref,
    sweep_ref,
    sweep_bias_ref,
    grad_out_ref,
    grads_ref,
    small_ref,
    k_aux,
    value_rows,
    onehot_t,
    g_t,
    q_feat,
    g_feat,
    scores_0,
    scores_1,
    kept,
    factors,
    g_factored,
    stats,
    from_sibling,
    stats_1,
    stats_x,
    stats_2,
    stats_z,
    k_stage,
    v_stage,
    mark_stage,
    probs,
    scaled,
    part_sum,
    from_ring,
    relay,
    from_z,
    grad_q_t,
    bias_sum,
    q_parts,
    from_core,
    bias_1,
    q_x,
    got_q_x,
    q_z,
    got_q_z,
    bias_2,
    bias_z,
    sent_s1,
    got_s1,
    sent_sx,
    got_sx,
    sent_sz,
    got_sz,
    sent_ring,
    got_ring,
    sent_near,
    got_near,
    sent_far,
    got_far,
    sent_core,
    got_core,
    sent_b1,
    got_b1,
    sent_qx,
    got_qx,
    sent_qz,
    got_qz,
    sent_b2,
    got_b2,
):
    points, latents = keys_ref.shape[0], latents_ref.shape[0]
    span = latents // 2
    cols = min(256, span)
    per_span = span // cols
    tiles = HEADS * 2 * per_span
    pairs = tiles // 2
    chunk = min(1024, points)
    chunks = points // chunk
    block = points // (2 * YS)
    half = block // 2
    quarter = block // 4
    chips = count // 2
    nz = 4 if chips % 4 == 0 else chips
    nx = chips // nz
    heights = 2 * nz
    rows_out = latents // count

    me = lax.axis_index("pts")
    lat = lax.axis_index("lat")
    core = lax.rem(me, 2)
    chip = me // 2
    z, y = lat // YS, lax.rem(lat, YS)
    up = z * YS + lax.rem(y + 1, YS)
    down = z * YS + lax.rem(y + YS - 1, YS)
    x, zl = chip // nz, lax.rem(chip, nz)
    height = z * nz + zl

    def x_peer(k):
        return {"pts": (lax.rem(x + k, nx) * nz + zl) * 2 + core}

    def z_peer(k):
        return {"pts": (x * nz + lax.rem(zl + k, nz)) * 2 + core}

    def y_peer(k):
        there = lax.rem(y * 2 + core + k, 2 * YS)
        return {"pts": chip * 2 + lax.rem(there, 2), "lat": z * YS + there // 2}

    def at_height(shift):
        there = lax.rem(height + shift + heights, heights)
        return {"pts": (x * nz + lax.rem(there, nz)) * 2 + core, "lat": (there // nz) * YS + y}

    def remote(src, dst, sent, got, device):
        return pltpu.make_async_remote_copy(
            src_ref=src,
            dst_ref=dst,
            send_sem=sent,
            recv_sem=got,
            device_id=device,
            device_id_type=MESH,
        )

    def every(start, stop, action):
        def step(k, unused):
            action(k)
            return unused

        lax.fori_loop(start, stop, step, 0)

    barrier = pltpu.get_barrier_semaphore()
    greeted = (
        [x_peer(k) for k in range(1, nx)]
        + [at_height(k) for k in range(1, heights)]
        + [y_peer(k) for k in range(1, 2 * YS)]
    )
    for device in greeted:
        pl.semaphore_signal(barrier, inc=1, device_id=device, device_id_type=MESH)

    k_aux[:, :WIDTH] = keys_ref[...]

    def build(c):
        rows = pl.ds(pl.multiple_of(c * chunk, chunk), chunk)
        swept = sweep_ref[:, rows]
        row = lax.broadcasted_iota(jnp.int32, (SWEEPS, chunk), 0)
        marked = jnp.where(row == swept, 1.0, 0.0)
        ones = jnp.where(row < 3, 1.0, 0.0)
        rest = jnp.zeros((WIDTH - 4 * SWEEPS, chunk), F32)
        aux_t = jnp.concatenate([marked, marked, marked, ones, rest], axis=0)
        onehot_t[:, rows] = marked.astype(BF)
        k_aux[rows, WIDTH:] = aux_t.T.astype(BF)
        value_t = values_ref[rows, :].T
        for h in range(HEADS):
            value_rows[h, :HEAD_DIM, rows] = value_t[h * HEAD_DIM : (h + 1) * HEAD_DIM, :]
            value_rows[h, HEAD_DIM:, rows] = jnp.where(row == 0, 1.0, 0.0).astype(BF)

    every(0, chunks, build)
    q_t = latents_ref[...].T
    g_t[...] = grad_out_ref[...].T
    eye = lax.broadcasted_iota(jnp.int32, (SWEEPS, SWEEPS), 0) == lax.broadcasted_iota(
        jnp.int32, (SWEEPS, SWEEPS), 1
    )
    for h in range(HEADS):
        rows = slice(h * HEAD_DIM, (h + 1) * HEAD_DIM)
        column = jnp.sum(
            jnp.where(eye, sweep_bias_ref[h : h + 1, :], 0.0), axis=1, keepdims=True
        ) * (1.0 / SCALE)
        bias_pieces = three_pieces(jnp.broadcast_to(column, (SWEEPS, span)))
        for s in range(2):
            n = s * HEADS + h
            here = slice(s * span, (s + 1) * span)
            q_feat[n] = jnp.zeros((2 * WIDTH, span), BF)
            g_feat[n] = jnp.zeros((2 * WIDTH, span), BF)
            q_feat[n, rows, :] = q_t[rows, here]
            g_feat[n, rows, :] = g_t[rows, here]
            for index, piece in enumerate(bias_pieces):
                q_feat[n, WIDTH + index * SWEEPS : WIDTH + (index + 1) * SWEEPS, :] = piece
    grad_q_t[...] = jnp.zeros_like(grad_q_t)
    bias_sum[...] = jnp.zeros_like(bias_sum)

    def merge(parts):
        best = functools.reduce(jnp.maximum, [part[0] for part in parts])
        weights = [jnp.exp2(part[0] - best) for part in parts]
        sums = [sum(w * part[kind] for w, part in zip(weights, parts)) for kind in (1, 2)]
        return [best] + sums

    def keep(ref, merged):
        for kind, value in enumerate(merged):
            ref[kind] = value

    def to_sibling(s):
        return remote(
            stats.at[s], from_sibling.at[s], sent_s1.at[s], got_s1.at[s], {"pts": me + 1 - 2 * core}
        )

    def along_x(s, k):
        return remote(
            stats_1.at[s], stats_x.at[s, x], sent_sx.at[s, k], got_sx.at[s, k], x_peer(k)
        )

    def along_z(s, k):
        return remote(
            stats_2.at[s], stats_z.at[s, zl], sent_sz.at[s, k], got_sz.at[s, k], z_peer(k)
        )

    def exchange_x(s):
        to_sibling(s).wait_recv()
        merged = merge([stats[s], from_sibling[s]])
        keep(stats_1.at[s], merged)
        for k in range(1, nx):
            along_x(s, k).start()
        keep(stats_x.at[s, x], merged)

    def exchange_z(s):
        for k in range(1, nx):
            along_x(s, k).wait_recv()
        merged = merge([stats_x[s, i] for i in range(nx)])
        keep(stats_2.at[s], merged)
        for k in range(1, nz):
            along_z(s, k).start()
        keep(stats_z.at[s, zl], merged)

    def take_results(s):
        for k in range(1, nz):
            along_z(s, k).wait_recv()
        best, total, weighted = merge([stats_z[s, i] for i in range(nz)])
        if s == 0:
            first = (best + jnp.log(total) * LOG2E) * (-1.0 / TO_LOG2)
        else:
            first = jnp.exp2(stats[s, 0] - best) / total
        delta = -(weighted / total)
        row16 = lax.broadcasted_iota(jnp.int32, (16, 128), 0)
        per_tile = cols // 128
        for n in range(tiles // 2):
            it, h = n // HEADS, n % HEADS
            for part in range(per_tile):
                line = n * per_tile + part
                left = it * cols + part * 128
                if s == 1:
                    factors[h : h + 1, left : left + 128] = first[line : line + 1, :]
                for value, feat in ((first, q_feat), (delta, g_feat))[s:]:
                    hi, mid, low = three_pieces(value[line : line + 1, :])
                    feat[
                        s * HEADS + h,
                        WIDTH + ONES_ROW : WIDTH + ONES_ROW + 16,
                        left : left + 128,
                    ] = jnp.where(
                        row16 == 0,
                        hi.astype(F32),
                        jnp.where(
                            row16 == 1, mid.astype(F32), jnp.where(row16 == 2, low.astype(F32), 0.0)
                        ),
                    ).astype(BF)

        if s == 1:
            for h in range(HEADS):
                rows = slice(h * HEAD_DIM, (h + 1) * HEAD_DIM)
                product = g_t[rows, span:].astype(F32) * factors[h : h + 1, :]
                hi, mid, _ = three_pieces(product)
                g_factored[h, :HEAD_DIM, :] = hi
                g_factored[h, HEAD_DIM:, :] = mid

    lowest = jnp.full((32, cols), -jnp.inf, F32)

    def feature_of(n):
        it = n // HEADS
        return (
            (it // per_span) * HEADS + lax.rem(n, HEADS),
            pl.ds(pl.multiple_of(lax.rem(it, per_span) * cols, cols), cols),
        )

    def score_chunk(n, into, c, top):
        index, lanes = feature_of(n)
        rows = pl.ds(c * chunk, chunk)
        s = dot(k_aux[rows, :], q_feat[index, :, lanes])
        into[rows, :] = s
        return jnp.maximum(top, jnp.max(s.reshape(chunk // 32, 32, cols), axis=0))

    def tile_sums(keep_e, n, scores, top_rows, following, into):
        top = jnp.max(top_rows, axis=0, keepdims=True)
        head = lax.rem(n, HEADS)
        next_top = lowest
        unused_index, lanes = feature_of(n)
        out = jnp.zeros((48, cols), F32)
        for c in range(chunks):
            rows = pl.ds(c * chunk, chunk)
            next_top = score_chunk(following, into, c, next_top)
            e = jnp.exp2((scores[rows, :] - top) * TO_LOG2).astype(BF)
            if keep_e:
                kept[head, rows, lanes] = e
            out = out + dot(value_rows[head, :, rows], e)
        g = g_t[
            pl.ds(pl.multiple_of(head * HEAD_DIM, HEAD_DIM), HEAD_DIM),
            pl.ds(pl.multiple_of((n // HEADS) * cols, cols), cols),
        ].astype(F32)
        weighted = jnp.sum(out[:HEAD_DIM] * g, axis=0, keepdims=True)
        total = out[HEAD_DIM : HEAD_DIM + 1]
        per_tile = cols // 128
        for kind, value in enumerate((top * TO_LOG2, total, weighted)):
            for part in range(per_tile):
                line = lax.rem(n, tiles // 2) * per_tile + part
                stats[n // (tiles // 2), kind, pl.ds(line, 1), :] = value[
                    :, part * 128 : (part + 1) * 128
                ]
        return next_top

    first_top = lowest
    for c in range(chunks):
        first_top = score_chunk(0, scores_0, c, first_top)

    def per_pair(keep_e, pair, top_rows):
        n = pair * 2
        top_rows = tile_sums(keep_e, n, scores_0, top_rows, n + 1, scores_1)
        top_rows = tile_sums(
            keep_e, n + 1, scores_1, top_rows, lax.rem(n + 2, tiles), scores_0
        )

        @pl.when(pair == pairs // 2 - 1)
        def _():
            pl.semaphore_wait(barrier, len(greeted))
            to_sibling(0).start()

        @pl.when(pair == pairs // 2)
        def _():
            exchange_x(0)

        @pl.when(pair == pairs // 2 + 1)
        def _():
            exchange_z(0)

        return top_rows

    first_top = lax.fori_loop(0, pairs // 2, functools.partial(per_pair, False), first_top)
    lax.fori_loop(pairs // 2, pairs, functools.partial(per_pair, True), first_top)
    to_sibling(1).start()
    take_results(0)
    exchange_x(1)

    lane_row = lax.broadcasted_iota(jnp.int32, (block, 128), 1)

    def compute(step, s):
        turn = lax.rem(step, YS)
        owner_z = jnp.where(step < YS, 1 - z, z)
        at_up = (owner_z * YS + lax.rem(y + 2 * YS - 1 - turn, YS)) * block
        at_down = (owner_z * YS + lax.rem(y + 1 + turn, YS)) * block + half
        places = []
        for row, at in ((0, at_up), (half, at_down)):
            source = pl.ds(pl.multiple_of(at, half), half)
            rows = pl.ds(row, half)
            if s == 0:
                k_stage[rows, :] = k_aux[source, :]
            else:
                k_stage[rows, :WIDTH] = keys_ref[source, :]
            v_stage[rows, :WIDTH] = values_ref[source, :]
            v_stage[rows, WIDTH:] = k_aux[source, WIDTH:]
            mark_stage[:, row : row + half] = onehot_t[:, source]
            places.append((slice(row, row + half), source))
        k_t = k_stage[:, :WIDTH].T
        row_sums = jnp.zeros((block, 128), F32)
        lanes = slice(s * span, (s + 1) * span)
        for h in range(HEADS):
            n = s * HEADS + h
            rows = slice(h * HEAD_DIM, (h + 1) * HEAD_DIM)
            rows_v = slice(WIDTH + h * HEAD_DIM, WIDTH + (h + 1) * HEAD_DIM)
            out_prod = dot(v_stage[...], g_feat[n])
            if s == 0:
                p = jnp.exp2(dot(k_stage[...], q_feat[n]) * TO_LOG2)
                low = (p * out_prod) * SCALE
                probs[h] = p.astype(BF)
                part_sum[step, rows_v, :] = dot_transposed(g_feat[n, rows, :], probs[h])
            else:
                out_prod = out_prod * (factors[h : h + 1, :] * SCALE)
                low = jnp.concatenate(
                    [
                        kept[h, source, :].astype(F32) * out_prod[place]
                        for place, source in places
                    ],
                    axis=0,
                )
                for place, source in places:
                    both = dot_transposed(g_factored[h], kept[h, source, :])
                    part_sum[step, rows_v, place] += both[:HEAD_DIM] + both[HEAD_DIM:]
            scaled[h] = low.astype(BF)
            folded = low[:, :128]
            for part in range(1, span // 128):
                folded = folded + low[:, part * 128 : (part + 1) * 128]
            row_sums = row_sums + jnp.where(
                lane_row == h, jnp.sum(folded, axis=1, keepdims=True), 0.0
            )
            grad_k = dot_transposed(q_feat[n, rows, :], scaled[h])
            if s == 0:
                part_sum[step, rows, :] = grad_k
            else:
                part_sum[step, rows, :] += grad_k
            grad_q_t[rows, lanes] += dot(k_t[rows, :], scaled[h])
        for piece in three_pieces(row_sums * (1.0 / SCALE)):
            bias_sum[:SWEEPS, :] += dot(mark_stage[...], piece)

    def lanes_of(part, way):
        return pl.ds(pl.multiple_of(way * half + part * quarter, quarter), quarter)

    def ring(step, part, way):
        here = lanes_of(part, way)
        return remote(
            part_sum.at[step, :, here],
            from_ring.at[step, :, here],
            sent_ring.at[step, part, way],
            got_ring.at[step, part, way],
            {"lat": down if way else up},
        )

    def near(part, way):
        return remote(
            part_sum.at[YS - 1, :, lanes_of(part, way)],
            relay.at[part, way],
            sent_near.at[part, way],
            got_near.at[part, way],
            at_height(-1 if way else 1),
        )

    def far(part, way):
        return remote(
            relay.at[part, way],
            from_z.at[:, lanes_of(part, way)],
            sent_far.at[part, way],
            got_far.at[part, way],
            at_height(1 - nz if way else nz - 1),
        )

    def finish(step, part):
        turn = lax.rem(step, YS)

        @pl.when(turn > 0)
        def _():
            for way in range(2):
                ring(step - 1, part, way).wait_recv()
                here = lanes_of(part, way)
                part_sum[step, :, here] += from_ring[step - 1, :, here]

        @pl.when(turn < YS - 1)
        def _():
            for way in range(2):
                ring(step, part, way).start()

        @pl.when(step == YS - 1)
        def _():
            for way in range(2):
                near(part, way).start()

    def per_item(t, unused):
        swapped = (t == 1) | (t == 2)
        step = jnp.where(swapped, 2 - t, t // 2)
        s = jnp.where(swapped, t - 1, lax.rem(t, 2))

        @pl.when(t == 2)
        def _():
            take_results(1)

        for index in range(2):
            pl.when(s == index)(functools.partial(compute, step, index))

        @pl.when(t == 0)
        def _():
            exchange_z(1)

        @pl.when((t >= 2) & (t != 10))
        def _():
            finish(
                jnp.where(t < 10, (t - 2) // 2, (t - 1) // 2),
                jnp.where(t < 10, lax.rem(t, 2), lax.rem(t + 1, 2)),
            )

        @pl.when((t == 9) | (t == 10))
        def _():
            finish(YS, t - 9)

        for part in range(2):

            @pl.when(t == 10 + part)
            def _():
                for way in range(2):
                    near(part, way).wait_recv()
                    far(part, way).start()

        return unused

    lax.fori_loop(0, 4 * YS, per_item, 0)

    swap = remote(q_parts.at[1 - core], from_core, sent_core, got_core, {"pts": me + 1 - 2 * core})

    def bias_y(k):
        return remote(
            bias_sum.at[pl.ds(0, SWEEPS)],
            bias_1.at[y * 2 + core],
            sent_b1.at[k],
            got_b1.at[k],
            y_peer(k),
        )

    def q_along_x(k):
        return remote(
            q_x.at[lax.rem(x + k, nx)], got_q_x.at[x], sent_qx.at[k], got_qx.at[k], x_peer(k)
        )

    def q_along_z(k):
        return remote(
            q_z.at[lax.rem(zl + k, nz)], got_q_z.at[zl], sent_qz.at[k], got_qz.at[k], z_peer(k)
        )

    def bias_along_z(k):
        return remote(bias_2, bias_z.at[height], sent_b2.at[k], got_b2.at[k], at_height(k))

    bias_copies = [bias_y(k) for k in range(1, 2 * YS)]
    x_copies = [q_along_x(k) for k in range(1, nx)]
    z_copies = [q_along_z(k) for k in range(1, nz)]
    bias_z_copies = [bias_along_z(k) for k in range(1, heights)]

    for copy in bias_copies:
        copy.start()
    grad_q = grad_q_t[...].T
    for p in range(count):
        q_parts[p % 2, p // 2] = grad_q[p * rows_out : (p + 1) * rows_out]
    swap.start()
    bias_1[y * 2 + core] = bias_sum[:SWEEPS, :]
    for copy in bias_copies:
        copy.wait_recv()
    bias = jnp.sum(bias_1[...], axis=0)
    swap.wait_recv()
    for i in range(nx):
        for j in range(nz):
            q_x[i, j * rows_out : (j + 1) * rows_out, :] = (
                q_parts[core, i * nz + j] + from_core[i * nz + j]
            )
        q_x[i, nz * rows_out :, :] = bias
    for copy in x_copies:
        copy.start()
    got_q_x[x] = q_x[x]
    finish(2 * YS - 1, 1)
    for s in range(2):
        to_sibling(s).wait_send()
        for k in range(1, nx):
            along_x(s, k).wait_send()
        for k in range(1, nz):
            along_z(s, k).wait_send()
    for part in range(2):
        for way in range(2):
            for step in range(2 * YS):
                if step % YS < YS - 1:
                    ring(step, part, way).wait_send()
            near(part, way).wait_send()
    for copy in x_copies:
        copy.wait_recv()
    summed = jnp.sum(got_q_x[...], axis=0)
    bias_2[...] = summed[nz * rows_out :]
    for j in range(nz):
        q_z[j] = summed[j * rows_out : (j + 1) * rows_out]
    for copy in bias_z_copies + z_copies:
        copy.start()
    got_q_z[zl] = q_z[zl]
    bias_z[height] = bias_2[...]
    swap.wait_send()
    for copy in bias_copies + x_copies:
        copy.wait_send()
    for part in range(2):
        for way in range(2):
            far(part, way).wait_send()
            far(part, way).wait_recv()
    grads_ref[...] = part_sum[2 * YS - 1] + from_z[...]
    for copy in bias_z_copies + z_copies:
        copy.wait_recv()
    small_ref[:rows_out, :] = jnp.sum(got_q_z[...], axis=0)
    small_ref[rows_out:, :] = jnp.sum(bias_z[...], axis=0)

    for copy in z_copies + bias_z_copies:
        copy.wait_send()


def whole(latents, keys, values, sweep, sweep_bias, grad_out, count, lats):
    rows, points = latents.shape[0], keys.shape[0]
    block, span, chips = points // (2 * YS), rows // 2, count // 2
    cols = min(256, span)
    lines = HEADS * rows // 256
    nz = 4 if chips % 4 == 0 else chips
    nx = chips // nz
    heights = 2 * nz
    rows_out = rows // count
    dma = pltpu.SemaphoreType.DMA
    return pl.pallas_call(
        functools.partial(whole_kernel, count, lats),
        out_shape=[
            jax.ShapeDtypeStruct((2 * WIDTH, block), F32),
            jax.ShapeDtypeStruct((rows_out + SWEEPS, WIDTH), F32),
        ],
        in_specs=vmem_specs(6),
        out_specs=vmem_specs(2),
        scratch_shapes=[
            pltpu.VMEM((points, 2 * WIDTH), BF),
            pltpu.VMEM((HEADS, 48, points), BF),
            pltpu.VMEM((SWEEPS, points), BF),
            pltpu.VMEM((WIDTH, rows), BF),
            pltpu.VMEM((2 * HEADS, 2 * WIDTH, span), BF),
            pltpu.VMEM((2 * HEADS, 2 * WIDTH, span), BF),
            pltpu.VMEM((points, cols), F32),
            pltpu.VMEM((points, cols), F32),
            pltpu.VMEM((HEADS, points, span), BF),
            pltpu.VMEM((8, span), F32),
            pltpu.VMEM((HEADS, 2 * HEAD_DIM, span), BF),
            pltpu.VMEM((2, 3, lines, 128), F32),
            pltpu.VMEM((2, 3, lines, 128), F32),
            pltpu.VMEM((2, 3, lines, 128), F32),
            pltpu.VMEM((2, nx, 3, lines, 128), F32),
            pltpu.VMEM((2, 3, lines, 128), F32),
            pltpu.VMEM((2, nz, 3, lines, 128), F32),
            pltpu.VMEM((block, 2 * WIDTH), BF),
            pltpu.VMEM((block, 2 * WIDTH), BF),
            pltpu.VMEM((SWEEPS, block), BF),
            pltpu.VMEM((HEADS, block, span), BF),
            pltpu.VMEM((HEADS, block, span), BF),
            pltpu.VMEM((2 * YS, 2 * WIDTH, block), F32),
            pltpu.VMEM((2 * YS, 2 * WIDTH, block), F32),
            pltpu.VMEM((2, 2, 2 * WIDTH, block // 4), F32),
            pltpu.VMEM((2 * WIDTH, block), F32),
            pltpu.VMEM((WIDTH, rows), F32),
            pltpu.VMEM((128, 128), F32),
            pltpu.VMEM((2, chips, rows_out, WIDTH), F32),
            pltpu.VMEM((chips, rows_out, WIDTH), F32),
            pltpu.VMEM((2 * YS, SWEEPS, 128), F32),
            pltpu.VMEM((nx, nz * rows_out + SWEEPS, WIDTH), F32),
            pltpu.VMEM((nx, nz * rows_out + SWEEPS, WIDTH), F32),
            pltpu.VMEM((nz, rows_out, WIDTH), F32),
            pltpu.VMEM((nz, rows_out, WIDTH), F32),
            pltpu.VMEM((SWEEPS, 128), F32),
            pltpu.VMEM((heights, SWEEPS, 128), F32),
            dma((2,)),
            dma((2,)),
            dma((2, nx)),
            dma((2, nx)),
            dma((2, nz)),
            dma((2, nz)),
            dma((2 * YS, 2, 2)),
            dma((2 * YS, 2, 2)),
            dma((2, 2)),
            dma((2, 2)),
            dma((2, 2)),
            dma((2, 2)),
            dma,
            dma,
            dma((2 * YS,)),
            dma((2 * YS,)),
            dma((nx,)),
            dma((nx,)),
            dma((nz,)),
            dma((nz,)),
            dma((heights,)),
            dma((heights,)),
        ],
        compiler_params=pltpu.CompilerParams(
            collective_id=0, has_side_effects=True, vmem_limit_bytes=VMEM_BYTES
        ),
    )(latents, keys, values, sweep, sweep_bias, grad_out)


def deliver_kernel(small_ref, grads_ref, q_out, k_out, v_out, bias_out, square):
    rows_out = q_out.shape[0]
    q_out[...] = small_ref[:rows_out, :]
    k_out[...] = grads_ref[:WIDTH, :].T
    v_out[...] = grads_ref[WIDTH:, :].T
    square[...] = jnp.zeros_like(square)
    square[:SWEEPS, :] = small_ref[rows_out:, :]
    bias_out[...] = square[...].T[:HEADS, :SWEEPS]


def deliver(small, grads):
    block = grads.shape[1]
    return pl.pallas_call(
        deliver_kernel,
        out_shape=[
            jax.ShapeDtypeStruct((small.shape[0] - SWEEPS, WIDTH), F32),
            jax.ShapeDtypeStruct((block, WIDTH), F32),
            jax.ShapeDtypeStruct((block, WIDTH), F32),
            jax.ShapeDtypeStruct((HEADS, SWEEPS), F32),
        ],
        in_specs=vmem_specs(2),
        out_specs=vmem_specs(4),
        scratch_shapes=[pltpu.VMEM((128, 128), F32)],
    )(small, grads)


def per_device(count, lats, latents, keys, values, sweep, sweep_bias, grad_out):
    grads, small = whole(
        latents, keys, values, sweep.reshape(1, -1), sweep_bias, grad_out, count, lats
    )
    return tuple(deliver(small, grads))


def solution(mesh):
    return jax.shard_map(
        functools.partial(per_device, mesh.shape["pts"], mesh.shape["lat"]),
        mesh=mesh,
        in_specs=(P("lat", None), P("pts", None), P("pts", None), P("pts"), P(), P("lat", None)),
        out_specs=(P(("lat", "pts"), None), P(("pts", "lat"), None), P(("pts", "lat"), None), P()),
        check_vma=False,
    )
```
